32 devices in a mesh: outer: 4 (over x, core), inner: 8 (over z, y).
Axes of the slice: x: 2, y: 2, z: 4, core: 2. Of those that a mesh axis runs over, the one named last changes fastest.
Arguments:
- query: bfloat16 [131072, 256], P(('outer', 'inner')), may hold values from -6 to 6
- keys: bfloat16 [131072, 256], P(('outer', 'inner')), may hold values from -1.5 to 1.5
- values: bfloat16 [131072, 256], P(('outer', 'inner')), may hold values from -6 to 6
- out_grad: bfloat16 [131072, 256], P(('outer', 'inner')), may hold values from -1.5 to 1.5
Outputs:
- attended: bfloat16 [131072, 256], P(('outer', 'inner'))
- query_grad: bfloat16 [131072, 256], P(('outer', 'inner'))
- keys_grad: bfloat16 [131072, 256], P(('outer', 'inner'))
- values_grad: bfloat16 [131072, 256], P(('outer', 'inner'))
The draws below stay inside these ranges and needn't reach their ends.
All inputs are finite; a program needn't handle non-finite values.
Results may differ from the reference program's by a relative error of at most 0.008.
Values sent between devices are 32-bit elements; how exact they have to be, the bound alone decides.
No kernel may reach another device: no remote copies, remote signals or barrier semaphores. Data moves between devices by JAX's collectives and lax.ppermute only.
A program may use at most 192 MiB of HBM per device.

```python
import jax
import jax.numpy as jnp
from jax import lax

H = 2
E = 128
BLK = 512
TOKENS = 131072


def steps_of(own_key, extent, shards, low, top_value):
    factor_of = 1.0
    for dim, blocks in shards:
        steps = jax.random.uniform(jax.random.fold_in(jax.random.fold_in(own_key, 6), dim), (blocks,), jnp.float32, low / len(shards), top_value / len(shards))
        factor_of = factor_of * jnp.repeat(jnp.exp(steps), extent[dim] // blocks).reshape((-1,) + (1,) * (len(extent) - 1 - dim))
    return factor_of


def centred(rng, extent, scale, reach, pieces=(), kind=jnp.bfloat16):
    values = jax.random.normal(rng, extent, jnp.float32) * scale
    if len(pieces) > 0:
        values = steps_of(rng, extent, pieces, -0.22, 0.18) * values
    return jnp.clip(values, min=-reach, max=reach).astype(kind)


def setup_inputs(seed: int = 0) -> dict:
    splits = jax.random.split(jax.random.key(seed), 5)
    return {
        "query": centred(splits[0], (TOKENS, H * E), 1.0, 6.0, ((0, 32),)),
        "keys": centred(splits[1], (TOKENS, H * E), 0.25, 1.5, ((0, 32),)),
        "values": centred(splits[2], (TOKENS, H * E), 1.0, 6.0, ((0, 32),)),
        "out_grad": centred(splits[3], (TOKENS, H * E), 0.25, 1.5, ((0, 32),)),
    }


def block_terms(query_block, keys_block, values_block, grad_block, scaling):
    scaled = (query_block.astype(jnp.float32) * scaling[:, None, None]).astype(jnp.bfloat16)
    causal = jnp.tril(jnp.ones((BLK, BLK), dtype=bool))[None]
    ascore = jnp.einsum('thd,shd->hts', scaled.astype(jnp.float32), keys_block.astype(jnp.float32))
    bscore = jnp.einsum('the,she->hts', grad_block.astype(jnp.float32), values_block.astype(jnp.float32))
    amat = jnp.where(causal, ascore, 0.0).astype(jnp.bfloat16)
    bmat = jnp.where(causal, bscore, 0.0).astype(jnp.bfloat16)
    return scaled, amat, bmat


def reference(query, keys, values, out_grad):
    blocks = TOKENS // BLK

    def split(array):
        return array.reshape(blocks, BLK, H, E)

    position = jnp.arange(TOKENS, dtype=jnp.int32).reshape(blocks, BLK)
    scaling = (position.astype(jnp.float32) + 1.0) ** -0.5
    inputs = (split(query), split(keys), split(values), split(out_grad), scaling)
    highest = lax.Precision.HIGHEST

    def forward_step(state, items):
        query_block, keys_block, values_block, grad_block, scale_row = items
        scaled, amat, bmat = block_terms(query_block, keys_block, values_block, grad_block, scale_row)
        attended = jnp.einsum('hts,she->the', amat.astype(jnp.float32), values_block.astype(jnp.float32))
        attended = attended + jnp.einsum('thd,hde->the', scaled.astype(jnp.float32), state, precision=highest)
        qgrad = jnp.einsum('hts,shd->thd', bmat.astype(jnp.float32), keys_block.astype(jnp.float32))
        qgrad = qgrad + jnp.einsum('the,hde->thd', grad_block.astype(jnp.float32), state, precision=highest)
        qgrad = qgrad * scale_row[:, None, None]
        state = state + jnp.einsum('shd,she->hde', keys_block.astype(jnp.float32), values_block.astype(jnp.float32))
        return state, (attended.astype(jnp.bfloat16), qgrad.astype(jnp.bfloat16))

    def backward_step(state, items):
        query_block, keys_block, values_block, grad_block, scale_row = items
        scaled, amat, bmat = block_terms(query_block, keys_block, values_block, grad_block, scale_row)
        kgrad = jnp.einsum('hts,thd->shd', bmat.astype(jnp.float32), scaled.astype(jnp.float32))
        kgrad = kgrad + jnp.einsum('she,hde->shd', values_block.astype(jnp.float32), state, precision=highest)
        vgrad = jnp.einsum('hts,the->she', amat.astype(jnp.float32), grad_block.astype(jnp.float32))
        vgrad = vgrad + jnp.einsum('shd,hde->she', keys_block.astype(jnp.float32), state, precision=highest)
        state = state + jnp.einsum('thd,the->hde', scaled.astype(jnp.float32), grad_block.astype(jnp.float32))
        return state, (kgrad.astype(jnp.bfloat16), vgrad.astype(jnp.bfloat16))

    start = jnp.zeros((H, E, E), jnp.float32)
    last, (attended, qgrad) = lax.scan(forward_step, start, inputs)
    first, (kgrad, vgrad) = lax.scan(backward_step, start, inputs, reverse=True)
    width = H * E
    return (attended.reshape(TOKENS, width), qgrad.reshape(TOKENS, width),
            kgrad.reshape(TOKENS, width), vgrad.reshape(TOKENS, width))
```

```python
import functools

import jax
import jax.numpy as jnp
from jax import lax
from jax.experimental import pallas as pl
from jax.experimental.pallas import tpu as pltpu
from jax.sharding import PartitionSpec as P

E = 128
SUB = 256
CHUNK = 1024
PIECES = 4
AXES = ("outer", "inner")
MIB = 1 << 20
ROWS_DIM = (((0,), (0,)), ((), ()))
COLS_DIM = (((1,), (1,)), ((), ()))
PLAIN = (((1,), (0,)), ((), ()))


def dot(a, b, dims):
    return lax.dot_general(a, b, dims, preferred_element_type=jnp.float32)


def scales(first, rows):
    place = first + lax.broadcasted_iota(jnp.int32, (rows, E), 0)
    return lax.rsqrt(place.astype(jnp.float32) + 1.0)


def wide(scale, heads):
    return jnp.concatenate([scale] * heads, axis=1)


def kv_kernel(k_hbm, v_hbm, k_out, v_out, local_out, total_out, acc, sems):
    rows, width = k_hbm.shape
    heads = width // E
    copies = []
    for c in range(rows // CHUNK):
        at = pl.ds(c * CHUNK, CHUNK)
        pair = (
            pltpu.make_async_copy(k_hbm.at[at], k_out.at[at], sems.at[0, c]),
            pltpu.make_async_copy(v_hbm.at[at], v_out.at[at], sems.at[1, c]),
        )
        for copy in pair:
            copy.start()
        copies.append(pair)
    acc[...] = jnp.zeros_like(acc)
    for c in range(rows // CHUNK):
        for copy in copies[c]:
            copy.wait()
        for b in range(c * (CHUNK // SUB), (c + 1) * (CHUNK // SUB)):
            local_out[b] = acc[...].astype(jnp.bfloat16)
            at = pl.ds(b * SUB, SUB)
            for h in range(heads):
                cols = pl.ds(h * E, E)
                acc[cols, cols] += dot(k_out[at, cols], v_out[at, cols], ROWS_DIM)
    for h in range(heads):
        cols = pl.ds(h * E, E)
        total_out[cols, :] = acc[cols, cols]


def qg_kernel(first_ref, q_hbm, g_hbm, s_out, g_out, local_out, total_out, held, acc, sems):
    rows, width = q_hbm.shape
    heads = width // E
    chunks = rows // CHUNK
    copies = [None] * chunks
    for c in reversed(range(chunks)):
        at = pl.ds(c * CHUNK, CHUNK)
        copies[c] = (
            pltpu.make_async_copy(q_hbm.at[at], held.at[at], sems.at[0, c]),
            pltpu.make_async_copy(g_hbm.at[at], g_out.at[at], sems.at[1, c]),
        )
        for copy in copies[c]:
            copy.start()
    acc[...] = jnp.zeros_like(acc)
    for c in reversed(range(chunks)):
        for copy in copies[c]:
            copy.wait()
        for b in reversed(range(c * (CHUNK // SUB), (c + 1) * (CHUNK // SUB))):
            local_out[b] = acc[...].astype(jnp.bfloat16)
            at = pl.ds(b * SUB, SUB)
            scale = scales(first_ref[0] + b * SUB, SUB)
            for h in range(heads):
                cols = pl.ds(h * E, E)
                scaled = (held[at, cols].astype(jnp.float32) * scale).astype(jnp.bfloat16)
                s_out[at, cols] = scaled
                acc[cols, cols] += dot(scaled, g_out[at, cols], ROWS_DIM)
    for h in range(heads):
        cols = pl.ds(h * E, E)
        total_out[cols, :] = acc[cols, cols]


def inner_kernel(piece, first_ref, s_ref, k_ref, v_ref, g_ref, before_ref, after_ref,
                 att_ref, qgrad_ref, kgrad_ref, vgrad_ref):
    rows, width = s_ref.shape
    heads = width // E
    blocks = rows // PIECES // SUB
    t = lax.broadcasted_iota(jnp.int32, (SUB, SUB), 0)
    s = lax.broadcasted_iota(jnp.int32, (SUB, SUB), 1)
    causal = s <= t
    for i in range(blocks):
        b = piece * blocks + i
        at = pl.ds(b * SUB, SUB)
        to = pl.ds(i * SUB, SUB)
        scale = scales(first_ref[0] + b * SUB, SUB)
        att_state = dot(s_ref[at, :], before_ref[b], PLAIN)
        qgrad_state = dot(g_ref[at, :], before_ref[b], COLS_DIM)
        kgrad_state = dot(v_ref[at, :], after_ref[b], COLS_DIM)
        vgrad_state = dot(k_ref[at, :], after_ref[b], PLAIN)
        for h in range(heads):
            cols = pl.ds(h * E, E)
            part = slice(h * E, (h + 1) * E)
            sh, kh, vh, gh = s_ref[at, cols], k_ref[at, cols], v_ref[at, cols], g_ref[at, cols]
            a = jnp.where(causal, dot(sh, kh, COLS_DIM), 0.0).astype(jnp.bfloat16)
            m = jnp.where(causal, dot(gh, vh, COLS_DIM), 0.0).astype(jnp.bfloat16)
            att_ref[to, cols] = (dot(a, vh, PLAIN) + att_state[:, part]).astype(jnp.bfloat16)
            qgrad_ref[to, cols] = (
                (dot(m, kh, PLAIN) + qgrad_state[:, part]) * scale
            ).astype(jnp.bfloat16)
            kgrad_ref[to, cols] = (dot(m, sh, ROWS_DIM) + kgrad_state[:, part]).astype(jnp.bfloat16)
            vgrad_ref[to, cols] = (dot(a, gh, ROWS_DIM) + vgrad_state[:, part]).astype(jnp.bfloat16)


def last_kernel(rounds, device_ref, s_ref, k_ref, v_ref, g_ref, *refs):
    rows, width = s_ref.shape
    heads = width // E
    kv_in, refs = refs[:rounds], refs[rounds:]
    qg_in, refs = refs[:rounds], refs[rounds:]
    parts, refs = refs[:4 * PIECES], refs[4 * PIECES:]
    outs, (held, before, after, sems) = refs[:4], refs[4:]
    device = device_ref[0]
    kv = jnp.zeros(kv_in[0].shape, jnp.float32)
    qg = jnp.zeros(qg_in[0].shape, jnp.float32)
    for r in range(rounds):
        high = (lax.shift_right_logical(device, r) & 1) == 1
        kv = kv + jnp.where(high, kv_in[r][...], 0.0)
        qg = qg + jnp.where(high, 0.0, qg_in[r][...])
    before[...] = jnp.zeros_like(before)
    after[...] = jnp.zeros_like(after)
    for h in range(heads):
        cols = pl.ds(h * E, E)
        before[cols, cols] = kv[h * E:(h + 1) * E].astype(jnp.bfloat16)
        after[cols, cols] = qg[h * E:(h + 1) * E].astype(jnp.bfloat16)
    step = rows // PIECES
    copies = []
    for p in range(PIECES):
        for i in range(step // SUB):
            at = pl.ds(p * step + i * SUB, SUB)
            of = pl.ds(i * SUB, SUB)
            scale = wide(scales(device * rows + p * step + i * SUB, SUB), heads)
            att = dot(s_ref[at, :], before[...], PLAIN)
            held[0, at, :] = (parts[4 * p][of, :].astype(jnp.float32) + att).astype(jnp.bfloat16)
            qgrad = dot(g_ref[at, :], before[...], COLS_DIM) * scale
            held[1, at, :] = (parts[4 * p + 1][of, :].astype(jnp.float32) + qgrad).astype(jnp.bfloat16)
            kgrad = dot(v_ref[at, :], after[...], COLS_DIM)
            held[2, at, :] = (parts[4 * p + 2][of, :].astype(jnp.float32) + kgrad).astype(jnp.bfloat16)
            vgrad = dot(k_ref[at, :], after[...], PLAIN)
            held[3, at, :] = (parts[4 * p + 3][of, :].astype(jnp.float32) + vgrad).astype(jnp.bfloat16)
        at = pl.ds(p * step, step)
        for o in range(4):
            copy = pltpu.make_async_copy(held.at[o, at], outs[o].at[at], sems.at[o, p])
            copy.start()
            copies.append(copy)
    for copy in copies:
        copy.wait()


VM = pl.BlockSpec(memory_space=pltpu.VMEM)
ANY = pl.BlockSpec(memory_space=pl.ANY)
SM = pl.BlockSpec(memory_space=pltpu.SMEM)


def in_vmem(x):
    return pltpu.with_memory_space_constraint(x, pltpu.VMEM)


def in_hbm(x):
    return pltpu.with_memory_space_constraint(x, pltpu.HBM)


def on_device(count, query, keys, values, out_grad):
    rows, width = query.shape
    bf16 = jnp.bfloat16
    subs = rows // SUB
    chunks = rows // CHUNK
    device = lax.axis_index(AXES).astype(jnp.int32)
    device_ref = device.reshape(1)
    first_ref = (device * rows).reshape(1)
    array = pltpu.VMEM((rows, width), bf16)
    states = pltpu.VMEM((subs, width, width), bf16)
    total = jax.ShapeDtypeStruct((width, E), jnp.float32)
    mover = pltpu.CompilerParams(vmem_limit_bytes=24 * MIB)

    k_vm, v_vm, before, kv_total = pl.pallas_call(
        kv_kernel,
        out_shape=(array, array, states, total),
        in_specs=[ANY, ANY],
        out_specs=[VM] * 4,
        scratch_shapes=[
            pltpu.VMEM((width, width), jnp.float32),
            pltpu.SemaphoreType.DMA((2, chunks)),
        ],
        compiler_params=mover,
        name="kv_sums",
    )(in_hbm(keys), in_hbm(values))
    s_vm, g_vm, after, qg_total = pl.pallas_call(
        qg_kernel,
        out_shape=(array, array, states, total),
        in_specs=[SM, ANY, ANY],
        out_specs=[VM] * 4,
        scratch_shapes=[
            pltpu.VMEM((rows, width), bf16),
            pltpu.VMEM((width, width), jnp.float32),
            pltpu.SemaphoreType.DMA((2, chunks)),
        ],
        compiler_params=mover,
        name="qg_sums",
    )(first_ref, in_hbm(query), in_hbm(out_grad))

    rounds = count.bit_length() - 1
    kv_in, qg_in = [], []
    for r in range(rounds):
        bit = 1 << r
        both = [(d, d ^ bit) for d in range(count)]
        last = r == rounds - 1
        up = [(d, t) for d, t in both if d < t]
        down = [(d, t) for d, t in both if d > t]
        kv_in.append(lax.ppermute(kv_total, AXES, up if last else both))
        qg_in.append(lax.ppermute(qg_total, AXES, down if last else both))
        if not last:
            kv_total = kv_total + kv_in[-1]
            qg_total = qg_total + qg_in[-1]

    part = pltpu.VMEM((rows // PIECES, width), bf16)
    parts = []
    for p in range(PIECES):
        operands = [s_vm, k_vm, v_vm, g_vm, before, after]
        parts += pl.pallas_call(
            functools.partial(inner_kernel, p),
            out_shape=(part,) * 4,
            in_specs=[SM] + [VM] * 6,
            out_specs=[VM] * 4,
            compiler_params=mover,
            cost_estimate=pl.CostEstimate(
                flops=2_300_000_000, bytes_accessed=4 * MIB, transcendentals=0
            ),
            name="within_blocks",
        )(first_ref, *[in_vmem(x) for x in operands])

    result = jax.ShapeDtypeStruct((rows, width), bf16)
    return pl.pallas_call(
        functools.partial(last_kernel, rounds),
        out_shape=(result,) * 4,
        in_specs=[SM] + [VM] * (4 + 2 * rounds + 4 * PIECES),
        out_specs=[ANY] * 4,
        scratch_shapes=[
            pltpu.VMEM((4, rows, width), bf16),
            pltpu.VMEM((width, width), bf16),
            pltpu.VMEM((width, width), bf16),
            pltpu.SemaphoreType.DMA((4, PIECES)),
        ],
        compiler_params=mover,
        name="add_states",
    )(
        device_ref,
        *[in_vmem(x) for x in (s_vm, k_vm, v_vm, g_vm)],
        *kv_in,
        *qg_in,
        *[in_vmem(x) for x in parts],
    )


def solution(mesh):
    spec = P(AXES, None)
    count = mesh.shape["outer"] * mesh.shape["inner"]
    return jax.shard_map(
        functools.partial(on_device, count),
        mesh=mesh,
        in_specs=(spec,) * 4,
        out_specs=(spec,) * 4,
        check_vma=False,
    )
```

```python
import functools

import jax
import jax.numpy as jnp
from jax import lax
from jax.experimental import pallas as pl
from jax.experimental.pallas import tpu as pltpu
from jax.sharding import PartitionSpec as P

E = 128
SUB = 256
CHUNK = 1024
PIECES = 8
AXES = ("outer", "inner")
MIB = 1 << 20
ROWS_DIM = (((0,), (0,)), ((), ()))
COLS_DIM = (((1,), (1,)), ((), ()))
PLAIN = (((1,), (0,)), ((), ()))


def dot(a, b, dims):
    return lax.dot_general(a, b, dims, preferred_element_type=jnp.float32)


def scales(first, rows):
    place = first + lax.broadcasted_iota(jnp.int32, (rows, E), 0)
    return lax.rsqrt(place.astype(jnp.float32) + 1.0)


def split_heads(device, acc, keep_out, send_out):
    first, second = pl.ds(0, E), pl.ds(E, E)
    odd = (device & 1) == 1
    low, high = acc[first, first], acc[second, second]
    keep_out[...] = jnp.where(odd, high, low)
    send_out[...] = jnp.where(odd, low, high)


def kv_kernel(device_ref, k_hbm, v_hbm, q_hbm, g_hbm, k_out, v_out, q_out, g_out, local_out,
              keep_out, send_out, acc, sems):
    rows, width = k_hbm.shape
    heads = width // E
    chunks = rows // CHUNK
    copies = []
    for c in range(chunks):
        at = pl.ds(c * CHUNK, CHUNK)
        copies.append((
            pltpu.make_async_copy(k_hbm.at[at], k_out.at[at], sems.at[0, c]),
            pltpu.make_async_copy(v_hbm.at[at], v_out.at[at], sems.at[1, c]),
        ))
    rest = (
        pltpu.make_async_copy(q_hbm, q_out, sems.at[0, chunks]),
        pltpu.make_async_copy(g_hbm, g_out, sems.at[1, chunks]),
    )
    for pair in copies + [rest]:
        for copy in pair:
            copy.start()
    acc[...] = jnp.zeros_like(acc)
    for c in range(chunks):
        for copy in copies[c]:
            copy.wait()
        for b in range(c * (CHUNK // SUB), (c + 1) * (CHUNK // SUB)):
            local_out[b] = acc[...].astype(jnp.bfloat16)
            at = pl.ds(b * SUB, SUB)
            for h in range(heads):
                cols = pl.ds(h * E, E)
                acc[cols, cols] += dot(k_out[at, cols], v_out[at, cols], ROWS_DIM)
    split_heads(device_ref[0], acc, keep_out, send_out)
    for copy in rest:
        copy.wait()


def qg_kernel(device_ref, q_ref, g_ref, earlier, s_out, local_out, keep_out, send_out, acc):
    rows, width = q_ref.shape
    heads = width // E
    first = device_ref[0] * rows
    acc[...] = jnp.zeros_like(acc)
    for b in reversed(range(rows // SUB)):
        local_out[b] = acc[...].astype(jnp.bfloat16)
        at = pl.ds(b * SUB, SUB)
        scale = scales(first + b * SUB, SUB)
        for h in range(heads):
            cols = pl.ds(h * E, E)
            scaled = (q_ref[at, cols].astype(jnp.float32) * scale).astype(jnp.bfloat16)
            s_out[at, cols] = scaled
            acc[cols, cols] += dot(scaled, g_ref[at, cols], ROWS_DIM)
    split_heads(device_ref[0], acc, keep_out, send_out)


def inner_kernel(piece, device_ref, s_ref, k_ref, v_ref, g_ref, before_ref, after_ref, earlier,
                 att_ref, qgrad_ref, kgrad_ref, vgrad_ref):
    rows, width = s_ref.shape
    heads = width // E
    blocks = rows // PIECES // SUB
    t = lax.broadcasted_iota(jnp.int32, (SUB, SUB), 0)
    s = lax.broadcasted_iota(jnp.int32, (SUB, SUB), 1)
    causal = s <= t
    for i in range(blocks):
        b = piece * blocks + i
        at = pl.ds(b * SUB, SUB)
        to = pl.ds(i * SUB, SUB)
        scale = scales(device_ref[0] * rows + b * SUB, SUB)
        att_state = dot(s_ref[at, :], before_ref[b], PLAIN)
        qgrad_state = dot(g_ref[at, :], before_ref[b], COLS_DIM)
        kgrad_state = dot(v_ref[at, :], after_ref[b], COLS_DIM)
        vgrad_state = dot(k_ref[at, :], after_ref[b], PLAIN)
        for h in range(heads):
            cols = pl.ds(h * E, E)
            part = slice(h * E, (h + 1) * E)
            sh, kh, vh, gh = s_ref[at, cols], k_ref[at, cols], v_ref[at, cols], g_ref[at, cols]
            a = jnp.where(causal, dot(sh, kh, COLS_DIM), 0.0).astype(jnp.bfloat16)
            m = jnp.where(causal, dot(gh, vh, COLS_DIM), 0.0).astype(jnp.bfloat16)
            att_ref[to, cols] = (dot(a, vh, PLAIN) + att_state[:, part]).astype(jnp.bfloat16)
            qgrad_ref[to, cols] = (
                (dot(m, kh, PLAIN) + qgrad_state[:, part]) * scale
            ).astype(jnp.bfloat16)
            kgrad_ref[to, cols] = (dot(m, sh, ROWS_DIM) + kgrad_state[:, part]).astype(jnp.bfloat16)
            vgrad_ref[to, cols] = (dot(a, gh, ROWS_DIM) + vgrad_state[:, part]).astype(jnp.bfloat16)


def last_kernel(scaled_second, device_ref, x_ref, y_ref, own_ref, other_ref, earlier, *refs):
    rows, width = x_ref.shape
    parts, refs = refs[:2 * PIECES], refs[2 * PIECES:]
    outs, (held, state, sems) = refs[:2], refs[2:]
    device = device_ref[0]
    odd = (device & 1) == 1
    own, other = own_ref[...], other_ref[...]
    first, second = pl.ds(0, E), pl.ds(E, E)
    state[...] = jnp.zeros_like(state)
    state[first, first] = jnp.where(odd, other, own).astype(jnp.bfloat16)
    state[second, second] = jnp.where(odd, own, other).astype(jnp.bfloat16)
    step = rows // PIECES
    copies = []
    for p in range(PIECES):
        for i in range(step // SUB):
            at = pl.ds(p * step + i * SUB, SUB)
            of = pl.ds(i * SUB, SUB)
            plain = dot(x_ref[at, :], state[...], PLAIN)
            held[0, at, :] = (parts[2 * p][of, :].astype(jnp.float32) + plain).astype(jnp.bfloat16)
            turned = dot(y_ref[at, :], state[...], COLS_DIM)
            if scaled_second:
                scale = scales(device * rows + p * step + i * SUB, SUB)
                turned = turned * jnp.concatenate([scale] * (width // E), axis=1)
            held[1, at, :] = (parts[2 * p + 1][of, :].astype(jnp.float32) + turned).astype(jnp.bfloat16)
        at = pl.ds(p * step, step)
        for o in range(2):
            copy = pltpu.make_async_copy(held.at[o, at], outs[o].at[at], sems.at[o, p])
            copy.start()
            copies.append(copy)
    for copy in copies:
        copy.wait()


VM = pl.BlockSpec(memory_space=pltpu.VMEM)
ANY = pl.BlockSpec(memory_space=pl.ANY)
SM = pl.BlockSpec(memory_space=pltpu.SMEM)


def in_vmem(x):
    return pltpu.with_memory_space_constraint(x, pltpu.VMEM)


def in_hbm(x):
    return pltpu.with_memory_space_constraint(x, pltpu.HBM)


def add_from_others(keep, send, count, device, upward):
    both = [(d, d ^ 1) for d in range(count)]
    beside = lax.ppermute(send, AXES, both)
    running = keep + beside
    seen = [running]
    before = jnp.zeros_like(keep)
    rounds = count.bit_length() - 1
    for r in range(1, rounds):
        bit = 1 << r
        pairs = [(d, d ^ bit) for d in range(count)]
        if r == rounds - 1:
            pairs = [(d, t) for d, t in pairs if (d < t) == upward]
        came = lax.ppermute(running, AXES, pairs)
        wanted = ((device & bit) != 0) == upward
        before = before + jnp.where(wanted, came, 0.0)
        if r < rounds - 1:
            running = running + came
            seen.append(running)
    late = ((device & 1) != 0) == upward
    own = before + jnp.where(late, beside, 0.0)
    given = before + jnp.where(late, 0.0, keep)
    seen.append(given)
    other = lax.ppermute(given, AXES, both)
    return own, other, seen


def on_device(count, query, keys, values, out_grad):
    rows, width = query.shape
    bf16 = jnp.bfloat16
    subs = rows // SUB
    chunks = rows // CHUNK
    device = lax.axis_index(AXES).astype(jnp.int32)
    device_ref = device.reshape(1)
    array = pltpu.VMEM((rows, width), bf16)
    states = pltpu.VMEM((subs, width, width), bf16)
    half = jax.ShapeDtypeStruct((E, E), jnp.float32)
    params = pltpu.CompilerParams(vmem_limit_bytes=24 * MIB)

    k_vm, v_vm, q_vm, g_vm, before, kv_keep, kv_send = pl.pallas_call(
        kv_kernel,
        out_shape=(array,) * 4 + (states, half, half),
        in_specs=[SM] + [ANY] * 4,
        out_specs=[VM] * 7,
        scratch_shapes=[
            pltpu.VMEM((width, width), jnp.float32),
            pltpu.SemaphoreType.DMA((2, chunks + 1)),
        ],
        compiler_params=params,
        name="kv_sums",
    )(device_ref, *[in_hbm(x) for x in (keys, values, query, out_grad)])
    s_vm, after, qg_keep, qg_send = pl.pallas_call(
        qg_kernel,
        out_shape=(array, states, half, half),
        in_specs=[SM, VM, VM, ANY],
        out_specs=[VM] * 4,
        scratch_shapes=[pltpu.VMEM((width, width), jnp.float32)],
        compiler_params=params,
        name="qg_sums",
    )(device_ref, in_vmem(q_vm), in_vmem(g_vm), kv_keep)
    kv_own, kv_other, kv_seen = add_from_others(kv_keep, kv_send, count, device, True)
    qg_own, qg_other, qg_seen = add_from_others(qg_keep, qg_send, count, device, False)
    marks = [x for pair in zip(kv_seen, qg_seen) for x in pair]

    part = pltpu.VMEM((rows // PIECES, width), bf16)
    parts = []
    for p in range(PIECES):
        operands = [s_vm, k_vm, v_vm, g_vm, before, after]
        parts.append(pl.pallas_call(
            functools.partial(inner_kernel, p),
            out_shape=(part,) * 4,
            in_specs=[SM] + [VM] * 6 + [ANY],
            out_specs=[VM] * 4,
            compiler_params=params,
            cost_estimate=pl.CostEstimate(
                flops=9_200_000_000 // PIECES, bytes_accessed=16 * MIB // PIECES, transcendentals=0
            ),
            name="within_blocks",
        )(device_ref, *[in_vmem(x) for x in operands], marks[min(p, len(marks) - 1)]))

    result = jax.ShapeDtypeStruct((rows, width), bf16)

    def last(x, y, own, other, earlier, pieces, scaled_second, name):
        return pl.pallas_call(
            functools.partial(last_kernel, scaled_second),
            out_shape=(result,) * 2,
            in_specs=[SM] + [VM] * 4 + [ANY] + [VM] * (2 * PIECES),
            out_specs=[ANY] * 2,
            scratch_shapes=[
                pltpu.VMEM((2, rows, width), bf16),
                pltpu.VMEM((width, width), bf16),
                pltpu.SemaphoreType.DMA((2, PIECES)),
            ],
            compiler_params=params,
            name=name,
        )(device_ref, in_vmem(x), in_vmem(y), own, other, earlier, *[in_vmem(p) for p in pieces])

    att, qgrad = last(
        s_vm, g_vm, kv_own, kv_other, kv_own, [x for p in parts for x in p[:2]], True, "add_before"
    )
    vgrad, kgrad = last(
        k_vm, v_vm, qg_own, qg_other, att, [x for p in parts for x in p[:1:-1]], False, "add_after"
    )
    return att, qgrad, kgrad, vgrad


def solution(mesh):
    spec = P(AXES, None)
    count = mesh.shape["outer"] * mesh.shape["inner"]
    return jax.shard_map(
        functools.partial(on_device, count),
        mesh=mesh,
        in_specs=(spec,) * 4,
        out_specs=(spec,) * 4,
        check_vma=False,
    )
```

```python
import functools

import jax
import jax.numpy as jnp
from jax import lax
from jax.experimental import pallas as pl
from jax.experimental.pallas import tpu as pltpu
from jax.sharding import PartitionSpec as P

E = 128
SUB = 256
CHUNK = 1024
PIECES = 2
SEND = 512
AXES = ("outer", "inner")
MIB = 1 << 20
ROWS_DIM = (((0,), (0,)), ((), ()))
COLS_DIM = (((1,), (1,)), ((), ()))
PLAIN = (((1,), (0,)), ((), ()))


def dot(a, b, dims):
    return lax.dot_general(a, b, dims, preferred_element_type=jnp.float32)


def scales(first, rows):
    place = first + lax.broadcasted_iota(jnp.int32, (rows, E), 0)
    return lax.rsqrt(place.astype(jnp.float32) + 1.0)


def kv_kernel(device_ref, k_hbm, v_hbm, q_hbm, g_hbm, k_out, v_out, q_out, g_out, local_out,
              total_out, acc, sems):
    rows, width = k_hbm.shape
    heads = width // E
    chunks = rows // CHUNK
    copies = []
    for c in range(chunks):
        at = pl.ds(c * CHUNK, CHUNK)
        copies.append((
            pltpu.make_async_copy(k_hbm.at[at], k_out.at[at], sems.at[0, c]),
            pltpu.make_async_copy(v_hbm.at[at], v_out.at[at], sems.at[1, c]),
        ))
    rest = (
        pltpu.make_async_copy(q_hbm, q_out, sems.at[0, chunks]),
        pltpu.make_async_copy(g_hbm, g_out, sems.at[1, chunks]),
    )
    for pair in copies + [rest]:
        for copy in pair:
            copy.start()
    acc[...] = jnp.zeros_like(acc)
    for c in range(chunks):
        for copy in copies[c]:
            copy.wait()
        for b in range(c * (CHUNK // SUB), (c + 1) * (CHUNK // SUB)):
            local_out[b] = acc[...].astype(jnp.bfloat16)
            at = pl.ds(b * SUB, SUB)
            for h in range(heads):
                cols = pl.ds(h * E, E)
                acc[cols, cols] += dot(k_out[at, cols], v_out[at, cols], ROWS_DIM)
    for h in range(heads):
        cols = pl.ds(h * E, E)
        total_out[cols, :] = acc[cols, cols]
    for copy in rest:
        copy.wait()


def qg_kernel(device_ref, q_ref, g_ref, kv_ref, s_out, local_out, total_out, acc):
    rows, width = q_ref.shape
    heads = width // E
    first = device_ref[0] * rows
    acc[...] = jnp.zeros_like(acc)
    for b in reversed(range(rows // SUB)):
        local_out[b] = acc[...].astype(jnp.bfloat16)
        at = pl.ds(b * SUB, SUB)
        scale = scales(first + b * SUB, SUB)
        for h in range(heads):
            cols = pl.ds(h * E, E)
            scaled = (q_ref[at, cols].astype(jnp.float32) * scale).astype(jnp.bfloat16)
            s_out[at, cols] = scaled
            acc[cols, cols] += dot(scaled, g_ref[at, cols], ROWS_DIM)
    total_out[pl.ds(0, width), :] = kv_ref[...]
    for h in range(heads):
        cols = pl.ds(h * E, E)
        total_out[pl.ds(width + h * E, E), :] = acc[cols, cols]


def inner_kernel(piece, device_ref, s_ref, k_ref, v_ref, g_ref, before_ref, after_ref, earlier,
                 att_ref, qgrad_ref, kgrad_ref, vgrad_ref):
    rows, width = s_ref.shape
    heads = width // E
    blocks = rows // PIECES // SUB
    t = lax.broadcasted_iota(jnp.int32, (SUB, SUB), 0)
    s = lax.broadcasted_iota(jnp.int32, (SUB, SUB), 1)
    causal = s <= t
    for i in range(blocks):
        b = piece * blocks + i
        at = pl.ds(b * SUB, SUB)
        to = pl.ds(i * SUB, SUB)
        scale = scales(device_ref[0] * rows + b * SUB, SUB)
        att_state = dot(s_ref[at, :], before_ref[b], PLAIN)
        qgrad_state = dot(g_ref[at, :], before_ref[b], COLS_DIM)
        kgrad_state = dot(v_ref[at, :], after_ref[b], COLS_DIM)
        vgrad_state = dot(k_ref[at, :], after_ref[b], PLAIN)
        for h in range(heads):
            cols = pl.ds(h * E, E)
            part = slice(h * E, (h + 1) * E)
            sh, kh, vh, gh = s_ref[at, cols], k_ref[at, cols], v_ref[at, cols], g_ref[at, cols]
            a = jnp.where(causal, dot(sh, kh, COLS_DIM), 0.0).astype(jnp.bfloat16)
            m = jnp.where(causal, dot(gh, vh, COLS_DIM), 0.0).astype(jnp.bfloat16)
            att_ref[to, cols] = (dot(a, vh, PLAIN) + att_state[:, part]).astype(jnp.bfloat16)
            qgrad_ref[to, cols] = (
                (dot(m, kh, PLAIN) + qgrad_state[:, part]) * scale
            ).astype(jnp.bfloat16)
            kgrad_ref[to, cols] = (dot(m, sh, ROWS_DIM) + kgrad_state[:, part]).astype(jnp.bfloat16)
            vgrad_ref[to, cols] = (dot(a, gh, ROWS_DIM) + vgrad_state[:, part]).astype(jnp.bfloat16)


def scan_kernel(count, device_ref, pieces_ref, out_ref):
    step = pieces_ref.shape[0] // count

    def run(order):
        total = jnp.zeros((step, E), jnp.float32)
        for i in order:
            at = pl.ds(i * step, step)
            out_ref[at, :] = total
            total = total + pieces_ref[at, :]

    first_half = device_ref[0] < count // 2

    @pl.when(first_half)
    def _():
        run(range(count))

    @pl.when(jnp.logical_not(first_half))
    def _():
        run(reversed(range(count)))


def last_kernel(device_ref, s_ref, k_ref, v_ref, g_ref, states_ref, *refs):
    rows, width = s_ref.shape
    heads = width // E
    parts, refs = refs[:4 * PIECES], refs[4 * PIECES:]
    outs, (held, before, after, sems) = refs[:4], refs[4:]
    before[...] = jnp.zeros_like(before)
    after[...] = jnp.zeros_like(after)
    for h in range(heads):
        cols = pl.ds(h * E, E)
        before[cols, cols] = states_ref[cols, :].astype(jnp.bfloat16)
        after[cols, cols] = states_ref[pl.ds(width + h * E, E), :].astype(jnp.bfloat16)
    step = rows // PIECES
    copies = []
    for c in range(rows // SEND):
        for i in range(SEND // SUB):
            row = c * SEND + i * SUB
            p, at, of = row // step, pl.ds(row, SUB), pl.ds(row % step, SUB)
            scale = scales(device_ref[0] * rows + row, SUB)
            sums = (
                dot(s_ref[at, :], before[...], PLAIN),
                dot(g_ref[at, :], before[...], COLS_DIM) * jnp.concatenate([scale] * heads, axis=1),
                dot(v_ref[at, :], after[...], COLS_DIM),
                dot(k_ref[at, :], after[...], PLAIN),
            )
            for o in range(4):
                part = parts[4 * p + o][of, :].astype(jnp.float32)
                held[o, at, :] = (part + sums[o]).astype(jnp.bfloat16)
        at = pl.ds(c * SEND, SEND)
        for o in range(4):
            copy = pltpu.make_async_copy(held.at[o, at], outs[o].at[at], sems.at[o, c])
            copy.start()
            copies.append(copy)
    for copy in copies:
        copy.wait()


VM = pl.BlockSpec(memory_space=pltpu.VMEM)
ANY = pl.BlockSpec(memory_space=pl.ANY)
SM = pl.BlockSpec(memory_space=pltpu.SMEM)


def in_vmem(x):
    return pltpu.with_memory_space_constraint(x, pltpu.VMEM)


def in_hbm(x):
    return pltpu.with_memory_space_constraint(x, pltpu.HBM)


def on_device(count, query, keys, values, out_grad):
    rows, width = query.shape
    bf16 = jnp.bfloat16
    subs = rows // SUB
    chunks = rows // CHUNK
    device_ref = lax.axis_index(AXES).astype(jnp.int32).reshape(1)
    array = pltpu.VMEM((rows, width), bf16)
    states = pltpu.VMEM((subs, width, width), bf16)
    total = jax.ShapeDtypeStruct((width, E), jnp.float32)
    both = jax.ShapeDtypeStruct((2 * width, E), jnp.float32)
    params = pltpu.CompilerParams(vmem_limit_bytes=24 * MIB)

    k_vm, v_vm, q_vm, g_vm, before, kv_total = pl.pallas_call(
        kv_kernel,
        out_shape=(array,) * 4 + (states, total),
        in_specs=[SM] + [ANY] * 4,
        out_specs=[VM] * 6,
        scratch_shapes=[
            pltpu.VMEM((width, width), jnp.float32),
            pltpu.SemaphoreType.DMA((2, chunks + 1)),
        ],
        compiler_params=params,
        name="kv_sums",
    )(device_ref, *[in_hbm(x) for x in (keys, values, query, out_grad)])
    s_vm, after, totals = pl.pallas_call(
        qg_kernel,
        out_shape=(array, states, both),
        in_specs=[SM, VM, VM, VM],
        out_specs=[VM] * 3,
        scratch_shapes=[pltpu.VMEM((width, width), jnp.float32)],
        compiler_params=params,
        name="qg_sums",
    )(device_ref, in_vmem(q_vm), in_vmem(g_vm), kv_total)
    spread = lax.all_to_all(totals, AXES, 0, 0, tiled=True)
    scanned = pl.pallas_call(
        functools.partial(scan_kernel, count),
        out_shape=both,
        in_specs=[SM, VM],
        out_specs=VM,
        compiler_params=params,
        name="scan_devices",
    )(device_ref, spread)
    outside = lax.all_to_all(scanned, AXES, 0, 0, tiled=True)
    marks = [totals] * (PIECES // 2) + [scanned] * (PIECES - PIECES // 2)

    part = pltpu.VMEM((rows // PIECES, width), bf16)
    parts = []
    for p in range(PIECES):
        operands = [s_vm, k_vm, v_vm, g_vm, before, after]
        parts += pl.pallas_call(
            functools.partial(inner_kernel, p),
            out_shape=(part,) * 4,
            in_specs=[SM] + [VM] * 6 + [ANY],
            out_specs=[VM] * 4,
            compiler_params=params,
            cost_estimate=pl.CostEstimate(
                flops=9_200_000_000 // PIECES, bytes_accessed=16 * MIB // PIECES, transcendentals=0
            ),
            name="within_blocks",
        )(device_ref, *[in_vmem(x) for x in operands], marks[p])

    result = jax.ShapeDtypeStruct((rows, width), bf16)
    return pl.pallas_call(
        last_kernel,
        out_shape=(result,) * 4,
        in_specs=[SM] + [VM] * (5 + 4 * PIECES),
        out_specs=[ANY] * 4,
        scratch_shapes=[
            pltpu.VMEM((4, rows, width), bf16),
            pltpu.VMEM((width, width), bf16),
            pltpu.VMEM((width, width), bf16),
            pltpu.SemaphoreType.DMA((4, rows // SEND)),
        ],
        compiler_params=params,
        name="add_states",
    )(
        device_ref,
        *[in_vmem(x) for x in (s_vm, k_vm, v_vm, g_vm)],
        outside,
        *[in_vmem(x) for x in parts],
    )


def solution(mesh):
    spec = P(AXES, None)
    count = mesh.shape["outer"] * mesh.shape["inner"]
    return jax.shard_map(
        functools.partial(on_device, count),
        mesh=mesh,
        in_specs=(spec,) * 4,
        out_specs=(spec,) * 4,
        check_vma=False,
    )
```

```python
import functools

import jax
import jax.numpy as jnp
from jax import lax
from jax.experimental import pallas as pl
from jax.experimental.pallas import tpu as pltpu
from jax.sharding import PartitionSpec as P

E = 128
SUB = 256
CHUNK = 1024
SEND = 512
PIECES = 6
AXES = ("outer", "inner")
MIB = 1 << 20
ROWS_DIM = (((0,), (0,)), ((), ()))
COLS_DIM = (((1,), (1,)), ((), ()))
PLAIN = (((1,), (0,)), ((), ()))


def dot(a, b, dims):
    return lax.dot_general(a, b, dims, preferred_element_type=jnp.float32)


def scales(first, rows):
    place = first + lax.broadcasted_iota(jnp.int32, (rows, E), 0)
    return lax.rsqrt(place.astype(jnp.float32) + 1.0)


def rows_at(index, size):
    return pl.ds(pl.multiple_of(index * size, size), size)


def loop(count, body):
    lax.fori_loop(0, count, lambda i, carry: (body(i), carry)[1], 0)


def split_heads(device, acc, keep_out, send_out):
    first, second = pl.ds(0, E), pl.ds(E, E)
    odd = (device & 1) == 1
    low, high = acc[first, first], acc[second, second]
    keep_out[...] = jnp.where(odd, high, low)
    send_out[...] = jnp.where(odd, low, high)


def kv_kernel(device_ref, k_hbm, v_hbm, q_hbm, g_hbm, k_out, v_out, q_out, g_out, local_out,
              keep_out, send_out, acc, sems):
    rows, width = k_hbm.shape
    heads = width // E
    chunks = rows // CHUNK
    subs = CHUNK // SUB

    def pair(c):
        at = rows_at(c, CHUNK)
        return (
            pltpu.make_async_copy(k_hbm.at[at], k_out.at[at], sems.at[0, c]),
            pltpu.make_async_copy(v_hbm.at[at], v_out.at[at], sems.at[1, c]),
        )

    rest = (
        pltpu.make_async_copy(q_hbm, q_out, sems.at[0, chunks]),
        pltpu.make_async_copy(g_hbm, g_out, sems.at[1, chunks]),
    )
    for c in range(chunks):
        for copy in pair(c):
            copy.start()
    for copy in rest:
        copy.start()
    acc[...] = jnp.zeros_like(acc)

    def chunk(c):
        for copy in pair(c):
            copy.wait()
        for i in range(subs):
            b = c * subs + i
            local_out[b] = acc[...].astype(jnp.bfloat16)
            at = rows_at(b, SUB)
            for h in range(heads):
                cols = pl.ds(h * E, E)
                acc[cols, cols] += dot(k_out[at, cols], v_out[at, cols], ROWS_DIM)

    loop(chunks, chunk)
    split_heads(device_ref[0], acc, keep_out, send_out)
    for copy in rest:
        copy.wait()


def qg_kernel(device_ref, q_ref, g_ref, earlier, s_out, local_out, keep_out, send_out, acc):
    rows, width = q_ref.shape
    heads = width // E
    chunks = rows // CHUNK
    subs = CHUNK // SUB
    acc[...] = jnp.zeros_like(acc)

    def chunk(c):
        for i in range(subs):
            b = rows // SUB - 1 - (c * subs + i)
            local_out[b] = acc[...].astype(jnp.bfloat16)
            at = rows_at(b, SUB)
            scale = scales(device_ref[0] * rows + b * SUB, SUB)
            for h in range(heads):
                cols = pl.ds(h * E, E)
                scaled = (q_ref[at, cols].astype(jnp.float32) * scale).astype(jnp.bfloat16)
                s_out[at, cols] = scaled
                acc[cols, cols] += dot(scaled, g_ref[at, cols], ROWS_DIM)

    loop(chunks, chunk)
    split_heads(device_ref[0], acc, keep_out, send_out)


def inner_kernel(first, blocks, device_ref, s_ref, k_ref, v_ref, g_ref, before_ref, after_ref,
                 *refs):
    att_ref, qgrad_ref, kgrad_ref, vgrad_ref = refs[-4:]
    rows, width = s_ref.shape
    heads = width // E
    t = lax.broadcasted_iota(jnp.int32, (SUB, SUB), 0)
    s = lax.broadcasted_iota(jnp.int32, (SUB, SUB), 1)
    causal = s <= t

    def block(i):
        b = first + i
        at = rows_at(b, SUB)
        scale = scales(device_ref[0] * rows + b * SUB, SUB)
        att_state = dot(s_ref[at, :], before_ref[b], PLAIN)
        qgrad_state = dot(g_ref[at, :], before_ref[b], COLS_DIM)
        kgrad_state = dot(v_ref[at, :], after_ref[b], COLS_DIM)
        vgrad_state = dot(k_ref[at, :], after_ref[b], PLAIN)
        for h in range(heads):
            cols = pl.ds(h * E, E)
            part = slice(h * E, (h + 1) * E)
            sh, kh, vh, gh = s_ref[at, cols], k_ref[at, cols], v_ref[at, cols], g_ref[at, cols]
            a = jnp.where(causal, dot(sh, kh, COLS_DIM), 0.0).astype(jnp.bfloat16)
            m = jnp.where(causal, dot(gh, vh, COLS_DIM), 0.0).astype(jnp.bfloat16)
            att_ref[at, cols] = (dot(a, vh, PLAIN) + att_state[:, part]).astype(jnp.bfloat16)
            qgrad_ref[at, cols] = (
                (dot(m, kh, PLAIN) + qgrad_state[:, part]) * scale
            ).astype(jnp.bfloat16)
            kgrad_ref[at, cols] = (dot(m, sh, ROWS_DIM) + kgrad_state[:, part]).astype(jnp.bfloat16)
            vgrad_ref[at, cols] = (dot(a, gh, ROWS_DIM) + vgrad_state[:, part]).astype(jnp.bfloat16)

    loop(blocks, block)


def combine_kernel(upward, device_ref, keep_ref, beside_ref, *refs):
    came, (own_ref, given_ref) = refs[:-2], refs[-2:]
    device = device_ref[0]

    def wanted(bit):
        there = (lax.shift_right_logical(device, bit) & 1) == 1
        return there if upward else jnp.logical_not(there)

    total = jnp.zeros(keep_ref.shape, jnp.float32)
    for r, ref in enumerate(came):
        total = total + jnp.where(wanted(r + 1), ref[...], 0.0)
    own_ref[...] = total + jnp.where(wanted(0), beside_ref[...], 0.0)
    given_ref[...] = total + jnp.where(wanted(0), 0.0, keep_ref[...])


def last_kernel(device_ref, s_ref, k_ref, v_ref, g_ref, kv_own, kv_other, qg_own, qg_other, *refs):
    rows, width = s_ref.shape
    heads = width // E
    parts, outs, (held, before, after, sems) = refs[:4], refs[4:8], refs[8:]
    odd = (device_ref[0] & 1) == 1
    for state, own_ref, other_ref in ((before, kv_own, kv_other), (after, qg_own, qg_other)):
        own, other = own_ref[...], other_ref[...]
        first, second = pl.ds(0, E), pl.ds(E, E)
        state[...] = jnp.zeros_like(state)
        state[first, first] = jnp.where(odd, other, own).astype(jnp.bfloat16)
        state[second, second] = jnp.where(odd, own, other).astype(jnp.bfloat16)

    def sends(c):
        at = rows_at(c, SEND)
        return [
            pltpu.make_async_copy(held.at[o, at], outs[o].at[at], sems.at[o, c]) for o in range(4)
        ]

    def chunk(c):
        for i in range(SEND // SUB):
            b = c * (SEND // SUB) + i
            at = rows_at(b, SUB)
            scale = scales(device_ref[0] * rows + b * SUB, SUB)
            sums = (
                dot(s_ref[at, :], before[...], PLAIN),
                dot(g_ref[at, :], before[...], COLS_DIM) * jnp.concatenate([scale] * heads, axis=1),
                dot(v_ref[at, :], after[...], COLS_DIM),
                dot(k_ref[at, :], after[...], PLAIN),
            )
            for o in range(4):
                part = parts[o][at, :].astype(jnp.float32)
                held[o, at, :] = (part + sums[o]).astype(jnp.bfloat16)
        for copy in sends(c):
            copy.start()

    loop(rows // SEND, chunk)

    def finish(c):
        for copy in sends(c):
            copy.wait()

    loop(rows // SEND, finish)


VM = pl.BlockSpec(memory_space=pltpu.VMEM)
ANY = pl.BlockSpec(memory_space=pl.ANY)
SM = pl.BlockSpec(memory_space=pltpu.SMEM)
PARAMS = pltpu.CompilerParams(vmem_limit_bytes=24 * MIB)


def in_vmem(x):
    return pltpu.with_memory_space_constraint(x, pltpu.VMEM)


def in_hbm(x):
    return pltpu.with_memory_space_constraint(x, pltpu.HBM)


def add_from_others(keep, send, count, device_ref, upward):
    both = [(d, d ^ 1) for d in range(count)]
    beside = lax.ppermute(send, AXES, both)
    running = keep + beside
    seen, came = [running], []
    rounds = count.bit_length() - 1
    for r in range(1, rounds):
        bit = 1 << r
        pairs = [(d, d ^ bit) for d in range(count)]
        if r == rounds - 1:
            pairs = [(d, t) for d, t in pairs if (d < t) == upward]
        came.append(lax.ppermute(running, AXES, pairs))
        if r < rounds - 1:
            running = running + came[-1]
            seen.append(running)
    half = jax.ShapeDtypeStruct(keep.shape, jnp.float32)
    own, given = pl.pallas_call(
        functools.partial(combine_kernel, upward),
        out_shape=(half, half),
        in_specs=[SM] + [VM] * (2 + len(came)),
        out_specs=[VM] * 2,
        compiler_params=PARAMS,
        name="combine_rounds",
    )(device_ref, keep, beside, *came)
    seen.append(given)
    other = lax.ppermute(given, AXES, both)
    return own, other, seen


def on_device(count, query, keys, values, out_grad):
    rows, width = query.shape
    bf16 = jnp.bfloat16
    subs = rows // SUB
    chunks = rows // CHUNK
    device_ref = lax.axis_index(AXES).astype(jnp.int32).reshape(1)
    array = pltpu.VMEM((rows, width), bf16)
    states = pltpu.VMEM((subs, width, width), bf16)
    half = jax.ShapeDtypeStruct((E, E), jnp.float32)

    k_vm, v_vm, q_vm, g_vm, before, kv_keep, kv_send = pl.pallas_call(
        kv_kernel,
        out_shape=(array,) * 4 + (states, half, half),
        in_specs=[SM] + [ANY] * 4,
        out_specs=[VM] * 7,
        scratch_shapes=[
            pltpu.VMEM((width, width), jnp.float32),
            pltpu.SemaphoreType.DMA((2, chunks + 1)),
        ],
        compiler_params=PARAMS,
        name="kv_sums",
    )(device_ref, *[in_hbm(x) for x in (keys, values, query, out_grad)])
    s_vm, after, qg_keep, qg_send = pl.pallas_call(
        qg_kernel,
        out_shape=(array, states, half, half),
        in_specs=[SM, VM, VM, ANY],
        out_specs=[VM] * 4,
        scratch_shapes=[pltpu.VMEM((width, width), jnp.float32)],
        compiler_params=PARAMS,
        name="qg_sums",
    )(device_ref, in_vmem(q_vm), in_vmem(g_vm), kv_keep)
    kv_own, kv_other, kv_seen = add_from_others(kv_keep, kv_send, count, device_ref, True)
    qg_own, qg_other, qg_seen = add_from_others(qg_keep, qg_send, count, device_ref, False)
    marks = [kv_seen[0], kv_seen[1], qg_seen[1]] + kv_seen[2:]

    parts = ()
    first = 0
    for p in range(PIECES):
        blocks = subs // PIECES + (p < subs % PIECES)
        operands = [s_vm, k_vm, v_vm, g_vm, before, after, *parts]
        parts = pl.pallas_call(
            functools.partial(inner_kernel, first, blocks),
            out_shape=(array,) * 4,
            in_specs=[SM] + [VM] * len(operands) + [ANY],
            out_specs=[VM] * 4,
            input_output_aliases={7 + o: o for o in range(len(parts))},
            compiler_params=PARAMS,
            cost_estimate=pl.CostEstimate(
                flops=575_000_000 * blocks, bytes_accessed=MIB * blocks, transcendentals=0
            ),
            name="within_blocks",
        )(device_ref, *[in_vmem(x) for x in operands], marks[min(p, len(marks) - 1)])
        first += blocks

    result = jax.ShapeDtypeStruct((rows, width), bf16)
    return pl.pallas_call(
        last_kernel,
        out_shape=(result,) * 4,
        in_specs=[SM] + [VM] * 12,
        out_specs=[ANY] * 4,
        scratch_shapes=[
            pltpu.VMEM((4, rows, width), bf16),
            pltpu.VMEM((width, width), bf16),
            pltpu.VMEM((width, width), bf16),
            pltpu.SemaphoreType.DMA((4, rows // SEND)),
        ],
        compiler_params=PARAMS,
        name="add_states",
    )(
        device_ref,
        *[in_vmem(x) for x in (s_vm, k_vm, v_vm, g_vm)],
        kv_own,
        kv_other,
        qg_own,
        qg_other,
        *[in_vmem(x) for x in parts],
    )


def solution(mesh):
    spec = P(AXES, None)
    count = mesh.shape["outer"] * mesh.shape["inner"]
    return jax.shard_map(
        functools.partial(on_device, count),
        mesh=mesh,
        in_specs=(spec,) * 4,
        out_specs=(spec,) * 4,
        check_vma=False,
    )
```

```python
import functools

import jax
import jax.numpy as jnp
from jax import lax
from jax.experimental import pallas as pl
from jax.experimental.pallas import tpu as pltpu
from jax.sharding import PartitionSpec as P

E = 128
SUB = 256
CHUNK = 1024
SEND = 512
WEIGHTS = (3, 3, 5, 2, 3)
AXES = ("outer", "inner")
MIB = 1 << 20
ROWS_DIM = (((0,), (0,)), ((), ()))
COLS_DIM = (((1,), (1,)), ((), ()))
PLAIN = (((1,), (0,)), ((), ()))


def dot(a, b, dims):
    return lax.dot_general(a, b, dims, preferred_element_type=jnp.float32)


def scales(first, rows):
    place = first + lax.broadcasted_iota(jnp.int32, (rows, E), 0)
    return lax.rsqrt(place.astype(jnp.float32) + 1.0)


def keep_and_send(device, acc, where, keep_out, send_out):
    first, second = pl.ds(0, E), pl.ds(E, E)
    odd = (device & 1) == 1
    low, high = acc[first, first], acc[second, second]
    keep_out[where, :] = jnp.where(odd, high, low)
    send_out[where, :] = jnp.where(odd, low, high)


def sums_kernel(device_ref, k_hbm, v_hbm, q_hbm, g_hbm, k_out, v_out, s_out, g_out, before_out,
                after_out, keep_out, send_out, held, kv_acc, qg_acc, sems):
    rows, width = k_hbm.shape
    heads = width // E
    chunks = rows // CHUNK
    subs = CHUNK // SUB
    copies = []
    for c in range(chunks):
        at, back = pl.ds(c * CHUNK, CHUNK), pl.ds((chunks - 1 - c) * CHUNK, CHUNK)
        copies.append([
            pltpu.make_async_copy(k_hbm.at[at], k_out.at[at], sems.at[0, c]),
            pltpu.make_async_copy(v_hbm.at[at], v_out.at[at], sems.at[1, c]),
            pltpu.make_async_copy(q_hbm.at[back], held.at[back], sems.at[2, c]),
            pltpu.make_async_copy(g_hbm.at[back], g_out.at[back], sems.at[3, c]),
        ])
        for copy in copies[c]:
            copy.start()
    kv_acc[...] = jnp.zeros_like(kv_acc)
    qg_acc[...] = jnp.zeros_like(qg_acc)
    for c in range(chunks):
        for copy in copies[c][:2]:
            copy.wait()
        for i in range(subs):
            b = c * subs + i
            before_out[b] = kv_acc[...].astype(jnp.bfloat16)
            at = pl.ds(b * SUB, SUB)
            for h in range(heads):
                cols = pl.ds(h * E, E)
                kv_acc[cols, cols] += dot(k_out[at, cols], v_out[at, cols], ROWS_DIM)
        for copy in copies[c][2:]:
            copy.wait()
        for i in range(subs):
            b = rows // SUB - 1 - (c * subs + i)
            after_out[b] = qg_acc[...].astype(jnp.bfloat16)
            at = pl.ds(b * SUB, SUB)
            scale = scales(device_ref[0] * rows + b * SUB, SUB)
            for h in range(heads):
                cols = pl.ds(h * E, E)
                scaled = (held[at, cols].astype(jnp.float32) * scale).astype(jnp.bfloat16)
                s_out[at, cols] = scaled
                qg_acc[cols, cols] += dot(scaled, g_out[at, cols], ROWS_DIM)
    keep_and_send(device_ref[0], kv_acc, pl.ds(0, E), keep_out, send_out)
    keep_and_send(device_ref[0], qg_acc, pl.ds(E, E), keep_out, send_out)


def inner_kernel(first, blocks, device_ref, s_ref, k_ref, v_ref, g_ref, before_ref, after_ref,
                 *refs):
    att_ref, qgrad_ref, kgrad_ref, vgrad_ref, tick_ref = refs[-5:]
    tick_ref[...] = jnp.zeros_like(tick_ref)
    rows, width = s_ref.shape
    heads = width // E
    t = lax.broadcasted_iota(jnp.int32, (SUB, SUB), 0)
    s = lax.broadcasted_iota(jnp.int32, (SUB, SUB), 1)
    causal = s <= t

    def block(i):
        b = first + i
        at = pl.ds(b * SUB, SUB)
        scale = scales(device_ref[0] * rows + b * SUB, SUB)
        att_state = dot(s_ref[at, :], before_ref[b], PLAIN)
        qgrad_state = dot(g_ref[at, :], before_ref[b], COLS_DIM)
        kgrad_state = dot(v_ref[at, :], after_ref[b], COLS_DIM)
        vgrad_state = dot(k_ref[at, :], after_ref[b], PLAIN)
        for h in range(heads):
            cols = pl.ds(h * E, E)
            part = slice(h * E, (h + 1) * E)
            sh, kh, vh, gh = s_ref[at, cols], k_ref[at, cols], v_ref[at, cols], g_ref[at, cols]
            a = jnp.where(causal, dot(sh, kh, COLS_DIM), 0.0).astype(jnp.bfloat16)
            m = jnp.where(causal, dot(gh, vh, COLS_DIM), 0.0).astype(jnp.bfloat16)
            att_ref[at, cols] = (dot(a, vh, PLAIN) + att_state[:, part]).astype(jnp.bfloat16)
            qgrad_ref[at, cols] = (
                (dot(m, kh, PLAIN) + qgrad_state[:, part]) * scale
            ).astype(jnp.bfloat16)
            kgrad_ref[at, cols] = (dot(m, sh, ROWS_DIM) + kgrad_state[:, part]).astype(jnp.bfloat16)
            vgrad_ref[at, cols] = (dot(a, gh, ROWS_DIM) + vgrad_state[:, part]).astype(jnp.bfloat16)

    for i in range(blocks):
        block(i)


def bit_of(device_ref, bit):
    return (lax.shift_right_logical(device_ref[0], bit) & 1) == 1


def add_kernel(device_ref, mine_ref, came_ref, tick_ref, out_ref):
    out_ref[...] = mine_ref[...] + came_ref[...]


def pick_kernel(bit, device_ref, mine_ref, came_ref, out_ref):
    up, down = pl.ds(0, E), pl.ds(E, E)
    out_ref[...] = jnp.where(
        bit_of(device_ref, bit), mine_ref[down, :] + came_ref[down, :],
        mine_ref[up, :] + came_ref[up, :],
    )


def combine_kernel(device_ref, keep_ref, beside_ref, last_ref, tick_ref, *refs):
    came, (own_ref, given_ref) = refs[:-2], refs[-2:]
    odd = bit_of(device_ref, 0)
    for upward, part in ((True, pl.ds(0, E)), (False, pl.ds(E, E))):

        def chosen(bit, value):
            there = bit_of(device_ref, bit)
            return jnp.where(there, value, 0.0) if upward else jnp.where(there, 0.0, value)

        total = chosen(len(came) + 1, last_ref[...])
        for r, ref in enumerate(came):
            total = total + chosen(r + 1, ref[part, :])
        beside, keep = beside_ref[part, :], keep_ref[part, :]
        own_ref[part, :] = total + chosen(0, beside)
        given_ref[part, :] = total + (keep - chosen(0, keep))


def last_kernel(device_ref, s_ref, k_ref, v_ref, g_ref, own_ref, other_ref, *refs):
    rows, width = s_ref.shape
    heads = width // E
    parts, outs, (held, before, after, sems) = refs[:4], refs[4:8], refs[8:]
    odd = (device_ref[0] & 1) == 1
    for state, part in ((before, pl.ds(0, E)), (after, pl.ds(E, E))):
        own, other = own_ref[part, :], other_ref[part, :]
        first, second = pl.ds(0, E), pl.ds(E, E)
        state[...] = jnp.zeros_like(state)
        state[first, first] = jnp.where(odd, other, own).astype(jnp.bfloat16)
        state[second, second] = jnp.where(odd, own, other).astype(jnp.bfloat16)

    copies = []
    for c in range(rows // SEND):
        for i in range(SEND // SUB):
            b = c * (SEND // SUB) + i
            at = pl.ds(b * SUB, SUB)
            scale = scales(device_ref[0] * rows + b * SUB, SUB)
            sums = (
                dot(s_ref[at, :], before[...], PLAIN),
                dot(g_ref[at, :], before[...], COLS_DIM) * jnp.concatenate([scale] * heads, axis=1),
                dot(v_ref[at, :], after[...], COLS_DIM),
                dot(k_ref[at, :], after[...], PLAIN),
            )
            for o in range(4):
                part = parts[o][at, :].astype(jnp.float32)
                held[o, at, :] = (part + sums[o]).astype(jnp.bfloat16)
        at = pl.ds(c * SEND, SEND)
        for o in range(4):
            copy = pltpu.make_async_copy(held.at[o, at], outs[o].at[at], sems.at[o, c])
            copy.start()
            copies.append(copy)
    for copy in copies:
        copy.wait()


VM = pl.BlockSpec(memory_space=pltpu.VMEM)
ANY = pl.BlockSpec(memory_space=pl.ANY)
SM = pl.BlockSpec(memory_space=pltpu.SMEM)
PARAMS = pltpu.CompilerParams(vmem_limit_bytes=24 * MIB)


def in_vmem(x):
    return pltpu.with_memory_space_constraint(x, pltpu.VMEM)


def in_hbm(x):
    return pltpu.with_memory_space_constraint(x, pltpu.HBM)


def from_others(keep, send, count, device_ref, work):
    def exchange(x, bit):
        return lax.ppermute(x, AXES, [(d, d ^ (1 << bit)) for d in range(count)])

    def call(kernel, outs, name, *operands):
        shapes = [jax.ShapeDtypeStruct(shape, jnp.float32) for shape in outs]
        return pl.pallas_call(
            kernel,
            out_shape=shapes,
            in_specs=[SM] + [VM] * len(operands),
            out_specs=[VM] * len(outs),
            compiler_params=PARAMS,
            name=name,
        )(device_ref, *operands)

    full, half = keep.shape, (E, E)
    last = count.bit_length() - 2
    beside = exchange(send, 0)
    tick = work(0, keep)
    [running] = call(add_kernel, [full], "add_round", keep, beside, tick)
    came = []
    for bit in range(1, last):
        came.append(exchange(running, bit))
        if bit < 3:
            tick = work(bit, running)
        if bit < last - 1:
            [running] = call(add_kernel, [full], "add_round", running, came[-1], tick)
    [picked] = call(functools.partial(pick_kernel, last), [half], "pick_half", running, came[-1])
    crossed = exchange(picked, last)
    tick = work(3, picked)
    own, given = call(combine_kernel, [full] * 2, "combine_rounds", keep, beside, crossed, tick, *came)
    other = exchange(given, 0)
    work(4, given)
    return own, other


def on_device(count, query, keys, values, out_grad):
    rows, width = query.shape
    bf16 = jnp.bfloat16
    subs = rows // SUB
    chunks = rows // CHUNK
    device_ref = lax.axis_index(AXES).astype(jnp.int32).reshape(1)
    array = pltpu.VMEM((rows, width), bf16)
    states = pltpu.VMEM((subs, width, width), bf16)
    half = jax.ShapeDtypeStruct((2 * E, E), jnp.float32)

    k_vm, v_vm, s_vm, g_vm, before, after, keep, send = pl.pallas_call(
        sums_kernel,
        out_shape=(array,) * 4 + (states,) * 2 + (half,) * 2,
        in_specs=[SM] + [ANY] * 4,
        out_specs=[VM] * 8,
        scratch_shapes=[
            pltpu.VMEM((rows, width), bf16),
            pltpu.VMEM((width, width), jnp.float32),
            pltpu.VMEM((width, width), jnp.float32),
            pltpu.SemaphoreType.DMA((4, chunks)),
        ],
        compiler_params=PARAMS,
        name="sums",
    )(device_ref, *[in_hbm(x) for x in (keys, values, query, out_grad)])
    parts = []
    tick_shape = pltpu.VMEM((8, E), jnp.float32)

    def work(p, mark):
        first = subs * sum(WEIGHTS[:p]) // sum(WEIGHTS)
        blocks = subs * sum(WEIGHTS[:p + 1]) // sum(WEIGHTS) - first
        operands = [s_vm, k_vm, v_vm, g_vm, before, after, *parts]
        *parts[:], tick = pl.pallas_call(
            functools.partial(inner_kernel, first, blocks),
            out_shape=(array,) * 4 + (tick_shape,),
            in_specs=[SM] + [VM] * len(operands) + [ANY],
            out_specs=[VM] * 5,
            input_output_aliases={7 + o: o for o in range(len(parts))},
            compiler_params=PARAMS,
            cost_estimate=pl.CostEstimate(
                flops=575_000_000 * blocks, bytes_accessed=MIB * blocks, transcendentals=0
            ),
            name="within_blocks",
        )(device_ref, *[in_vmem(x) for x in operands], mark)
        return tick

    own, other = from_others(keep, send, count, device_ref, work)

    result = jax.ShapeDtypeStruct((rows, width), bf16)
    return pl.pallas_call(
        last_kernel,
        out_shape=(result,) * 4,
        in_specs=[SM] + [VM] * 10,
        out_specs=[ANY] * 4,
        scratch_shapes=[
            pltpu.VMEM((4, rows, width), bf16),
            pltpu.VMEM((width, width), bf16),
            pltpu.VMEM((width, width), bf16),
            pltpu.SemaphoreType.DMA((4, rows // SEND)),
        ],
        compiler_params=PARAMS,
        name="add_states",
    )(
        device_ref,
        *[in_vmem(x) for x in (s_vm, k_vm, v_vm, g_vm)],
        own,
        other,
        *[in_vmem(x) for x in parts],
    )


def solution(mesh):
    spec = P(AXES, None)
    count = mesh.shape["outer"] * mesh.shape["inner"]
    return jax.shard_map(
        functools.partial(on_device, count),
        mesh=mesh,
        in_specs=(spec,) * 4,
        out_specs=(spec,) * 4,
        check_vma=False,
    )
```

```python
import functools

import jax
import jax.numpy as jnp
from jax import lax
from jax.experimental import pallas as pl
from jax.experimental.pallas import tpu as pltpu
from jax.sharding import PartitionSpec as P

E = 128
SUB = 256
CHUNK = 512
SEND = 512
WEIGHTS = (4, 4, 5, 3)
AXES = ("outer", "inner")
MIB = 1 << 20
ROWS_DIM = (((0,), (0,)), ((), ()))
COLS_DIM = (((1,), (1,)), ((), ()))
PLAIN = (((1,), (0,)), ((), ()))


def dot(a, b, dims):
    return lax.dot_general(a, b, dims, preferred_element_type=jnp.float32)


def scales(first, rows):
    place = first + lax.broadcasted_iota(jnp.int32, (rows, E), 0)
    return lax.rsqrt(place.astype(jnp.float32) + 1.0)


def keep_and_send(device, acc, where, keep_out, send_out):
    first, second = pl.ds(0, E), pl.ds(E, E)
    odd = (device & 1) == 1
    low, high = acc[first, first], acc[second, second]
    keep_out[where, :] = jnp.where(odd, high, low)
    send_out[where, :] = jnp.where(odd, low, high)


def sums_kernel(device_ref, k_hbm, v_hbm, q_hbm, g_hbm, k_out, v_out, s_out, g_out, before_out,
                after_out, keep_out, send_out, held, kv_acc, qg_acc, sems):
    rows, width = k_hbm.shape
    heads = width // E
    chunks = rows // CHUNK
    subs = CHUNK // SUB
    copies = []
    for c in range(chunks):
        at, back = pl.ds(c * CHUNK, CHUNK), pl.ds((chunks - 1 - c) * CHUNK, CHUNK)
        copies.append([
            pltpu.make_async_copy(k_hbm.at[at], k_out.at[at], sems.at[0, c]),
            pltpu.make_async_copy(v_hbm.at[at], v_out.at[at], sems.at[1, c]),
            pltpu.make_async_copy(q_hbm.at[back], held.at[back], sems.at[2, c]),
            pltpu.make_async_copy(g_hbm.at[back], g_out.at[back], sems.at[3, c]),
        ])
        for copy in copies[c]:
            copy.start()
    kv_acc[...] = jnp.zeros_like(kv_acc)
    qg_acc[...] = jnp.zeros_like(qg_acc)
    for c in range(chunks):
        for copy in copies[c][:2]:
            copy.wait()
        for i in range(subs):
            b = c * subs + i
            before_out[b] = kv_acc[...].astype(jnp.bfloat16)
            at = pl.ds(b * SUB, SUB)
            for h in range(heads):
                cols = pl.ds(h * E, E)
                kv_acc[cols, cols] += dot(k_out[at, cols], v_out[at, cols], ROWS_DIM)
        for copy in copies[c][2:]:
            copy.wait()
        for i in range(subs):
            b = rows // SUB - 1 - (c * subs + i)
            after_out[b] = qg_acc[...].astype(jnp.bfloat16)
            at = pl.ds(b * SUB, SUB)
            scale = scales(device_ref[0] * rows + b * SUB, SUB)
            for h in range(heads):
                cols = pl.ds(h * E, E)
                scaled = (held[at, cols].astype(jnp.float32) * scale).astype(jnp.bfloat16)
                s_out[at, cols] = scaled
                qg_acc[cols, cols] += dot(scaled, g_out[at, cols], ROWS_DIM)
    keep_and_send(device_ref[0], kv_acc, pl.ds(0, E), keep_out, send_out)
    keep_and_send(device_ref[0], qg_acc, pl.ds(E, E), keep_out, send_out)


def inner_kernel(first, blocks, device_ref, s_ref, k_ref, v_ref, g_ref, before_ref, after_ref,
                 *refs):
    att_ref, qgrad_ref, kgrad_ref, vgrad_ref, tick_ref = refs[-5:]
    tick_ref[...] = jnp.zeros_like(tick_ref)
    rows, width = s_ref.shape
    heads = width // E
    t = lax.broadcasted_iota(jnp.int32, (SUB, SUB), 0)
    s = lax.broadcasted_iota(jnp.int32, (SUB, SUB), 1)
    causal = s <= t

    def block(i):
        b = first + i
        at = pl.ds(b * SUB, SUB)
        scale = scales(device_ref[0] * rows + b * SUB, SUB)
        att_state = dot(s_ref[at, :], before_ref[b], PLAIN)
        qgrad_state = dot(g_ref[at, :], before_ref[b], COLS_DIM)
        kgrad_state = dot(v_ref[at, :], after_ref[b], COLS_DIM)
        vgrad_state = dot(k_ref[at, :], after_ref[b], PLAIN)
        for h in range(heads):
            cols = pl.ds(h * E, E)
            part = slice(h * E, (h + 1) * E)
            sh, kh, vh, gh = s_ref[at, cols], k_ref[at, cols], v_ref[at, cols], g_ref[at, cols]
            a = jnp.where(causal, dot(sh, kh, COLS_DIM), 0.0).astype(jnp.bfloat16)
            m = jnp.where(causal, dot(gh, vh, COLS_DIM), 0.0).astype(jnp.bfloat16)
            att_ref[at, cols] = (dot(a, vh, PLAIN) + att_state[:, part]).astype(jnp.bfloat16)
            qgrad_ref[at, cols] = (
                (dot(m, kh, PLAIN) + qgrad_state[:, part]) * scale
            ).astype(jnp.bfloat16)
            kgrad_ref[at, cols] = (dot(m, sh, ROWS_DIM) + kgrad_state[:, part]).astype(jnp.bfloat16)
            vgrad_ref[at, cols] = (dot(a, gh, ROWS_DIM) + vgrad_state[:, part]).astype(jnp.bfloat16)

    for i in range(blocks):
        block(i)


def bit_of(device_ref, bit):
    return (lax.shift_right_logical(device_ref[0], bit) & 1) == 1


def add_kernel(device_ref, mine_ref, came_ref, tick_ref, out_ref):
    out_ref[...] = mine_ref[...] + came_ref[...]


def pick_kernel(bit, device_ref, mine_ref, came_ref, out_ref):
    up, down = pl.ds(0, E), pl.ds(E, E)
    out_ref[...] = jnp.where(
        bit_of(device_ref, bit), mine_ref[down, :] + came_ref[down, :],
        mine_ref[up, :] + came_ref[up, :],
    )


def combine_kernel(device_ref, keep_ref, beside_ref, last_ref, tick_ref, *refs):
    came, (own_ref, given_ref) = refs[:-2], refs[-2:]
    odd = bit_of(device_ref, 0)
    for upward, part in ((True, pl.ds(0, E)), (False, pl.ds(E, E))):

        def chosen(bit, value):
            there = bit_of(device_ref, bit)
            return jnp.where(there, value, 0.0) if upward else jnp.where(there, 0.0, value)

        total = chosen(len(came) + 1, last_ref[...])
        for r, ref in enumerate(came):
            total = total + chosen(r + 1, ref[part, :])
        beside, keep = beside_ref[part, :], keep_ref[part, :]
        own_ref[part, :] = total + chosen(0, beside)
        given_ref[part, :] = total + (keep - chosen(0, keep))


def last_kernel(mine, device_ref, s_ref, k_ref, v_ref, g_ref, state_ref, *refs):
    att, qgrad, kgrad, vgrad = refs[:4]
    outs, (held, plain, turned, sems) = refs[-8:-4], refs[-4:]
    rows, width = s_ref.shape
    head = device_ref[0] & 1
    if not mine:
        head = 1 - head
    cols = pl.ds(pl.multiple_of(head * E, E), E)
    up, down = pl.ds(0, E), pl.ds(E, E)
    plain[...] = jnp.zeros_like(plain)
    turned[...] = jnp.zeros_like(turned)
    for part in (up, down):
        state = state_ref[part, :]
        plain[part, part] = state.astype(jnp.bfloat16)
        turned[part, part] = state.T.astype(jnp.bfloat16)
    copies = []
    for c in range(rows // SEND):
        for i in range(SEND // SUB):
            b = c * (SEND // SUB) + i
            at = pl.ds(b * SUB, SUB)
            scale = scales(device_ref[0] * rows + b * SUB, SUB)
            left = jnp.concatenate([s_ref[at, cols], k_ref[at, cols]], axis=1)
            right = jnp.concatenate([g_ref[at, cols], v_ref[at, cols]], axis=1)
            first, second = dot(left, plain[...], PLAIN), dot(right, turned[...], PLAIN)
            sums = (first[:, :E], second[:, :E] * scale, second[:, E:], first[:, E:])
            for o, part in enumerate((att, qgrad, kgrad, vgrad)):
                value = part[at, cols].astype(jnp.float32) + sums[o]
                held[o, at, :] = value.astype(jnp.bfloat16)
        at = pl.ds(c * SEND, SEND)
        for o in range(4):
            copy = pltpu.make_async_copy(held.at[o, at], outs[o].at[at, cols], sems.at[o, c])
            copy.start()
            copies.append(copy)
    for copy in copies:
        copy.wait()


VM = pl.BlockSpec(memory_space=pltpu.VMEM)
ANY = pl.BlockSpec(memory_space=pl.ANY)
SM = pl.BlockSpec(memory_space=pltpu.SMEM)
PARAMS = pltpu.CompilerParams(vmem_limit_bytes=24 * MIB, fuse_transposed_lhs_in_matmul=True)


def in_vmem(x):
    return pltpu.with_memory_space_constraint(x, pltpu.VMEM)


def in_hbm(x):
    return pltpu.with_memory_space_constraint(x, pltpu.HBM)


def from_others(keep, send, count, device_ref, work):
    def exchange(x, bit):
        return lax.ppermute(x, AXES, [(d, d ^ (1 << bit)) for d in range(count)])

    def call(kernel, outs, name, *operands):
        shapes = [jax.ShapeDtypeStruct(shape, jnp.float32) for shape in outs]
        return pl.pallas_call(
            kernel,
            out_shape=shapes,
            in_specs=[SM] + [VM] * len(operands),
            out_specs=[VM] * len(outs),
            compiler_params=PARAMS,
            name=name,
        )(device_ref, *operands)

    full, half = keep.shape, (E, E)
    last = count.bit_length() - 2
    beside = exchange(send, 0)
    tick = work(0, keep)
    [running] = call(add_kernel, [full], "add_round", keep, beside, tick)
    came = []
    for bit in range(1, last):
        came.append(exchange(running, bit))
        if bit < 3:
            tick = work(bit, running)
        if bit < last - 1:
            [running] = call(add_kernel, [full], "add_round", running, came[-1], tick)
    [picked] = call(functools.partial(pick_kernel, last), [half], "pick_half", running, came[-1])
    crossed = exchange(picked, last)
    tick = work(3, picked)
    own, given = call(combine_kernel, [full] * 2, "combine_rounds", keep, beside, crossed, tick, *came)
    return own, exchange(given, 0)


def on_device(count, query, keys, values, out_grad):
    rows, width = query.shape
    bf16 = jnp.bfloat16
    subs = rows // SUB
    chunks = rows // CHUNK
    device_ref = lax.axis_index(AXES).astype(jnp.int32).reshape(1)
    array = pltpu.VMEM((rows, width), bf16)
    states = pltpu.VMEM((subs, width, width), bf16)
    half = jax.ShapeDtypeStruct((2 * E, E), jnp.float32)

    k_vm, v_vm, s_vm, g_vm, before, after, keep, send = pl.pallas_call(
        sums_kernel,
        out_shape=(array,) * 4 + (states,) * 2 + (half,) * 2,
        in_specs=[SM] + [ANY] * 4,
        out_specs=[VM] * 8,
        scratch_shapes=[
            pltpu.VMEM((rows, width), bf16),
            pltpu.VMEM((width, width), jnp.float32),
            pltpu.VMEM((width, width), jnp.float32),
            pltpu.SemaphoreType.DMA((4, chunks)),
        ],
        compiler_params=PARAMS,
        name="sums",
    )(device_ref, *[in_hbm(x) for x in (keys, values, query, out_grad)])
    parts = []
    tick_shape = pltpu.VMEM((8, E), jnp.float32)

    def work(p, mark):
        first = subs * sum(WEIGHTS[:p]) // sum(WEIGHTS)
        blocks = subs * sum(WEIGHTS[:p + 1]) // sum(WEIGHTS) - first
        operands = [s_vm, k_vm, v_vm, g_vm, before, after, *parts]
        *parts[:], tick = pl.pallas_call(
            functools.partial(inner_kernel, first, blocks),
            out_shape=(array,) * 4 + (tick_shape,),
            in_specs=[SM] + [VM] * len(operands) + [ANY],
            out_specs=[VM] * 5,
            input_output_aliases={7 + o: o for o in range(len(parts))},
            compiler_params=PARAMS,
            cost_estimate=pl.CostEstimate(
                flops=575_000_000 * blocks, bytes_accessed=MIB * blocks, transcendentals=0
            ),
            name="within_blocks",
        )(device_ref, *[in_vmem(x) for x in operands], mark)
        return tick

    own, other = from_others(keep, send, count, device_ref, work)

    result = jax.ShapeDtypeStruct((rows, width), bf16)
    outs = ()
    for mine, state, name in ((True, own, "add_own_head"), (False, other, "add_other_head")):
        outs = pl.pallas_call(
            functools.partial(last_kernel, mine),
            out_shape=(result,) * 4,
            in_specs=[SM] + [VM] * 9 + [ANY] * len(outs),
            out_specs=[ANY] * 4,
            input_output_aliases={10 + o: o for o in range(len(outs))},
            scratch_shapes=[
                pltpu.VMEM((4, rows, E), bf16),
                pltpu.VMEM((2 * E, 2 * E), bf16),
                pltpu.VMEM((2 * E, 2 * E), bf16),
                pltpu.SemaphoreType.DMA((4, rows // SEND)),
            ],
            compiler_params=PARAMS,
            name=name,
        )(
            device_ref,
            *[in_vmem(x) for x in (s_vm, k_vm, v_vm, g_vm)],
            state,
            *[in_vmem(x) for x in parts],
            *[in_hbm(x) for x in outs],
        )
    return tuple(outs)


def solution(mesh):
    spec = P(AXES, None)
    count = mesh.shape["outer"] * mesh.shape["inner"]
    return jax.shard_map(
        functools.partial(on_device, count),
        mesh=mesh,
        in_specs=(spec,) * 4,
        out_specs=(spec,) * 4,
        check_vma=False,
    )
```

```python
import functools

import jax
import jax.numpy as jnp
from jax import lax
from jax.experimental import pallas as pl
from jax.experimental.pallas import tpu as pltpu
from jax.sharding import PartitionSpec as P

E = 128
SUB = 256
CHUNK = 512
SEND = 512
WEIGHTS = (3, 3, 7, 3)
AXES = ("outer", "inner")
MIB = 1 << 20
ROWS_DIM = (((0,), (0,)), ((), ()))
COLS_DIM = (((1,), (1,)), ((), ()))
PLAIN = (((1,), (0,)), ((), ()))


def dot(a, b, dims):
    return lax.dot_general(a, b, dims, preferred_element_type=jnp.float32)


def scales(first, rows):
    place = first + lax.broadcasted_iota(jnp.int32, (rows, E), 0)
    return lax.rsqrt(place.astype(jnp.float32) + 1.0)


def keep_and_send(device, acc, where, keep_out, send_out):
    odd = (device & 1) == 1
    low, high = acc[pl.ds(0, E), :], acc[pl.ds(E, E), :]
    keep_out[where, :] = jnp.where(odd, high, low)
    send_out[where, :] = jnp.where(odd, low, high)


def add_block(left, right, acc, states_out, b):
    heads = left.shape[1] // E
    new = dot(left, right, ROWS_DIM)
    for h in range(heads):
        cols = pl.ds(h * E, E)
        old = acc[cols, :]
        states_out[b, cols, cols] = old.astype(jnp.bfloat16)
        acc[cols, :] = old + new[h * E:(h + 1) * E, h * E:(h + 1) * E]
        for other in range(heads):
            if other != h:
                states_out[b, cols, pl.ds(other * E, E)] = jnp.zeros((E, E), jnp.bfloat16)


def sums_kernel(device_ref, k_hbm, v_hbm, q_hbm, g_hbm, k_out, v_out, s_out, g_out, before_out,
                after_out, keep_out, send_out, held, kv_acc, qg_acc, sems):
    rows, width = k_hbm.shape
    heads = width // E
    chunks = rows // CHUNK
    subs = CHUNK // SUB
    copies = []
    for c in range(chunks):
        at, back = pl.ds(c * CHUNK, CHUNK), pl.ds((chunks - 1 - c) * CHUNK, CHUNK)
        copies.append([
            pltpu.make_async_copy(k_hbm.at[at], k_out.at[at], sems.at[0, c]),
            pltpu.make_async_copy(v_hbm.at[at], v_out.at[at], sems.at[1, c]),
            pltpu.make_async_copy(q_hbm.at[back], held.at[back], sems.at[2, c]),
            pltpu.make_async_copy(g_hbm.at[back], g_out.at[back], sems.at[3, c]),
        ])
        for copy in copies[c]:
            copy.start()
    kv_acc[...] = jnp.zeros_like(kv_acc)
    qg_acc[...] = jnp.zeros_like(qg_acc)
    for c in range(chunks):
        for copy in copies[c][:2]:
            copy.wait()
        for i in range(subs):
            b = c * subs + i
            at = pl.ds(b * SUB, SUB)
            add_block(k_out[at, :], v_out[at, :], kv_acc, before_out, b)
        for copy in copies[c][2:]:
            copy.wait()
        for i in range(subs):
            b = rows // SUB - 1 - (c * subs + i)
            at = pl.ds(b * SUB, SUB)
            scale = jnp.concatenate([scales(device_ref[0] * rows + b * SUB, SUB)] * heads, axis=1)
            scaled = (held[at, :].astype(jnp.float32) * scale).astype(jnp.bfloat16)
            s_out[at, :] = scaled
            add_block(scaled, g_out[at, :], qg_acc, after_out, b)
    keep_and_send(device_ref[0], kv_acc, pl.ds(0, E), keep_out, send_out)
    keep_and_send(device_ref[0], qg_acc, pl.ds(E, E), keep_out, send_out)


def inner_kernel(first, blocks, device_ref, s_ref, k_ref, v_ref, g_ref, before_ref, after_ref,
                 *refs):
    att_ref, qgrad_ref, kgrad_ref, vgrad_ref, tick_ref = refs[-5:]
    tick_ref[...] = jnp.zeros_like(tick_ref)
    rows, width = s_ref.shape
    heads = width // E
    t = lax.broadcasted_iota(jnp.int32, (SUB, SUB), 0)
    s = lax.broadcasted_iota(jnp.int32, (SUB, SUB), 1)
    causal = s <= t

    def block(i):
        b = first + i
        at = pl.ds(b * SUB, SUB)
        scale = scales(device_ref[0] * rows + b * SUB, SUB)
        att_state = dot(s_ref[at, :], before_ref[b], PLAIN)
        qgrad_state = dot(g_ref[at, :], before_ref[b], COLS_DIM)
        kgrad_state = dot(v_ref[at, :], after_ref[b], COLS_DIM)
        vgrad_state = dot(k_ref[at, :], after_ref[b], PLAIN)
        for h in range(heads):
            cols = pl.ds(h * E, E)
            part = slice(h * E, (h + 1) * E)
            sh, kh, vh, gh = s_ref[at, cols], k_ref[at, cols], v_ref[at, cols], g_ref[at, cols]
            a = jnp.where(causal, dot(sh, kh, COLS_DIM), 0.0).astype(jnp.bfloat16)
            m = jnp.where(causal, dot(gh, vh, COLS_DIM), 0.0).astype(jnp.bfloat16)
            att_ref[at, cols] = (dot(a, vh, PLAIN) + att_state[:, part]).astype(jnp.bfloat16)
            qgrad_ref[at, cols] = (
                (dot(m, kh, PLAIN) + qgrad_state[:, part]) * scale
            ).astype(jnp.bfloat16)
            kgrad_ref[at, cols] = (dot(m, sh, ROWS_DIM) + kgrad_state[:, part]).astype(jnp.bfloat16)
            vgrad_ref[at, cols] = (dot(a, gh, ROWS_DIM) + vgrad_state[:, part]).astype(jnp.bfloat16)

    for i in range(blocks):
        block(i)


def bit_of(device_ref, bit):
    return (lax.shift_right_logical(device_ref[0], bit) & 1) == 1


def add_kernel(device_ref, mine_ref, came_ref, tick_ref, out_ref):
    out_ref[...] = mine_ref[...] + came_ref[...]


def pick_kernel(bit, device_ref, mine_ref, came_ref, out_ref):
    up, down = pl.ds(0, E), pl.ds(E, E)
    out_ref[...] = jnp.where(
        bit_of(device_ref, bit), mine_ref[down, :] + came_ref[down, :],
        mine_ref[up, :] + came_ref[up, :],
    )


def combine_kernel(device_ref, keep_ref, beside_ref, last_ref, tick_ref, *refs):
    came, (own_ref, given_ref) = refs[:-2], refs[-2:]
    odd = bit_of(device_ref, 0)
    for upward, part in ((True, pl.ds(0, E)), (False, pl.ds(E, E))):

        def chosen(bit, value):
            there = bit_of(device_ref, bit)
            return jnp.where(there, value, 0.0) if upward else jnp.where(there, 0.0, value)

        total = chosen(len(came) + 1, last_ref[...])
        for r, ref in enumerate(came):
            total = total + chosen(r + 1, ref[part, :])
        beside, keep = beside_ref[part, :], keep_ref[part, :]
        own_ref[part, :] = total + chosen(0, beside)
        given_ref[part, :] = total + (keep - chosen(0, keep))


def last_kernel(mine, device_ref, s_ref, k_ref, v_ref, g_ref, state_ref, *refs):
    att, qgrad, kgrad, vgrad = refs[:4]
    outs, (held, plain, turned, sems) = refs[-8:-4], refs[-4:]
    rows, width = s_ref.shape
    head = device_ref[0] & 1
    if not mine:
        head = 1 - head
    cols = pl.ds(pl.multiple_of(head * E, E), E)
    up, down = pl.ds(0, E), pl.ds(E, E)
    plain[...] = jnp.zeros_like(plain)
    turned[...] = jnp.zeros_like(turned)
    for part in (up, down):
        state = state_ref[part, :]
        plain[part, part] = state.astype(jnp.bfloat16)
        turned[part, part] = state.T.astype(jnp.bfloat16)
    copies = []
    for c in range(rows // SEND):
        for i in range(SEND // SUB):
            b = c * (SEND // SUB) + i
            at = pl.ds(b * SUB, SUB)
            scale = scales(device_ref[0] * rows + b * SUB, SUB)
            left = jnp.concatenate([s_ref[at, cols], k_ref[at, cols]], axis=1)
            right = jnp.concatenate([g_ref[at, cols], v_ref[at, cols]], axis=1)
            first, second = dot(left, plain[...], PLAIN), dot(right, turned[...], PLAIN)
            sums = (first[:, :E], second[:, :E] * scale, second[:, E:], first[:, E:])
            for o, part in enumerate((att, qgrad, kgrad, vgrad)):
                value = part[at, cols].astype(jnp.float32) + sums[o]
                held[o, at, :] = value.astype(jnp.bfloat16)
        at = pl.ds(c * SEND, SEND)
        for o in range(4):
            copy = pltpu.make_async_copy(held.at[o, at], outs[o].at[at, cols], sems.at[o, c])
            copy.start()
            copies.append(copy)
    for copy in copies:
        copy.wait()


VM = pl.BlockSpec(memory_space=pltpu.VMEM)
ANY = pl.BlockSpec(memory_space=pl.ANY)
SM = pl.BlockSpec(memory_space=pltpu.SMEM)
PARAMS = pltpu.CompilerParams(vmem_limit_bytes=24 * MIB)
FUSED = pltpu.CompilerParams(vmem_limit_bytes=24 * MIB, fuse_transposed_lhs_in_matmul=True)


def in_vmem(x):
    return pltpu.with_memory_space_constraint(x, pltpu.VMEM)


def in_hbm(x):
    return pltpu.with_memory_space_constraint(x, pltpu.HBM)


def from_others(keep, send, count, device_ref, work):
    def exchange(x, bit):
        return lax.ppermute(x, AXES, [(d, d ^ (1 << bit)) for d in range(count)])

    def call(kernel, outs, name, *operands):
        shapes = [jax.ShapeDtypeStruct(shape, jnp.float32) for shape in outs]
        return pl.pallas_call(
            kernel,
            out_shape=shapes,
            in_specs=[SM] + [VM] * len(operands),
            out_specs=[VM] * len(outs),
            compiler_params=PARAMS,
            name=name,
        )(device_ref, *operands)

    full, half = keep.shape, (E, E)
    last = count.bit_length() - 2
    beside = exchange(send, 0)
    tick = work(0, keep)
    [running] = call(add_kernel, [full], "add_round", keep, beside, tick)
    came = []
    for bit in range(1, last):
        came.append(exchange(running, bit))
        if bit < 3:
            tick = work(bit, running)
        if bit < last - 1:
            [running] = call(add_kernel, [full], "add_round", running, came[-1], tick)
    [picked] = call(functools.partial(pick_kernel, last), [half], "pick_half", running, came[-1])
    crossed = exchange(picked, last)
    tick = work(3, picked)
    own, given = call(combine_kernel, [full] * 2, "combine_rounds", keep, beside, crossed, tick, *came)
    return own, exchange(given, 0)


def on_device(count, query, keys, values, out_grad):
    rows, width = query.shape
    bf16 = jnp.bfloat16
    subs = rows // SUB
    chunks = rows // CHUNK
    device_ref = lax.axis_index(AXES).astype(jnp.int32).reshape(1)
    array = pltpu.VMEM((rows, width), bf16)
    states = pltpu.VMEM((subs, width, width), bf16)
    half = jax.ShapeDtypeStruct((2 * E, E), jnp.float32)

    k_vm, v_vm, s_vm, g_vm, before, after, keep, send = pl.pallas_call(
        sums_kernel,
        out_shape=(array,) * 4 + (states,) * 2 + (half,) * 2,
        in_specs=[SM] + [ANY] * 4,
        out_specs=[VM] * 8,
        scratch_shapes=[
            pltpu.VMEM((rows, width), bf16),
            pltpu.VMEM((width, E), jnp.float32),
            pltpu.VMEM((width, E), jnp.float32),
            pltpu.SemaphoreType.DMA((4, chunks)),
        ],
        compiler_params=PARAMS,
        name="sums",
    )(device_ref, *[in_hbm(x) for x in (keys, values, query, out_grad)])
    parts = []
    tick_shape = pltpu.VMEM((8, E), jnp.float32)

    def work(p, mark):
        first = subs * sum(WEIGHTS[:p]) // sum(WEIGHTS)
        blocks = subs * sum(WEIGHTS[:p + 1]) // sum(WEIGHTS) - first
        operands = [s_vm, k_vm, v_vm, g_vm, before, after, *parts]
        *parts[:], tick = pl.pallas_call(
            functools.partial(inner_kernel, first, blocks),
            out_shape=(array,) * 4 + (tick_shape,),
            in_specs=[SM] + [VM] * len(operands) + [ANY],
            out_specs=[VM] * 5,
            input_output_aliases={7 + o: o for o in range(len(parts))},
            compiler_params=FUSED,
            cost_estimate=pl.CostEstimate(
                flops=575_000_000 * blocks, bytes_accessed=MIB * blocks, transcendentals=0
            ),
            name="within_blocks",
        )(device_ref, *[in_vmem(x) for x in operands], mark)
        return tick

    own, other = from_others(keep, send, count, device_ref, work)

    result = jax.ShapeDtypeStruct((rows, width), bf16)
    outs = ()
    for mine, state, name in ((True, own, "add_own_head"), (False, other, "add_other_head")):
        outs = pl.pallas_call(
            functools.partial(last_kernel, mine),
            out_shape=(result,) * 4,
            in_specs=[SM] + [VM] * 9 + [ANY] * len(outs),
            out_specs=[ANY] * 4,
            input_output_aliases={10 + o: o for o in range(len(outs))},
            scratch_shapes=[
                pltpu.VMEM((4, rows, E), bf16),
                pltpu.VMEM((2 * E, 2 * E), bf16),
                pltpu.VMEM((2 * E, 2 * E), bf16),
                pltpu.SemaphoreType.DMA((4, rows // SEND)),
            ],
            compiler_params=PARAMS,
            name=name,
        )(
            device_ref,
            *[in_vmem(x) for x in (s_vm, k_vm, v_vm, g_vm)],
            state,
            *[in_vmem(x) for x in parts],
            *[in_hbm(x) for x in outs],
        )
    return tuple(outs)


def solution(mesh):
    spec = P(AXES, None)
    count = mesh.shape["outer"] * mesh.shape["inner"]
    return jax.shard_map(
        functools.partial(on_device, count),
        mesh=mesh,
        in_specs=(spec,) * 4,
        out_specs=(spec,) * 4,
        check_vma=False,
    )
```

```python
import functools

import jax
import jax.numpy as jnp
from jax import lax
from jax.experimental import pallas as pl
from jax.experimental.pallas import tpu as pltpu
from jax.sharding import PartitionSpec as P

E = 128
SUB = 256
CHUNK = 1024
SEND = 512
WEIGHTS = (4, 4, 5, 1, 2)
AXES = ("outer", "inner")
MIB = 1 << 20
ROWS_DIM = (((0,), (0,)), ((), ()))
COLS_DIM = (((1,), (1,)), ((), ()))
PLAIN = (((1,), (0,)), ((), ()))


def dot(a, b, dims):
    return lax.dot_general(a, b, dims, preferred_element_type=jnp.float32)


def scales(first, rows):
    place = first + lax.broadcasted_iota(jnp.int32, (rows, E), 0)
    return lax.rsqrt(place.astype(jnp.float32) + 1.0)


def keep_and_send(device, acc, where, keep_out, send_out):
    odd = (device & 1) == 1
    low, high = acc[pl.ds(0, E), :], acc[pl.ds(E, E), :]
    keep_out[where, :] = jnp.where(odd, high, low)
    send_out[where, :] = jnp.where(odd, low, high)


def add_block(left, right, acc, states_out, b):
    heads = left.shape[1] // E
    for h in range(heads):
        cols, part = pl.ds(h * E, E), slice(h * E, (h + 1) * E)
        old = acc[cols, :]
        states_out[b, cols, cols] = old.astype(jnp.bfloat16)
        acc[cols, :] = old + dot(left[:, part], right[:, part], ROWS_DIM)
        for other in range(heads):
            if other != h:
                states_out[b, cols, pl.ds(other * E, E)] = jnp.zeros((E, E), jnp.bfloat16)


def sums_kernel(device_ref, k_hbm, v_hbm, q_hbm, g_hbm, k_out, v_out, s_out, g_out, before_out,
                after_out, keep_out, send_out, held, kv_acc, qg_acc, sems):
    rows, width = k_hbm.shape
    heads = width // E
    chunks = rows // CHUNK
    subs = CHUNK // SUB
    copies = []
    for c in range(chunks):
        at, back = pl.ds(c * CHUNK, CHUNK), pl.ds((chunks - 1 - c) * CHUNK, CHUNK)
        copies.append([
            pltpu.make_async_copy(k_hbm.at[at], k_out.at[at], sems.at[0, c]),
            pltpu.make_async_copy(v_hbm.at[at], v_out.at[at], sems.at[1, c]),
            pltpu.make_async_copy(q_hbm.at[back], held.at[back], sems.at[2, c]),
            pltpu.make_async_copy(g_hbm.at[back], g_out.at[back], sems.at[3, c]),
        ])
        for copy in copies[c]:
            copy.start()
    kv_acc[...] = jnp.zeros_like(kv_acc)
    qg_acc[...] = jnp.zeros_like(qg_acc)
    for c in range(chunks):
        for copy in copies[c]:
            copy.wait()
        for i in range(subs):
            b = c * subs + i
            at = pl.ds(b * SUB, SUB)
            add_block(k_out[at, :], v_out[at, :], kv_acc, before_out, b)
            b = rows // SUB - 1 - b
            at = pl.ds(b * SUB, SUB)
            scale = jnp.concatenate([scales(device_ref[0] * rows + b * SUB, SUB)] * heads, axis=1)
            scaled = (held[at, :].astype(jnp.float32) * scale).astype(jnp.bfloat16)
            s_out[at, :] = scaled
            add_block(scaled, g_out[at, :], qg_acc, after_out, b)
    keep_and_send(device_ref[0], kv_acc, pl.ds(0, E), keep_out, send_out)
    keep_and_send(device_ref[0], qg_acc, pl.ds(E, E), keep_out, send_out)


def inner_kernel(first, blocks, device_ref, s_ref, k_ref, v_ref, g_ref, before_ref, after_ref,
                 *refs):
    att_ref, qgrad_ref, kgrad_ref, vgrad_ref, tick_ref = refs[-5:]
    tick_ref[...] = jnp.zeros_like(tick_ref)
    rows, width = s_ref.shape
    heads = width // E
    t = lax.broadcasted_iota(jnp.int32, (SUB, SUB), 0)
    s = lax.broadcasted_iota(jnp.int32, (SUB, SUB), 1)
    causal = s <= t

    def block(i):
        b = first + i
        at = pl.ds(b * SUB, SUB)
        scale = scales(device_ref[0] * rows + b * SUB, SUB)
        att_state = dot(s_ref[at, :], before_ref[b], PLAIN)
        qgrad_state = dot(g_ref[at, :], before_ref[b], COLS_DIM)
        kgrad_state = dot(v_ref[at, :], after_ref[b], COLS_DIM)
        vgrad_state = dot(k_ref[at, :], after_ref[b], PLAIN)
        for h in range(heads):
            cols = pl.ds(h * E, E)
            part = slice(h * E, (h + 1) * E)
            sh, kh, vh, gh = s_ref[at, cols], k_ref[at, cols], v_ref[at, cols], g_ref[at, cols]
            a = jnp.where(causal, dot(sh, kh, COLS_DIM), 0.0).astype(jnp.bfloat16)
            m = jnp.where(causal, dot(gh, vh, COLS_DIM), 0.0).astype(jnp.bfloat16)
            att_ref[at, cols] = (dot(a, vh, PLAIN) + att_state[:, part]).astype(jnp.bfloat16)
            qgrad_ref[at, cols] = (
                (dot(m, kh, PLAIN) + qgrad_state[:, part]) * scale
            ).astype(jnp.bfloat16)
            kgrad_ref[at, cols] = (dot(m, sh, ROWS_DIM) + kgrad_state[:, part]).astype(jnp.bfloat16)
            vgrad_ref[at, cols] = (dot(a, gh, ROWS_DIM) + vgrad_state[:, part]).astype(jnp.bfloat16)

    for i in range(blocks):
        block(i)


def bit_of(device_ref, bit):
    return (lax.shift_right_logical(device_ref[0], bit) & 1) == 1


def add_kernel(device_ref, mine_ref, came_ref, tick_ref, out_ref):
    out_ref[...] = mine_ref[...] + came_ref[...]


def pick_kernel(bit, device_ref, mine_ref, came_ref, tick_ref, out_ref):
    up, down = pl.ds(0, E), pl.ds(E, E)
    out_ref[...] = jnp.where(
        bit_of(device_ref, bit), mine_ref[down, :] + came_ref[down, :],
        mine_ref[up, :] + came_ref[up, :],
    )


def combine_kernel(device_ref, keep_ref, beside_ref, last_ref, tick_ref, *refs):
    came, (own_ref, given_ref) = refs[:-2], refs[-2:]
    odd = bit_of(device_ref, 0)
    for upward, part in ((True, pl.ds(0, E)), (False, pl.ds(E, E))):

        def chosen(bit, value):
            there = bit_of(device_ref, bit)
            return jnp.where(there, value, 0.0) if upward else jnp.where(there, 0.0, value)

        total = chosen(len(came) + 1, last_ref[...])
        for r, ref in enumerate(came):
            total = total + chosen(r + 1, ref[part, :])
        beside, keep = beside_ref[part, :], keep_ref[part, :]
        own_ref[part, :] = total + chosen(0, beside)
        given_ref[part, :] = total + (keep - chosen(0, keep))


def last_kernel(mine, device_ref, s_ref, k_ref, v_ref, g_ref, state_ref, *refs):
    att, qgrad, kgrad, vgrad = refs[:4]
    outs, (held, plain, turned, sems) = refs[-8:-4], refs[-4:]
    rows, width = s_ref.shape
    head = device_ref[0] & 1
    if not mine:
        head = 1 - head
    cols = pl.ds(pl.multiple_of(head * E, E), E)
    up, down = pl.ds(0, E), pl.ds(E, E)
    plain[...] = jnp.zeros_like(plain)
    turned[...] = jnp.zeros_like(turned)
    for part in (up, down):
        state = state_ref[part, :]
        plain[part, part] = state.astype(jnp.bfloat16)
        turned[part, part] = state.T.astype(jnp.bfloat16)
    copies = []
    for c in range(rows // SEND):
        for i in range(SEND // SUB):
            b = c * (SEND // SUB) + i
            at = pl.ds(b * SUB, SUB)
            scale = scales(device_ref[0] * rows + b * SUB, SUB)
            left = jnp.concatenate([s_ref[at, cols], k_ref[at, cols]], axis=1)
            right = jnp.concatenate([g_ref[at, cols], v_ref[at, cols]], axis=1)
            first, second = dot(left, plain[...], PLAIN), dot(right, turned[...], PLAIN)
            sums = (first[:, :E], second[:, :E] * scale, second[:, E:], first[:, E:])
            for o, part in enumerate((att, qgrad, kgrad, vgrad)):
                value = part[at, cols].astype(jnp.float32) + sums[o]
                held[o, at, :] = value.astype(jnp.bfloat16)
        at = pl.ds(c * SEND, SEND)
        for o in range(4):
            copy = pltpu.make_async_copy(held.at[o, at], outs[o].at[at, cols], sems.at[o, c])
            copy.start()
            copies.append(copy)
    for copy in copies:
        copy.wait()


VM = pl.BlockSpec(memory_space=pltpu.VMEM)
ANY = pl.BlockSpec(memory_space=pl.ANY)
SM = pl.BlockSpec(memory_space=pltpu.SMEM)
PARAMS = pltpu.CompilerParams(vmem_limit_bytes=24 * MIB)
FUSED = pltpu.CompilerParams(vmem_limit_bytes=24 * MIB, fuse_transposed_lhs_in_matmul=True)


def in_vmem(x):
    return pltpu.with_memory_space_constraint(x, pltpu.VMEM)


def in_hbm(x):
    return pltpu.with_memory_space_constraint(x, pltpu.HBM)


def from_others(keep, send, count, device_ref, work):
    def exchange(x, bit):
        return lax.ppermute(x, AXES, [(d, d ^ (1 << bit)) for d in range(count)])

    def call(kernel, outs, name, *operands):
        shapes = [jax.ShapeDtypeStruct(shape, jnp.float32) for shape in outs]
        return pl.pallas_call(
            kernel,
            out_shape=shapes,
            in_specs=[SM] + [VM] * len(operands),
            out_specs=[VM] * len(outs),
            compiler_params=PARAMS,
            name=name,
        )(device_ref, *operands)

    full, half = keep.shape, (E, E)
    last = count.bit_length() - 2
    beside = exchange(send, 0)
    tick = work(0, keep)
    [running] = call(add_kernel, [full], "add_round", keep, beside, tick)
    came = []
    for bit in range(1, last):
        came.append(exchange(running, bit))
        if bit < 3:
            tick = work(bit, running)
        if bit < last - 1:
            [running] = call(add_kernel, [full], "add_round", running, came[-1], tick)
    tick = work(3, running)
    [picked] = call(
        functools.partial(pick_kernel, last), [half], "pick_half", running, came[-1], tick
    )
    crossed = exchange(picked, last)
    tick = work(4, picked)
    own, given = call(combine_kernel, [full] * 2, "combine_rounds", keep, beside, crossed, tick, *came)
    return own, exchange(given, 0)


def on_device(count, query, keys, values, out_grad):
    rows, width = query.shape
    bf16 = jnp.bfloat16
    subs = rows // SUB
    chunks = rows // CHUNK
    device_ref = lax.axis_index(AXES).astype(jnp.int32).reshape(1)
    array = pltpu.VMEM((rows, width), bf16)
    states = pltpu.VMEM((subs, width, width), bf16)
    half = jax.ShapeDtypeStruct((2 * E, E), jnp.float32)

    k_vm, v_vm, s_vm, g_vm, before, after, keep, send = pl.pallas_call(
        sums_kernel,
        out_shape=(array,) * 4 + (states,) * 2 + (half,) * 2,
        in_specs=[SM] + [ANY] * 4,
        out_specs=[VM] * 8,
        scratch_shapes=[
            pltpu.VMEM((rows, width), bf16),
            pltpu.VMEM((width, E), jnp.float32),
            pltpu.VMEM((width, E), jnp.float32),
            pltpu.SemaphoreType.DMA((4, chunks)),
        ],
        compiler_params=PARAMS,
        name="sums",
    )(device_ref, *[in_hbm(x) for x in (keys, values, query, out_grad)])
    parts = []
    tick_shape = pltpu.VMEM((8, E), jnp.float32)

    def work(p, mark):
        first = subs * sum(WEIGHTS[:p]) // sum(WEIGHTS)
        blocks = subs * sum(WEIGHTS[:p + 1]) // sum(WEIGHTS) - first
        operands = [s_vm, k_vm, v_vm, g_vm, before, after, *parts]
        *parts[:], tick = pl.pallas_call(
            functools.partial(inner_kernel, first, blocks),
            out_shape=(array,) * 4 + (tick_shape,),
            in_specs=[SM] + [VM] * len(operands) + [ANY],
            out_specs=[VM] * 5,
            input_output_aliases={7 + o: o for o in range(len(parts))},
            compiler_params=FUSED,
            cost_estimate=pl.CostEstimate(
                flops=575_000_000 * blocks, bytes_accessed=MIB * blocks, transcendentals=0
            ),
            name="within_blocks",
        )(device_ref, *[in_vmem(x) for x in operands], mark)
        return tick

    own, other = from_others(keep, send, count, device_ref, work)

    result = jax.ShapeDtypeStruct((rows, width), bf16)
    outs = ()
    for mine, state, name in ((True, own, "add_own_head"), (False, other, "add_other_head")):
        outs = pl.pallas_call(
            functools.partial(last_kernel, mine),
            out_shape=(result,) * 4,
            in_specs=[SM] + [VM] * 9 + [ANY] * len(outs),
            out_specs=[ANY] * 4,
            input_output_aliases={10 + o: o for o in range(len(outs))},
            scratch_shapes=[
                pltpu.VMEM((4, rows, E), bf16),
                pltpu.VMEM((2 * E, 2 * E), bf16),
                pltpu.VMEM((2 * E, 2 * E), bf16),
                pltpu.SemaphoreType.DMA((4, rows // SEND)),
            ],
            compiler_params=PARAMS,
            name=name,
        )(
            device_ref,
            *[in_vmem(x) for x in (s_vm, k_vm, v_vm, g_vm)],
            state,
            *[in_vmem(x) for x in parts],
            *[in_hbm(x) for x in outs],
        )
    return tuple(outs)


def solution(mesh):
    spec = P(AXES, None)
    count = mesh.shape["outer"] * mesh.shape["inner"]
    return jax.shard_map(
        functools.partial(on_device, count),
        mesh=mesh,
        in_specs=(spec,) * 4,
        out_specs=(spec,) * 4,
        check_vma=False,
    )
```

```python
import functools

import jax
import jax.numpy as jnp
from jax import lax
from jax.experimental import pallas as pl
from jax.experimental.pallas import tpu as pltpu
from jax.sharding import PartitionSpec as P

E = 128
SUB = 256
CHUNK = 1024
SEND = 512
WEIGHTS = (2, 4, 6, 1, 3)
AXES = ("outer", "inner")
MIB = 1 << 20
ROWS_DIM = (((0,), (0,)), ((), ()))
COLS_DIM = (((1,), (1,)), ((), ()))
PLAIN = (((1,), (0,)), ((), ()))


def dot(a, b, dims):
    return lax.dot_general(a, b, dims, preferred_element_type=jnp.float32)


def scales(first, rows):
    place = first + lax.broadcasted_iota(jnp.int32, (rows, E), 0)
    return lax.rsqrt(place.astype(jnp.float32) + 1.0)


def head_columns(head):
    return pl.ds(pl.multiple_of(head * E, E), E)


def add_block(left, right, head, acc, states_out, b):
    cols = head_columns(head)
    states_out[b, cols, cols] = acc[...].astype(jnp.bfloat16)
    states_out[b, cols, head_columns(1 - head)] = jnp.zeros((E, E), jnp.bfloat16)
    acc[...] += dot(left, right, ROWS_DIM)


def head_sums(device_ref, head, blocks, k_ref, v_ref, q_ref, g_ref, s_out, before_out, after_out,
              kv_acc, qg_acc):
    rows = k_ref.shape[0]
    cols = head_columns(head)
    for b in blocks:
        at = pl.ds(b * SUB, SUB)
        add_block(k_ref[at, cols], v_ref[at, cols], head, kv_acc, before_out, b)
        b = rows // SUB - 1 - b
        at = pl.ds(b * SUB, SUB)
        scale = scales(device_ref[0] * rows + b * SUB, SUB)
        scaled = (q_ref[at, cols].astype(jnp.float32) * scale).astype(jnp.bfloat16)
        s_out[at, cols] = scaled
        add_block(scaled, g_ref[at, cols], head, qg_acc, after_out, b)


def sent_kernel(device_ref, k_hbm, v_hbm, q_hbm, g_hbm, k_out, v_out, q_out, g_out, s_out,
                before_out, after_out, send_out, kv_acc, qg_acc, sems):
    rows = k_hbm.shape[0]
    ends = list(range(CHUNK, rows, CHUNK)) + [rows - CHUNK // 2, rows]
    starts = [0] + ends[:-1]
    copies = []
    for c, (start, end) in enumerate(zip(starts, ends)):
        at, back = pl.ds(start, end - start), pl.ds(rows - end, end - start)
        copies.append([
            pltpu.make_async_copy(k_hbm.at[at], k_out.at[at], sems.at[0, c]),
            pltpu.make_async_copy(v_hbm.at[at], v_out.at[at], sems.at[1, c]),
            pltpu.make_async_copy(q_hbm.at[back], q_out.at[back], sems.at[2, c]),
            pltpu.make_async_copy(g_hbm.at[back], g_out.at[back], sems.at[3, c]),
        ])
        for copy in copies[c]:
            copy.start()
    kv_acc[...] = jnp.zeros_like(kv_acc)
    qg_acc[...] = jnp.zeros_like(qg_acc)
    head = 1 - (device_ref[0] & 1)
    for c, (start, end) in enumerate(zip(starts, ends)):
        for copy in copies[c]:
            copy.wait()
        head_sums(device_ref, head, range(start // SUB, end // SUB), k_out, v_out, q_out, g_out,
                  s_out, before_out, after_out, kv_acc, qg_acc)
    send_out[pl.ds(0, E), :] = kv_acc[...]
    send_out[pl.ds(E, E), :] = qg_acc[...]


def kept_kernel(device_ref, k_ref, v_ref, q_ref, g_ref, s_in, before_in, after_in, earlier, s_out,
                before_out, after_out, keep_out, kv_acc, qg_acc):
    kv_acc[...] = jnp.zeros_like(kv_acc)
    qg_acc[...] = jnp.zeros_like(qg_acc)
    head_sums(device_ref, device_ref[0] & 1, range(k_ref.shape[0] // SUB), k_ref, v_ref, q_ref,
              g_ref, s_out, before_out, after_out, kv_acc, qg_acc)
    keep_out[pl.ds(0, E), :] = kv_acc[...]
    keep_out[pl.ds(E, E), :] = qg_acc[...]


def inner_kernel(first, blocks, device_ref, s_ref, k_ref, v_ref, g_ref, before_ref, after_ref,
                 *refs):
    att_ref, qgrad_ref, kgrad_ref, vgrad_ref, tick_ref = refs[-5:]
    tick_ref[...] = jnp.zeros_like(tick_ref)
    rows, width = s_ref.shape
    heads = width // E
    t = lax.broadcasted_iota(jnp.int32, (SUB, SUB), 0)
    s = lax.broadcasted_iota(jnp.int32, (SUB, SUB), 1)
    causal = s <= t

    def block(i):
        b = first + i
        at = pl.ds(b * SUB, SUB)
        scale = scales(device_ref[0] * rows + b * SUB, SUB)
        att_state = dot(s_ref[at, :], before_ref[b], PLAIN)
        qgrad_state = dot(g_ref[at, :], before_ref[b], COLS_DIM)
        kgrad_state = dot(v_ref[at, :], after_ref[b], COLS_DIM)
        vgrad_state = dot(k_ref[at, :], after_ref[b], PLAIN)
        for h in range(heads):
            cols = pl.ds(h * E, E)
            part = slice(h * E, (h + 1) * E)
            sh, kh, vh, gh = s_ref[at, cols], k_ref[at, cols], v_ref[at, cols], g_ref[at, cols]
            a = jnp.where(causal, dot(sh, kh, COLS_DIM), 0.0).astype(jnp.bfloat16)
            m = jnp.where(causal, dot(gh, vh, COLS_DIM), 0.0).astype(jnp.bfloat16)
            att_ref[at, cols] = (dot(a, vh, PLAIN) + att_state[:, part]).astype(jnp.bfloat16)
            qgrad_ref[at, cols] = (
                (dot(m, kh, PLAIN) + qgrad_state[:, part]) * scale
            ).astype(jnp.bfloat16)
            kgrad_ref[at, cols] = (dot(m, sh, ROWS_DIM) + kgrad_state[:, part]).astype(jnp.bfloat16)
            vgrad_ref[at, cols] = (dot(a, gh, ROWS_DIM) + vgrad_state[:, part]).astype(jnp.bfloat16)

    for i in range(blocks):
        block(i)


def bit_of(device_ref, bit):
    return (lax.shift_right_logical(device_ref[0], bit) & 1) == 1


def add_kernel(device_ref, mine_ref, came_ref, tick_ref, out_ref):
    out_ref[...] = mine_ref[...] + came_ref[...]


def pick_kernel(bit, device_ref, mine_ref, came_ref, tick_ref, out_ref):
    up, down = pl.ds(0, E), pl.ds(E, E)
    out_ref[...] = jnp.where(
        bit_of(device_ref, bit), mine_ref[down, :] + came_ref[down, :],
        mine_ref[up, :] + came_ref[up, :],
    )


def combine_kernel(device_ref, keep_ref, beside_ref, last_ref, tick_ref, *refs):
    came, (own_ref, given_ref) = refs[:-2], refs[-2:]
    odd = bit_of(device_ref, 0)
    for upward, part in ((True, pl.ds(0, E)), (False, pl.ds(E, E))):

        def chosen(bit, value):
            there = bit_of(device_ref, bit)
            return jnp.where(there, value, 0.0) if upward else jnp.where(there, 0.0, value)

        total = chosen(len(came) + 1, last_ref[...])
        for r, ref in enumerate(came):
            total = total + chosen(r + 1, ref[part, :])
        beside, keep = beside_ref[part, :], keep_ref[part, :]
        own_ref[part, :] = total + chosen(0, beside)
        given_ref[part, :] = total + (keep - chosen(0, keep))


def last_kernel(mine, device_ref, s_ref, k_ref, v_ref, g_ref, state_ref, *refs):
    att, qgrad, kgrad, vgrad = refs[:4]
    outs, (held, plain, turned, sems) = refs[-8:-4], refs[-4:]
    rows, width = s_ref.shape
    head = device_ref[0] & 1
    if not mine:
        head = 1 - head
    cols = head_columns(head)
    up, down = pl.ds(0, E), pl.ds(E, E)
    plain[...] = jnp.zeros_like(plain)
    turned[...] = jnp.zeros_like(turned)
    for part in (up, down):
        state = state_ref[part, :]
        plain[part, part] = state.astype(jnp.bfloat16)
        turned[part, part] = state.T.astype(jnp.bfloat16)
    copies = []
    for c in range(rows // SEND):
        at = pl.ds(c * SEND, SEND)
        scale = scales(device_ref[0] * rows + c * SEND, SEND)
        left = jnp.concatenate([s_ref[at, cols], k_ref[at, cols]], axis=1)
        right = jnp.concatenate([g_ref[at, cols], v_ref[at, cols]], axis=1)
        first, second = dot(left, plain[...], PLAIN), dot(right, turned[...], PLAIN)
        sums = (first[:, :E], second[:, :E] * scale, second[:, E:], first[:, E:])
        for o, part in enumerate((att, qgrad, kgrad, vgrad)):
            value = part[at, cols].astype(jnp.float32) + sums[o]
            held[o, at, :] = value.astype(jnp.bfloat16)
        for o in range(4):
            copy = pltpu.make_async_copy(held.at[o, at], outs[o].at[at, cols], sems.at[o, c])
            copy.start()
            copies.append(copy)
    for copy in copies:
        copy.wait()


VM = pl.BlockSpec(memory_space=pltpu.VMEM)
ANY = pl.BlockSpec(memory_space=pl.ANY)
SM = pl.BlockSpec(memory_space=pltpu.SMEM)
PARAMS = pltpu.CompilerParams(vmem_limit_bytes=24 * MIB)
FUSED = pltpu.CompilerParams(vmem_limit_bytes=24 * MIB, fuse_transposed_lhs_in_matmul=True)


def in_vmem(x):
    return pltpu.with_memory_space_constraint(x, pltpu.VMEM)


def in_hbm(x):
    return pltpu.with_memory_space_constraint(x, pltpu.HBM)


def from_others(send, count, device_ref, keep_sums, work):
    def exchange(x, bit):
        return lax.ppermute(x, AXES, [(d, d ^ (1 << bit)) for d in range(count)])

    def call(kernel, outs, name, *operands):
        shapes = [jax.ShapeDtypeStruct(shape, jnp.float32) for shape in outs]
        return pl.pallas_call(
            kernel,
            out_shape=shapes,
            in_specs=[SM] + [VM] * len(operands),
            out_specs=[VM] * len(outs),
            compiler_params=PARAMS,
            name=name,
        )(device_ref, *operands)

    full, half = send.shape, (E, E)
    last = count.bit_length() - 2
    beside = exchange(send, 0)
    keep = keep_sums()
    tick = work(0, keep)
    [running] = call(add_kernel, [full], "add_round", keep, beside, tick)
    came = []
    for bit in range(1, last):
        came.append(exchange(running, bit))
        if bit < 3:
            tick = work(bit, running)
        if bit < last - 1:
            [running] = call(add_kernel, [full], "add_round", running, came[-1], tick)
    tick = work(3, running)
    [picked] = call(
        functools.partial(pick_kernel, last), [half], "pick_half", running, came[-1], tick
    )
    crossed = exchange(picked, last)
    tick = work(4, picked)
    own, given = call(combine_kernel, [full] * 2, "combine_rounds", keep, beside, crossed, tick, *came)
    return own, exchange(given, 0)


def on_device(count, query, keys, values, out_grad):
    rows, width = query.shape
    bf16 = jnp.bfloat16
    subs = rows // SUB
    chunks = rows // CHUNK
    device_ref = lax.axis_index(AXES).astype(jnp.int32).reshape(1)
    array = pltpu.VMEM((rows, width), bf16)
    states = pltpu.VMEM((subs, width, width), bf16)
    half = jax.ShapeDtypeStruct((2 * E, E), jnp.float32)

    sums = [pltpu.VMEM((E, E), jnp.float32)] * 2
    k_vm, v_vm, q_vm, g_vm, s_vm, before, after, send = pl.pallas_call(
        sent_kernel,
        out_shape=(array,) * 5 + (states,) * 2 + (half,),
        in_specs=[SM] + [ANY] * 4,
        out_specs=[VM] * 8,
        scratch_shapes=sums + [pltpu.SemaphoreType.DMA((4, chunks + 1))],
        compiler_params=PARAMS,
        name="sent_head_sums",
    )(device_ref, *[in_hbm(x) for x in (keys, values, query, out_grad)])

    def keep_sums():
        nonlocal s_vm, before, after
        operands = (k_vm, v_vm, q_vm, g_vm, s_vm, before, after)
        s_vm, before, after, keep = pl.pallas_call(
            kept_kernel,
            out_shape=(array,) + (states,) * 2 + (half,),
            in_specs=[SM] + [VM] * 7 + [ANY],
            out_specs=[VM] * 4,
            input_output_aliases={5: 0, 6: 1, 7: 2},
            scratch_shapes=sums,
            compiler_params=PARAMS,
            name="kept_head_sums",
        )(device_ref, *[in_vmem(x) for x in operands], send)
        return keep

    parts = []
    tick_shape = pltpu.VMEM((8, E), jnp.float32)

    def work(p, mark):
        first = subs * sum(WEIGHTS[:p]) // sum(WEIGHTS)
        blocks = subs * sum(WEIGHTS[:p + 1]) // sum(WEIGHTS) - first
        operands = [s_vm, k_vm, v_vm, g_vm, before, after, *parts]
        *parts[:], tick = pl.pallas_call(
            functools.partial(inner_kernel, first, blocks),
            out_shape=(array,) * 4 + (tick_shape,),
            in_specs=[SM] + [VM] * len(operands) + [ANY],
            out_specs=[VM] * 5,
            input_output_aliases={7 + o: o for o in range(len(parts))},
            compiler_params=FUSED,
            cost_estimate=pl.CostEstimate(
                flops=575_000_000 * blocks, bytes_accessed=MIB * blocks, transcendentals=0
            ),
            name="within_blocks",
        )(device_ref, *[in_vmem(x) for x in operands], mark)
        return tick

    own, other = from_others(send, count, device_ref, keep_sums, work)

    result = jax.ShapeDtypeStruct((rows, width), bf16)
    outs = ()
    for mine, state, name in ((True, own, "add_own_head"), (False, other, "add_other_head")):
        outs = pl.pallas_call(
            functools.partial(last_kernel, mine),
            out_shape=(result,) * 4,
            in_specs=[SM] + [VM] * 9 + [ANY] * len(outs),
            out_specs=[ANY] * 4,
            input_output_aliases={10 + o: o for o in range(len(outs))},
            scratch_shapes=[
                pltpu.VMEM((4, rows, E), bf16),
                pltpu.VMEM((2 * E, 2 * E), bf16),
                pltpu.VMEM((2 * E, 2 * E), bf16),
                pltpu.SemaphoreType.DMA((4, rows // SEND)),
            ],
            compiler_params=PARAMS,
            name=name,
        )(
            device_ref,
            *[in_vmem(x) for x in (s_vm, k_vm, v_vm, g_vm)],
            state,
            *[in_vmem(x) for x in parts],
            *[in_hbm(x) for x in outs],
        )
    return tuple(outs)


def solution(mesh):
    spec = P(AXES, None)
    count = mesh.shape["outer"] * mesh.shape["inner"]
    return jax.shard_map(
        functools.partial(on_device, count),
        mesh=mesh,
        in_specs=(spec,) * 4,
        out_specs=(spec,) * 4,
        check_vma=False,
    )
```

```python
import functools

import jax
import jax.numpy as jnp
from jax import lax
from jax.experimental import pallas as pl
from jax.experimental.pallas import tpu as pltpu
from jax.sharding import PartitionSpec as P

E = 128
SUB = 256
CHUNK = 1024
SEND = 256
WEIGHTS = (2, 4, 6, 1, 3)
AXES = ("outer", "inner")
MIB = 1 << 20
ROWS_DIM = (((0,), (0,)), ((), ()))
COLS_DIM = (((1,), (1,)), ((), ()))
PLAIN = (((1,), (0,)), ((), ()))


def dot(a, b, dims):
    return lax.dot_general(a, b, dims, preferred_element_type=jnp.float32)


def scales(first, rows):
    place = first + lax.broadcasted_iota(jnp.int32, (rows, E), 0)
    return lax.rsqrt(place.astype(jnp.float32) + 1.0)


def head_columns(head):
    return pl.ds(pl.multiple_of(head * E, E), E)


def add_block(left, right, head, acc, states_out, b):
    cols = head_columns(head)
    states_out[b, cols, cols] = acc[...].astype(jnp.bfloat16)
    states_out[b, cols, head_columns(1 - head)] = jnp.zeros((E, E), jnp.bfloat16)
    acc[...] += dot(left, right, ROWS_DIM)


def head_sums(device_ref, head, hbm, k_out, v_out, g_out, s_out, before_out, after_out, held,
              kv_acc, qg_acc, sems):
    k_hbm, v_hbm, q_hbm, g_hbm = hbm
    rows = k_hbm.shape[0]
    cols = head_columns(head)
    ends = list(range(CHUNK, rows, CHUNK)) + [rows - CHUNK // 2, rows]
    starts = [0] + ends[:-1]
    copies = []
    for c, (start, end) in enumerate(zip(starts, ends)):
        at, back = pl.ds(start, end - start), pl.ds(rows - end, end - start)
        copies.append([
            pltpu.make_async_copy(k_hbm.at[at, cols], k_out.at[at, cols], sems.at[0, c]),
            pltpu.make_async_copy(v_hbm.at[at, cols], v_out.at[at, cols], sems.at[1, c]),
            pltpu.make_async_copy(q_hbm.at[back, cols], held.at[back], sems.at[2, c]),
            pltpu.make_async_copy(g_hbm.at[back, cols], g_out.at[back, cols], sems.at[3, c]),
        ])
        for copy in copies[c]:
            copy.start()
    kv_acc[...] = jnp.zeros_like(kv_acc)
    qg_acc[...] = jnp.zeros_like(qg_acc)
    for c, (start, end) in enumerate(zip(starts, ends)):
        for copy in copies[c]:
            copy.wait()
        for b in range(start // SUB, end // SUB):
            at = pl.ds(b * SUB, SUB)
            add_block(k_out[at, cols], v_out[at, cols], head, kv_acc, before_out, b)
            b = rows // SUB - 1 - b
            at = pl.ds(b * SUB, SUB)
            scale = scales(device_ref[0] * rows + b * SUB, SUB)
            scaled = (held[at, :].astype(jnp.float32) * scale).astype(jnp.bfloat16)
            s_out[at, cols] = scaled
            add_block(scaled, g_out[at, cols], head, qg_acc, after_out, b)


def sums_kernel(kept, device_ref, *refs):
    hbm, refs = refs[:4], refs[-11:]
    outs, total_out, (held, kv_acc, qg_acc, sems) = refs[:6], refs[6], refs[7:]
    head = device_ref[0] & 1
    if not kept:
        head = 1 - head
    head_sums(device_ref, head, hbm, *outs, held, kv_acc, qg_acc, sems)
    total_out[pl.ds(0, E), :] = kv_acc[...]
    total_out[pl.ds(E, E), :] = qg_acc[...]


def inner_kernel(first, blocks, device_ref, s_ref, k_ref, v_ref, g_ref, before_ref, after_ref,
                 *refs):
    att_ref, qgrad_ref, kgrad_ref, vgrad_ref, tick_ref = refs[-5:]
    tick_ref[...] = jnp.zeros_like(tick_ref)
    rows, width = s_ref.shape
    heads = width // E
    t = lax.broadcasted_iota(jnp.int32, (SUB, SUB), 0)
    s = lax.broadcasted_iota(jnp.int32, (SUB, SUB), 1)
    causal = s <= t

    def block(i):
        b = first + i
        at = pl.ds(b * SUB, SUB)
        scale = scales(device_ref[0] * rows + b * SUB, SUB)
        att_state = dot(s_ref[at, :], before_ref[b], PLAIN)
        qgrad_state = dot(g_ref[at, :], before_ref[b], COLS_DIM)
        kgrad_state = dot(v_ref[at, :], after_ref[b], COLS_DIM)
        vgrad_state = dot(k_ref[at, :], after_ref[b], PLAIN)
        for h in range(heads):
            cols = pl.ds(h * E, E)
            part = slice(h * E, (h + 1) * E)
            sh, kh, vh, gh = s_ref[at, cols], k_ref[at, cols], v_ref[at, cols], g_ref[at, cols]
            a = jnp.where(causal, dot(sh, kh, COLS_DIM), 0.0).astype(jnp.bfloat16)
            m = jnp.where(causal, dot(gh, vh, COLS_DIM), 0.0).astype(jnp.bfloat16)
            att_ref[at, cols] = (dot(a, vh, PLAIN) + att_state[:, part]).astype(jnp.bfloat16)
            qgrad_ref[at, cols] = (
                (dot(m, kh, PLAIN) + qgrad_state[:, part]) * scale
            ).astype(jnp.bfloat16)
            kgrad_ref[at, cols] = (dot(m, sh, ROWS_DIM) + kgrad_state[:, part]).astype(jnp.bfloat16)
            vgrad_ref[at, cols] = (dot(a, gh, ROWS_DIM) + vgrad_state[:, part]).astype(jnp.bfloat16)

    for i in range(blocks):
        block(i)


def bit_of(device_ref, bit):
    return (lax.shift_right_logical(device_ref[0], bit) & 1) == 1


def add_kernel(device_ref, mine_ref, came_ref, tick_ref, out_ref):
    out_ref[...] = mine_ref[...] + came_ref[...]


def pick_kernel(bit, device_ref, mine_ref, came_ref, tick_ref, out_ref):
    up, down = pl.ds(0, E), pl.ds(E, E)
    out_ref[...] = jnp.where(
        bit_of(device_ref, bit), mine_ref[down, :] + came_ref[down, :],
        mine_ref[up, :] + came_ref[up, :],
    )


def combine_kernel(device_ref, keep_ref, beside_ref, last_ref, tick_ref, *refs):
    came, (own_ref, given_ref) = refs[:-2], refs[-2:]
    odd = bit_of(device_ref, 0)
    for upward, part in ((True, pl.ds(0, E)), (False, pl.ds(E, E))):

        def chosen(bit, value):
            there = bit_of(device_ref, bit)
            return jnp.where(there, value, 0.0) if upward else jnp.where(there, 0.0, value)

        total = chosen(len(came) + 1, last_ref[...])
        for r, ref in enumerate(came):
            total = total + chosen(r + 1, ref[part, :])
        beside, keep = beside_ref[part, :], keep_ref[part, :]
        own_ref[part, :] = total + chosen(0, beside)
        given_ref[part, :] = total + (keep - chosen(0, keep))


def last_kernel(mine, device_ref, s_ref, k_ref, v_ref, g_ref, state_ref, *refs):
    att, qgrad, kgrad, vgrad = refs[:4]
    outs, (held, plain, turned, sems) = refs[-8:-4], refs[-4:]
    rows, width = s_ref.shape
    head = device_ref[0] & 1
    if not mine:
        head = 1 - head
    cols = head_columns(head)
    up, down = pl.ds(0, E), pl.ds(E, E)
    plain[...] = jnp.zeros_like(plain)
    turned[...] = jnp.zeros_like(turned)
    for part in (up, down):
        state = state_ref[part, :]
        plain[part, part] = state.astype(jnp.bfloat16)
        turned[part, part] = state.T.astype(jnp.bfloat16)
    copies = []
    for c in range(rows // SEND):
        at = pl.ds(c * SEND, SEND)
        scale = scales(device_ref[0] * rows + c * SEND, SEND)
        left = jnp.concatenate([s_ref[at, cols], k_ref[at, cols]], axis=1)
        right = jnp.concatenate([g_ref[at, cols], v_ref[at, cols]], axis=1)
        first, second = dot(left, plain[...], PLAIN), dot(right, turned[...], PLAIN)
        sums = (first[:, :E], second[:, :E] * scale, second[:, E:], first[:, E:])
        for o, part in enumerate((att, qgrad, kgrad, vgrad)):
            value = part[at, cols].astype(jnp.float32) + sums[o]
            held[o, at, :] = value.astype(jnp.bfloat16)
        for o in range(4):
            copy = pltpu.make_async_copy(held.at[o, at], outs[o].at[at, cols], sems.at[o, c])
            copy.start()
            copies.append(copy)
    for copy in copies:
        copy.wait()


VM = pl.BlockSpec(memory_space=pltpu.VMEM)
ANY = pl.BlockSpec(memory_space=pl.ANY)
SM = pl.BlockSpec(memory_space=pltpu.SMEM)
PARAMS = pltpu.CompilerParams(vmem_limit_bytes=24 * MIB)
FUSED = pltpu.CompilerParams(vmem_limit_bytes=24 * MIB, fuse_transposed_lhs_in_matmul=True)


def in_vmem(x):
    return pltpu.with_memory_space_constraint(x, pltpu.VMEM)


def in_hbm(x):
    return pltpu.with_memory_space_constraint(x, pltpu.HBM)


def from_others(send, keep, count, device_ref, work):
    def exchange(x, bit):
        return lax.ppermute(x, AXES, [(d, d ^ (1 << bit)) for d in range(count)])

    def call(kernel, outs, name, *operands):
        shapes = [jax.ShapeDtypeStruct(shape, jnp.float32) for shape in outs]
        return pl.pallas_call(
            kernel,
            out_shape=shapes,
            in_specs=[SM] + [VM] * len(operands),
            out_specs=[VM] * len(outs),
            compiler_params=PARAMS,
            name=name,
        )(device_ref, *operands)

    full, half = send.shape, (E, E)
    last = count.bit_length() - 2
    beside = exchange(send, 0)
    tick = work(0, keep)
    [running] = call(add_kernel, [full], "add_round", keep, beside, tick)
    came = []
    for bit in range(1, last):
        came.append(exchange(running, bit))
        if bit < 3:
            tick = work(bit, running)
        if bit < last - 1:
            [running] = call(add_kernel, [full], "add_round", running, came[-1], tick)
    tick = work(3, running)
    [picked] = call(
        functools.partial(pick_kernel, last), [half], "pick_half", running, came[-1], tick
    )
    crossed = exchange(picked, last)
    tick = work(4, picked)
    own, given = call(combine_kernel, [full] * 2, "combine_rounds", keep, beside, crossed, tick, *came)
    return own, exchange(given, 0)


def on_device(count, query, keys, values, out_grad):
    rows, width = query.shape
    bf16 = jnp.bfloat16
    subs = rows // SUB
    chunks = rows // CHUNK
    device_ref = lax.axis_index(AXES).astype(jnp.int32).reshape(1)
    array = pltpu.VMEM((rows, width), bf16)
    states = pltpu.VMEM((subs, width, width), bf16)
    half = jax.ShapeDtypeStruct((2 * E, E), jnp.float32)

    def sums(kept, name, *filled):
        return pl.pallas_call(
            functools.partial(sums_kernel, kept),
            out_shape=(array,) * 4 + (states,) * 2 + (half,),
            in_specs=[SM] + [ANY] * 4 + [VM] * len(filled[:6]) + [ANY] * len(filled[6:]),
            out_specs=[VM] * 7,
            input_output_aliases={5 + o: o for o in range(len(filled[:6]))},
            scratch_shapes=[
                pltpu.VMEM((rows, E), bf16),
                pltpu.VMEM((E, E), jnp.float32),
                pltpu.VMEM((E, E), jnp.float32),
                pltpu.SemaphoreType.DMA((4, chunks + 1)),
            ],
            compiler_params=PARAMS,
            name=name,
        )(
            device_ref,
            *[in_hbm(x) for x in (keys, values, query, out_grad)],
            *[in_vmem(x) for x in filled[:6]],
            *filled[6:],
        )

    sent = sums(False, "sent_head_sums")
    send = sent[6]
    *filled, keep = sums(True, "kept_head_sums", *sent)
    k_vm, v_vm, g_vm, s_vm, before, after = filled

    parts = []
    tick_shape = pltpu.VMEM((8, E), jnp.float32)

    def work(p, mark):
        first = subs * sum(WEIGHTS[:p]) // sum(WEIGHTS)
        blocks = subs * sum(WEIGHTS[:p + 1]) // sum(WEIGHTS) - first
        operands = [s_vm, k_vm, v_vm, g_vm, before, after, *parts]
        *parts[:], tick = pl.pallas_call(
            functools.partial(inner_kernel, first, blocks),
            out_shape=(array,) * 4 + (tick_shape,),
            in_specs=[SM] + [VM] * len(operands) + [ANY],
            out_specs=[VM] * 5,
            input_output_aliases={7 + o: o for o in range(len(parts))},
            compiler_params=FUSED,
            cost_estimate=pl.CostEstimate(
                flops=575_000_000 * blocks, bytes_accessed=MIB * blocks, transcendentals=0
            ),
            name="within_blocks",
        )(device_ref, *[in_vmem(x) for x in operands], mark)
        return tick

    own, other = from_others(send, keep, count, device_ref, work)

    result = jax.ShapeDtypeStruct((rows, width), bf16)
    outs = ()
    for mine, state, name in ((True, own, "add_own_head"), (False, other, "add_other_head")):
        outs = pl.pallas_call(
            functools.partial(last_kernel, mine),
            out_shape=(result,) * 4,
            in_specs=[SM] + [VM] * 9 + [ANY] * len(outs),
            out_specs=[ANY] * 4,
            input_output_aliases={10 + o: o for o in range(len(outs))},
            scratch_shapes=[
                pltpu.VMEM((4, rows, E), bf16),
                pltpu.VMEM((2 * E, 2 * E), bf16),
                pltpu.VMEM((2 * E, 2 * E), bf16),
                pltpu.SemaphoreType.DMA((4, rows // SEND)),
            ],
            compiler_params=PARAMS,
            name=name,
        )(
            device_ref,
            *[in_vmem(x) for x in (s_vm, k_vm, v_vm, g_vm)],
            state,
            *[in_vmem(x) for x in parts],
            *[in_hbm(x) for x in outs],
        )
    return tuple(outs)


def solution(mesh):
    spec = P(AXES, None)
    count = mesh.shape["outer"] * mesh.shape["inner"]
    return jax.shard_map(
        functools.partial(on_device, count),
        mesh=mesh,
        in_specs=(spec,) * 4,
        out_specs=(spec,) * 4,
        check_vma=False,
    )
```

```python
import functools

import jax
import jax.numpy as jnp
from jax import lax
from jax.experimental import pallas as pl
from jax.experimental.pallas import tpu as pltpu
from jax.sharding import PartitionSpec as P

E = 128
SUB = 256
CHUNK = 1024
SEND = 512
WEIGHTS = (1, 4, 6, 1, 3, 1)
AXES = ("outer", "inner")
MIB = 1 << 20
ROWS_DIM = (((0,), (0,)), ((), ()))
COLS_DIM = (((1,), (1,)), ((), ()))
PLAIN = (((1,), (0,)), ((), ()))


def dot(a, b, dims):
    return lax.dot_general(a, b, dims, preferred_element_type=jnp.float32)


def scales(first, rows):
    place = first + lax.broadcasted_iota(jnp.int32, (rows, E), 0)
    return lax.rsqrt(place.astype(jnp.float32) + 1.0)


def head_columns(head):
    return pl.ds(pl.multiple_of(head * E, E), E)


def add_block(left, right, head, acc, states_out, b):
    cols = head_columns(head)
    states_out[b, cols, cols] = acc[...].astype(jnp.bfloat16)
    states_out[b, cols, head_columns(1 - head)] = jnp.zeros((E, E), jnp.bfloat16)
    acc[...] += dot(left, right, ROWS_DIM)


def head_sums(device_ref, head, hbm, k_out, v_out, g_out, s_out, before_out, after_out, held,
              kv_acc, qg_acc, sems):
    k_hbm, v_hbm, q_hbm, g_hbm = hbm
    rows = k_hbm.shape[0]
    cols = head_columns(head)
    ends = list(range(CHUNK, rows, CHUNK)) + [rows - CHUNK // 2, rows]
    starts = [0] + ends[:-1]
    copies = []
    for c, (start, end) in enumerate(zip(starts, ends)):
        at, back = pl.ds(start, end - start), pl.ds(rows - end, end - start)
        copies.append([
            pltpu.make_async_copy(k_hbm.at[at, cols], k_out.at[at, cols], sems.at[0, c]),
            pltpu.make_async_copy(v_hbm.at[at, cols], v_out.at[at, cols], sems.at[1, c]),
            pltpu.make_async_copy(q_hbm.at[back, cols], held.at[back], sems.at[2, c]),
            pltpu.make_async_copy(g_hbm.at[back, cols], g_out.at[back, cols], sems.at[3, c]),
        ])
        for copy in copies[c]:
            copy.start()
    kv_acc[...] = jnp.zeros_like(kv_acc)
    qg_acc[...] = jnp.zeros_like(qg_acc)
    for c, (start, end) in enumerate(zip(starts, ends)):
        for copy in copies[c]:
            copy.wait()
        for b in range(start // SUB, end // SUB):
            at = pl.ds(b * SUB, SUB)
            add_block(k_out[at, cols], v_out[at, cols], head, kv_acc, before_out, b)
            b = rows // SUB - 1 - b
            at = pl.ds(b * SUB, SUB)
            scale = scales(device_ref[0] * rows + b * SUB, SUB)
            scaled = (held[at, :].astype(jnp.float32) * scale).astype(jnp.bfloat16)
            s_out[at, cols] = scaled
            add_block(scaled, g_out[at, cols], head, qg_acc, after_out, b)


def sums_kernel(kept, device_ref, *refs):
    hbm, refs = refs[:4], refs[-11:]
    outs, total_out, (held, kv_acc, qg_acc, sems) = refs[:6], refs[6], refs[7:]
    head = device_ref[0] & 1
    if not kept:
        head = 1 - head
    head_sums(device_ref, head, hbm, *outs, held, kv_acc, qg_acc, sems)
    total_out[pl.ds(0, E), :] = kv_acc[...]
    total_out[pl.ds(E, E), :] = qg_acc[...]


def inner_kernel(first, blocks, device_ref, s_ref, k_ref, v_ref, g_ref, before_ref, after_ref,
                 *refs):
    att_ref, qgrad_ref, kgrad_ref, vgrad_ref, tick_ref = refs[-5:]
    tick_ref[...] = jnp.zeros_like(tick_ref)
    rows, width = s_ref.shape
    heads = width // E
    t = lax.broadcasted_iota(jnp.int32, (SUB, SUB), 0)
    s = lax.broadcasted_iota(jnp.int32, (SUB, SUB), 1)
    causal = s <= t

    def block(i):
        b = first + i
        at = pl.ds(b * SUB, SUB)
        scale = scales(device_ref[0] * rows + b * SUB, SUB)
        att_state = dot(s_ref[at, :], before_ref[b], PLAIN)
        qgrad_state = dot(g_ref[at, :], before_ref[b], COLS_DIM)
        kgrad_state = dot(v_ref[at, :], after_ref[b], COLS_DIM)
        vgrad_state = dot(k_ref[at, :], after_ref[b], PLAIN)
        for h in range(heads):
            cols = pl.ds(h * E, E)
            part = slice(h * E, (h + 1) * E)
            sh, kh, vh, gh = s_ref[at, cols], k_ref[at, cols], v_ref[at, cols], g_ref[at, cols]
            a = jnp.where(causal, dot(sh, kh, COLS_DIM), 0.0).astype(jnp.bfloat16)
            m = jnp.where(causal, dot(gh, vh, COLS_DIM), 0.0).astype(jnp.bfloat16)
            att_ref[at, cols] = (dot(a, vh, PLAIN) + att_state[:, part]).astype(jnp.bfloat16)
            qgrad_ref[at, cols] = (
                (dot(m, kh, PLAIN) + qgrad_state[:, part]) * scale
            ).astype(jnp.bfloat16)
            kgrad_ref[at, cols] = (dot(m, sh, ROWS_DIM) + kgrad_state[:, part]).astype(jnp.bfloat16)
            vgrad_ref[at, cols] = (dot(a, gh, ROWS_DIM) + vgrad_state[:, part]).astype(jnp.bfloat16)

    for i in range(blocks):
        block(i)


def bit_of(device_ref, bit):
    return (lax.shift_right_logical(device_ref[0], bit) & 1) == 1


def add_kernel(device_ref, mine_ref, came_ref, tick_ref, out_ref):
    out_ref[...] = mine_ref[...] + came_ref[...]


def pick_kernel(bit, device_ref, mine_ref, came_ref, tick_ref, out_ref):
    up, down = pl.ds(0, E), pl.ds(E, E)
    out_ref[...] = jnp.where(
        bit_of(device_ref, bit), mine_ref[down, :] + came_ref[down, :],
        mine_ref[up, :] + came_ref[up, :],
    )


def combine_kernel(device_ref, keep_ref, beside_ref, last_ref, tick_ref, *refs):
    came, (own_ref, given_ref) = refs[:-2], refs[-2:]
    odd = bit_of(device_ref, 0)
    for upward, part in ((True, pl.ds(0, E)), (False, pl.ds(E, E))):

        def chosen(bit, value):
            there = bit_of(device_ref, bit)
            return jnp.where(there, value, 0.0) if upward else jnp.where(there, 0.0, value)

        total = chosen(len(came) + 1, last_ref[...])
        for r, ref in enumerate(came):
            total = total + chosen(r + 1, ref[part, :])
        beside, keep = beside_ref[part, :], keep_ref[part, :]
        own_ref[part, :] = total + chosen(0, beside)
        given_ref[part, :] = total + (keep - chosen(0, keep))


def last_kernel(mine, device_ref, s_ref, k_ref, v_ref, g_ref, state_ref, *refs):
    att, qgrad, kgrad, vgrad = refs[:4]
    outs, (held, plain, turned, sems) = refs[-8:-4], refs[-4:]
    rows, width = s_ref.shape
    head = device_ref[0] & 1
    if not mine:
        head = 1 - head
    cols = head_columns(head)
    up, down = pl.ds(0, E), pl.ds(E, E)
    plain[...] = jnp.zeros_like(plain)
    turned[...] = jnp.zeros_like(turned)
    for part in (up, down):
        state = state_ref[part, :]
        plain[part, part] = state.astype(jnp.bfloat16)
        turned[part, part] = state.T.astype(jnp.bfloat16)
    copies = []
    for c in range(rows // SEND):
        at = pl.ds(c * SEND, SEND)
        scale = scales(device_ref[0] * rows + c * SEND, SEND)
        left = jnp.concatenate([s_ref[at, cols], k_ref[at, cols]], axis=1)
        right = jnp.concatenate([g_ref[at, cols], v_ref[at, cols]], axis=1)
        first, second = dot(left, plain[...], PLAIN), dot(right, turned[...], PLAIN)
        sums = (first[:, :E], second[:, :E] * scale, second[:, E:], first[:, E:])
        for o, part in enumerate((att, qgrad, kgrad, vgrad)):
            value = part[at, cols].astype(jnp.float32) + sums[o]
            held[o, at, :] = value.astype(jnp.bfloat16)
        for o in range(4):
            copy = pltpu.make_async_copy(held.at[o, at], outs[o].at[at, cols], sems.at[o, c])
            copy.start()
            copies.append(copy)
    for copy in copies:
        copy.wait()


VM = pl.BlockSpec(memory_space=pltpu.VMEM)
ANY = pl.BlockSpec(memory_space=pl.ANY)
SM = pl.BlockSpec(memory_space=pltpu.SMEM)
PARAMS = pltpu.CompilerParams(vmem_limit_bytes=24 * MIB)
FUSED = pltpu.CompilerParams(vmem_limit_bytes=24 * MIB, fuse_transposed_lhs_in_matmul=True)


def in_vmem(x):
    return pltpu.with_memory_space_constraint(x, pltpu.VMEM)


def in_hbm(x):
    return pltpu.with_memory_space_constraint(x, pltpu.HBM)


def from_others(send, keep, count, device_ref, work):
    def exchange(x, bit):
        return lax.ppermute(x, AXES, [(d, d ^ (1 << bit)) for d in range(count)])

    def call(kernel, outs, name, *operands):
        shapes = [jax.ShapeDtypeStruct(shape, jnp.float32) for shape in outs]
        return pl.pallas_call(
            kernel,
            out_shape=shapes,
            in_specs=[SM] + [VM] * len(operands),
            out_specs=[VM] * len(outs),
            compiler_params=PARAMS,
            name=name,
        )(device_ref, *operands)

    full, half = send.shape, (E, E)
    last = count.bit_length() - 2
    beside = exchange(send, 0)
    tick = work(0, keep)
    [running] = call(add_kernel, [full], "add_round", keep, beside, tick)
    came = []
    for bit in range(1, last):
        came.append(exchange(running, bit))
        if bit < 3:
            tick = work(bit, running)
        if bit < last - 1:
            [running] = call(add_kernel, [full], "add_round", running, came[-1], tick)
    tick = work(3, running)
    [picked] = call(
        functools.partial(pick_kernel, last), [half], "pick_half", running, came[-1], tick
    )
    crossed = exchange(picked, last)
    tick = work(4, picked)
    own, given = call(combine_kernel, [full] * 2, "combine_rounds", keep, beside, crossed, tick, *came)
    other = exchange(given, 0)
    work(5, given)
    return own, other


def on_device(count, query, keys, values, out_grad):
    rows, width = query.shape
    bf16 = jnp.bfloat16
    subs = rows // SUB
    chunks = rows // CHUNK
    device_ref = lax.axis_index(AXES).astype(jnp.int32).reshape(1)
    array = pltpu.VMEM((rows, width), bf16)
    states = pltpu.VMEM((subs, width, width), bf16)
    half = jax.ShapeDtypeStruct((2 * E, E), jnp.float32)

    def sums(kept, name, *filled):
        return pl.pallas_call(
            functools.partial(sums_kernel, kept),
            out_shape=(array,) * 4 + (states,) * 2 + (half,),
            in_specs=[SM] + [ANY] * 4 + [VM] * len(filled[:6]) + [ANY] * len(filled[6:]),
            out_specs=[VM] * 7,
            input_output_aliases={5 + o: o for o in range(len(filled[:6]))},
            scratch_shapes=[
                pltpu.VMEM((rows, E), bf16),
                pltpu.VMEM((E, E), jnp.float32),
                pltpu.VMEM((E, E), jnp.float32),
                pltpu.SemaphoreType.DMA((4, chunks + 1)),
            ],
            compiler_params=PARAMS,
            name=name,
        )(
            device_ref,
            *[in_hbm(x) for x in (keys, values, query, out_grad)],
            *[in_vmem(x) for x in filled[:6]],
            *filled[6:],
        )

    sent = sums(False, "sent_head_sums")
    send = sent[6]
    *filled, keep = sums(True, "kept_head_sums", *sent)
    k_vm, v_vm, g_vm, s_vm, before, after = filled

    parts = []
    tick_shape = pltpu.VMEM((8, E), jnp.float32)

    def work(p, mark):
        first = subs * sum(WEIGHTS[:p]) // sum(WEIGHTS)
        blocks = subs * sum(WEIGHTS[:p + 1]) // sum(WEIGHTS) - first
        operands = [s_vm, k_vm, v_vm, g_vm, before, after, *parts]
        *parts[:], tick = pl.pallas_call(
            functools.partial(inner_kernel, first, blocks),
            out_shape=(array,) * 4 + (tick_shape,),
            in_specs=[SM] + [VM] * len(operands) + [ANY],
            out_specs=[VM] * 5,
            input_output_aliases={7 + o: o for o in range(len(parts))},
            compiler_params=FUSED,
            cost_estimate=pl.CostEstimate(
                flops=575_000_000 * blocks, bytes_accessed=MIB * blocks, transcendentals=0
            ),
            name="within_blocks",
        )(device_ref, *[in_vmem(x) for x in operands], mark)
        return tick

    own, other = from_others(send, keep, count, device_ref, work)

    result = jax.ShapeDtypeStruct((rows, width), bf16)
    outs = ()
    for mine, state, name in ((True, own, "add_own_head"), (False, other, "add_other_head")):
        outs = pl.pallas_call(
            functools.partial(last_kernel, mine),
            out_shape=(result,) * 4,
            in_specs=[SM] + [VM] * 9 + [ANY] * len(outs),
            out_specs=[ANY] * 4,
            input_output_aliases={10 + o: o for o in range(len(outs))},
            scratch_shapes=[
                pltpu.VMEM((4, rows, E), bf16),
                pltpu.VMEM((2 * E, 2 * E), bf16),
                pltpu.VMEM((2 * E, 2 * E), bf16),
                pltpu.SemaphoreType.DMA((4, rows // SEND)),
            ],
            compiler_params=PARAMS,
            name=name,
        )(
            device_ref,
            *[in_vmem(x) for x in (s_vm, k_vm, v_vm, g_vm)],
            state,
            *[in_vmem(x) for x in parts],
            *[in_hbm(x) for x in outs],
        )
    return tuple(outs)


def solution(mesh):
    spec = P(AXES, None)
    count = mesh.shape["outer"] * mesh.shape["inner"]
    return jax.shard_map(
        functools.partial(on_device, count),
        mesh=mesh,
        in_specs=(spec,) * 4,
        out_specs=(spec,) * 4,
        check_vma=False,
    )
```

```python
import functools

import jax
import jax.numpy as jnp
from jax import lax
from jax.experimental import pallas as pl
from jax.experimental.pallas import tpu as pltpu
from jax.sharding import PartitionSpec as P

E = 128
SUB = 256
CHUNK = 1024
SEND = 1024
WEIGHTS = (1, 4, 7, 1, 3)
AXES = ("outer", "inner")
MIB = 1 << 20
ROWS_DIM = (((0,), (0,)), ((), ()))
COLS_DIM = (((1,), (1,)), ((), ()))
PLAIN = (((1,), (0,)), ((), ()))


def dot(a, b, dims):
    return lax.dot_general(a, b, dims, preferred_element_type=jnp.float32)


def scales(first, rows):
    place = first + lax.broadcasted_iota(jnp.int32, (rows, E), 0)
    return lax.rsqrt(place.astype(jnp.float32) + 1.0)


def head_columns(head):
    return pl.ds(pl.multiple_of(head * E, E), E)


def add_block(left, right, head, acc, states_out, b):
    cols = head_columns(head)
    states_out[b, cols, cols] = acc[...].astype(jnp.bfloat16)
    states_out[b, cols, head_columns(1 - head)] = jnp.zeros((E, E), jnp.bfloat16)
    acc[...] += dot(left, right, ROWS_DIM)


def head_sums(device_ref, head, hbm, k_out, v_out, g_out, s_out, before_out, after_out, held,
              kv_acc, qg_acc, sems):
    k_hbm, v_hbm, q_hbm, g_hbm = hbm
    rows = k_hbm.shape[0]
    cols = head_columns(head)
    ends = list(range(CHUNK, rows, CHUNK)) + [rows - CHUNK // 2, rows]
    starts = [0] + ends[:-1]
    copies = []
    for c, (start, end) in enumerate(zip(starts, ends)):
        at, back = pl.ds(start, end - start), pl.ds(rows - end, end - start)
        copies.append([
            pltpu.make_async_copy(k_hbm.at[at, cols], k_out.at[at, cols], sems.at[0, c]),
            pltpu.make_async_copy(v_hbm.at[at, cols], v_out.at[at, cols], sems.at[1, c]),
            pltpu.make_async_copy(q_hbm.at[back, cols], held.at[back], sems.at[2, c]),
            pltpu.make_async_copy(g_hbm.at[back, cols], g_out.at[back, cols], sems.at[3, c]),
        ])
        for copy in copies[c]:
            copy.start()
    kv_acc[...] = jnp.zeros_like(kv_acc)
    qg_acc[...] = jnp.zeros_like(qg_acc)
    for c, (start, end) in enumerate(zip(starts, ends)):
        for copy in copies[c]:
            copy.wait()
        for b in range(start // SUB, end // SUB):
            at = pl.ds(b * SUB, SUB)
            add_block(k_out[at, cols], v_out[at, cols], head, kv_acc, before_out, b)
            b = rows // SUB - 1 - b
            at = pl.ds(b * SUB, SUB)
            scale = scales(device_ref[0] * rows + b * SUB, SUB)
            scaled = (held[at, :].astype(jnp.float32) * scale).astype(jnp.bfloat16)
            s_out[at, cols] = scaled
            add_block(scaled, g_out[at, cols], head, qg_acc, after_out, b)


def sums_kernel(kept, device_ref, *refs):
    hbm, refs = refs[:4], refs[-11:]
    outs, total_out, (held, kv_acc, qg_acc, sems) = refs[:6], refs[6], refs[7:]
    head = device_ref[0] & 1
    if not kept:
        head = 1 - head
    head_sums(device_ref, head, hbm, *outs, held, kv_acc, qg_acc, sems)
    total_out[pl.ds(0, E), :] = kv_acc[...]
    total_out[pl.ds(E, E), :] = qg_acc[...]


def inner_kernel(first, blocks, device_ref, s_ref, k_ref, v_ref, g_ref, before_ref, after_ref,
                 *refs):
    att_ref, qgrad_ref, kgrad_ref, vgrad_ref, tick_ref = refs[-5:]
    tick_ref[...] = jnp.zeros_like(tick_ref)
    rows, width = s_ref.shape
    heads = width // E
    t = lax.broadcasted_iota(jnp.int32, (SUB, SUB), 0)
    s = lax.broadcasted_iota(jnp.int32, (SUB, SUB), 1)
    causal = s <= t

    def block(i):
        b = first + i
        at = pl.ds(b * SUB, SUB)
        scale = scales(device_ref[0] * rows + b * SUB, SUB)
        att_state = dot(s_ref[at, :], before_ref[b], PLAIN)
        qgrad_state = dot(g_ref[at, :], before_ref[b], COLS_DIM)
        kgrad_state = dot(v_ref[at, :], after_ref[b], COLS_DIM)
        vgrad_state = dot(k_ref[at, :], after_ref[b], PLAIN)
        for h in range(heads):
            cols = pl.ds(h * E, E)
            part = slice(h * E, (h + 1) * E)
            sh, kh, vh, gh = s_ref[at, cols], k_ref[at, cols], v_ref[at, cols], g_ref[at, cols]
            a = jnp.where(causal, dot(sh, kh, COLS_DIM), 0.0).astype(jnp.bfloat16)
            m = jnp.where(causal, dot(gh, vh, COLS_DIM), 0.0).astype(jnp.bfloat16)
            att_ref[at, cols] = (dot(a, vh, PLAIN) + att_state[:, part]).astype(jnp.bfloat16)
            qgrad_ref[at, cols] = (
                (dot(m, kh, PLAIN) + qgrad_state[:, part]) * scale
            ).astype(jnp.bfloat16)
            kgrad_ref[at, cols] = (dot(m, sh, ROWS_DIM) + kgrad_state[:, part]).astype(jnp.bfloat16)
            vgrad_ref[at, cols] = (dot(a, gh, ROWS_DIM) + vgrad_state[:, part]).astype(jnp.bfloat16)

    for i in range(blocks):
        block(i)


def bit_of(device_ref, bit):
    return (lax.shift_right_logical(device_ref[0], bit) & 1) == 1


def add_kernel(device_ref, mine_ref, came_ref, tick_ref, out_ref):
    out_ref[...] = mine_ref[...] + came_ref[...]


def pick_kernel(bit, device_ref, mine_ref, came_ref, tick_ref, out_ref):
    up, down = pl.ds(0, E), pl.ds(E, E)
    out_ref[...] = jnp.where(
        bit_of(device_ref, bit), mine_ref[down, :] + came_ref[down, :],
        mine_ref[up, :] + came_ref[up, :],
    )


def combine_kernel(device_ref, keep_ref, beside_ref, last_ref, tick_ref, *refs):
    came, (own_ref, given_ref) = refs[:-2], refs[-2:]
    odd = bit_of(device_ref, 0)
    for upward, part in ((True, pl.ds(0, E)), (False, pl.ds(E, E))):

        def chosen(bit, value):
            there = bit_of(device_ref, bit)
            return jnp.where(there, value, 0.0) if upward else jnp.where(there, 0.0, value)

        total = chosen(len(came) + 1, last_ref[...])
        for r, ref in enumerate(came):
            total = total + chosen(r + 1, ref[part, :])
        beside, keep = beside_ref[part, :], keep_ref[part, :]
        own_ref[part, :] = total + chosen(0, beside)
        given_ref[part, :] = total + (keep - chosen(0, keep))


def last_kernel(mine, device_ref, s_ref, k_ref, v_ref, g_ref, state_ref, *refs):
    att, qgrad, kgrad, vgrad = refs[:4]
    outs, (held, plain, turned, sems) = refs[-8:-4], refs[-4:]
    rows, width = s_ref.shape
    head = device_ref[0] & 1
    if not mine:
        head = 1 - head
    cols = head_columns(head)
    up, down = pl.ds(0, E), pl.ds(E, E)
    plain[...] = jnp.zeros_like(plain)
    turned[...] = jnp.zeros_like(turned)
    for part in (up, down):
        state = state_ref[part, :]
        plain[part, part] = state.astype(jnp.bfloat16)
        turned[part, part] = state.T.astype(jnp.bfloat16)
    copies = []
    for c in range(rows // SEND):
        at = pl.ds(c * SEND, SEND)
        scale = scales(device_ref[0] * rows + c * SEND, SEND)
        left = jnp.concatenate([s_ref[at, cols], k_ref[at, cols]], axis=1)
        right = jnp.concatenate([g_ref[at, cols], v_ref[at, cols]], axis=1)
        first, second = dot(left, plain[...], PLAIN), dot(right, turned[...], PLAIN)
        sums = (first[:, :E], second[:, :E] * scale, second[:, E:], first[:, E:])
        for o, part in enumerate((att, qgrad, kgrad, vgrad)):
            value = part[at, cols].astype(jnp.float32) + sums[o]
            held[o, at, :] = value.astype(jnp.bfloat16)
        for o in range(4):
            copy = pltpu.make_async_copy(held.at[o, at], outs[o].at[at, cols], sems.at[o, c])
            copy.start()
            copies.append(copy)
    for copy in copies:
        copy.wait()


VM = pl.BlockSpec(memory_space=pltpu.VMEM)
ANY = pl.BlockSpec(memory_space=pl.ANY)
SM = pl.BlockSpec(memory_space=pltpu.SMEM)
PARAMS = pltpu.CompilerParams(vmem_limit_bytes=24 * MIB)
FUSED = pltpu.CompilerParams(vmem_limit_bytes=24 * MIB, fuse_transposed_lhs_in_matmul=True)


def in_vmem(x):
    return pltpu.with_memory_space_constraint(x, pltpu.VMEM)


def in_hbm(x):
    return pltpu.with_memory_space_constraint(x, pltpu.HBM)


def from_others(send, keep, count, device_ref, work):
    def exchange(x, bit):
        return lax.ppermute(x, AXES, [(d, d ^ (1 << bit)) for d in range(count)])

    def call(kernel, outs, name, *operands):
        shapes = [jax.ShapeDtypeStruct(shape, jnp.float32) for shape in outs]
        return pl.pallas_call(
            kernel,
            out_shape=shapes,
            in_specs=[SM] + [VM] * len(operands),
            out_specs=[VM] * len(outs),
            compiler_params=PARAMS,
            name=name,
        )(device_ref, *operands)

    full, half = send.shape, (E, E)
    last = count.bit_length() - 2
    beside = exchange(send, 0)
    tick = work(0, keep)
    [running] = call(add_kernel, [full], "add_round", keep, beside, tick)
    came = []
    for bit in range(1, last):
        came.append(exchange(running, bit))
        if bit < 3:
            tick = work(bit, running)
        if bit < last - 1:
            [running] = call(add_kernel, [full], "add_round", running, came[-1], tick)
    tick = work(3, running)
    [picked] = call(
        functools.partial(pick_kernel, last), [half], "pick_half", running, came[-1], tick
    )
    crossed = exchange(picked, last)
    tick = work(4, picked)
    own, given = call(combine_kernel, [full] * 2, "combine_rounds", keep, beside, crossed, tick, *came)
    return own, exchange(given, 0)


def on_device(count, query, keys, values, out_grad):
    rows, width = query.shape
    bf16 = jnp.bfloat16
    subs = rows // SUB
    chunks = rows // CHUNK
    device_ref = lax.axis_index(AXES).astype(jnp.int32).reshape(1)
    array = pltpu.VMEM((rows, width), bf16)
    states = pltpu.VMEM((subs, width, width), bf16)
    half = jax.ShapeDtypeStruct((2 * E, E), jnp.float32)

    def sums(kept, name, *filled):
        return pl.pallas_call(
            functools.partial(sums_kernel, kept),
            out_shape=(array,) * 4 + (states,) * 2 + (half,),
            in_specs=[SM] + [ANY] * 4 + [VM] * len(filled[:6]) + [ANY] * len(filled[6:]),
            out_specs=[VM] * 7,
            input_output_aliases={5 + o: o for o in range(len(filled[:6]))},
            scratch_shapes=[
                pltpu.VMEM((rows, E), bf16),
                pltpu.VMEM((E, E), jnp.float32),
                pltpu.VMEM((E, E), jnp.float32),
                pltpu.SemaphoreType.DMA((4, chunks + 1)),
            ],
            compiler_params=PARAMS,
            name=name,
        )(
            device_ref,
            *[in_hbm(x) for x in (keys, values, query, out_grad)],
            *[in_vmem(x) for x in filled[:6]],
            *filled[6:],
        )

    sent = sums(False, "sent_head_sums")
    send = sent[6]
    *filled, keep = sums(True, "kept_head_sums", *sent)
    k_vm, v_vm, g_vm, s_vm, before, after = filled

    parts = []
    tick_shape = pltpu.VMEM((8, E), jnp.float32)

    def work(p, mark):
        first = subs * sum(WEIGHTS[:p]) // sum(WEIGHTS)
        blocks = subs * sum(WEIGHTS[:p + 1]) // sum(WEIGHTS) - first
        operands = [s_vm, k_vm, v_vm, g_vm, before, after, *parts]
        *parts[:], tick = pl.pallas_call(
            functools.partial(inner_kernel, first, blocks),
            out_shape=(array,) * 4 + (tick_shape,),
            in_specs=[SM] + [VM] * len(operands) + [ANY],
            out_specs=[VM] * 5,
            input_output_aliases={7 + o: o for o in range(len(parts))},
            compiler_params=FUSED,
            cost_estimate=pl.CostEstimate(
                flops=575_000_000 * blocks, bytes_accessed=MIB * blocks, transcendentals=0
            ),
            name="within_blocks",
        )(device_ref, *[in_vmem(x) for x in operands], mark)
        return tick

    own, other = from_others(send, keep, count, device_ref, work)

    result = jax.ShapeDtypeStruct((rows, width), bf16)
    outs = ()
    for mine, state, name in ((True, own, "add_own_head"), (False, other, "add_other_head")):
        outs = pl.pallas_call(
            functools.partial(last_kernel, mine),
            out_shape=(result,) * 4,
            in_specs=[SM] + [VM] * 9 + [ANY] * len(outs),
            out_specs=[ANY] * 4,
            input_output_aliases={10 + o: o for o in range(len(outs))},
            scratch_shapes=[
                pltpu.VMEM((4, rows, E), bf16),
                pltpu.VMEM((2 * E, 2 * E), bf16),
                pltpu.VMEM((2 * E, 2 * E), bf16),
                pltpu.SemaphoreType.DMA((4, rows // SEND)),
            ],
            compiler_params=PARAMS,
            name=name,
        )(
            device_ref,
            *[in_vmem(x) for x in (s_vm, k_vm, v_vm, g_vm)],
            state,
            *[in_vmem(x) for x in parts],
            *[in_hbm(x) for x in outs],
        )
    return tuple(outs)


def solution(mesh):
    spec = P(AXES, None)
    count = mesh.shape["outer"] * mesh.shape["inner"]
    return jax.shard_map(
        functools.partial(on_device, count),
        mesh=mesh,
        in_specs=(spec,) * 4,
        out_specs=(spec,) * 4,
        check_vma=False,
    )
```

```python
import functools

import jax
import jax.numpy as jnp
from jax import lax
from jax.experimental import pallas as pl
from jax.experimental.pallas import tpu as pltpu
from jax.sharding import PartitionSpec as P

E = 128
SUB = 256
CHUNK = 1024
SEND = 512
WEIGHTS = (1, 4, 6, 1, 3, 1)
AXES = ("outer", "inner")
MIB = 1 << 20
ROWS_DIM = (((0,), (0,)), ((), ()))
COLS_DIM = (((1,), (1,)), ((), ()))
PLAIN = (((1,), (0,)), ((), ()))


def dot(a, b, dims):
    return lax.dot_general(a, b, dims, preferred_element_type=jnp.float32)


def scales(first, rows):
    place = first + lax.broadcasted_iota(jnp.int32, (rows, E), 0)
    return lax.rsqrt(place.astype(jnp.float32) + 1.0)


def head_columns(head):
    return pl.ds(pl.multiple_of(head * E, E), E)


def add_block(left, right, head, acc, states_out, b):
    cols = head_columns(head)
    states_out[b, cols, cols] = acc[...].astype(jnp.bfloat16)
    states_out[b, cols, head_columns(1 - head)] = jnp.zeros((E, E), jnp.bfloat16)
    acc[...] += dot(left, right, ROWS_DIM)


def head_sums(device_ref, head, hbm, k_out, v_out, g_out, s_out, before_out, after_out, held,
              kv_acc, qg_acc, sems):
    k_hbm, v_hbm, q_hbm, g_hbm = hbm
    rows = k_hbm.shape[0]
    cols = head_columns(head)
    ends = list(range(CHUNK, rows, CHUNK)) + [rows - CHUNK // 2, rows]
    starts = [0] + ends[:-1]
    copies = []
    for c, (start, end) in enumerate(zip(starts, ends)):
        at, back = pl.ds(start, end - start), pl.ds(rows - end, end - start)
        copies.append([
            pltpu.make_async_copy(k_hbm.at[at, cols], k_out.at[at, cols], sems.at[0, c]),
            pltpu.make_async_copy(v_hbm.at[at, cols], v_out.at[at, cols], sems.at[1, c]),
            pltpu.make_async_copy(q_hbm.at[back, cols], held.at[back], sems.at[2, c]),
            pltpu.make_async_copy(g_hbm.at[back, cols], g_out.at[back, cols], sems.at[3, c]),
        ])
        for copy in copies[c]:
            copy.start()
    kv_acc[...] = jnp.zeros_like(kv_acc)
    qg_acc[...] = jnp.zeros_like(qg_acc)
    for c, (start, end) in enumerate(zip(starts, ends)):
        for copy in copies[c]:
            copy.wait()
        for b in range(start // SUB, end // SUB):
            at = pl.ds(b * SUB, SUB)
            add_block(k_out[at, cols], v_out[at, cols], head, kv_acc, before_out, b)
            b = rows // SUB - 1 - b
            at = pl.ds(b * SUB, SUB)
            scale = scales(device_ref[0] * rows + b * SUB, SUB)
            scaled = (held[at, :].astype(jnp.float32) * scale).astype(jnp.bfloat16)
            s_out[at, cols] = scaled
            add_block(scaled, g_out[at, cols], head, qg_acc, after_out, b)


def sums_kernel(kept, device_ref, *refs):
    hbm, refs = refs[:4], refs[-11:]
    outs, total_out, (held, kv_acc, qg_acc, sems) = refs[:6], refs[6], refs[7:]
    head = device_ref[0] & 1
    if not kept:
        head = 1 - head
    head_sums(device_ref, head, hbm, *outs, held, kv_acc, qg_acc, sems)
    total_out[pl.ds(0, E), :] = kv_acc[...]
    total_out[pl.ds(E, E), :] = qg_acc[...]


def inner_kernel(first, blocks, device_ref, s_ref, k_ref, v_ref, g_ref, before_ref, after_ref,
                 *refs):
    att_ref, qgrad_ref, kgrad_ref, vgrad_ref, tick_ref = refs[-5:]
    tick_ref[...] = jnp.zeros_like(tick_ref)
    rows, width = s_ref.shape
    heads = width // E
    t = lax.broadcasted_iota(jnp.int32, (SUB, SUB), 0)
    s = lax.broadcasted_iota(jnp.int32, (SUB, SUB), 1)
    causal = s <= t

    def block(i):
        b = first + i
        at = pl.ds(b * SUB, SUB)
        scale = scales(device_ref[0] * rows + b * SUB, SUB)
        att_state = dot(s_ref[at, :], before_ref[b], PLAIN)
        qgrad_state = dot(g_ref[at, :], before_ref[b], COLS_DIM)
        kgrad_state = dot(v_ref[at, :], after_ref[b], COLS_DIM)
        vgrad_state = dot(k_ref[at, :], after_ref[b], PLAIN)
        for h in range(heads):
            cols = pl.ds(h * E, E)
            part = slice(h * E, (h + 1) * E)
            sh, kh, vh, gh = s_ref[at, cols], k_ref[at, cols], v_ref[at, cols], g_ref[at, cols]
            a = jnp.where(causal, dot(sh, kh, COLS_DIM), 0.0).astype(jnp.bfloat16)
            m = jnp.where(causal, dot(gh, vh, COLS_DIM), 0.0).astype(jnp.bfloat16)
            att_ref[at, cols] = (dot(a, vh, PLAIN) + att_state[:, part]).astype(jnp.bfloat16)
            qgrad_ref[at, cols] = (
                (dot(m, kh, PLAIN) + qgrad_state[:, part]) * scale
            ).astype(jnp.bfloat16)
            kgrad_ref[at, cols] = (dot(m, sh, ROWS_DIM) + kgrad_state[:, part]).astype(jnp.bfloat16)
            vgrad_ref[at, cols] = (dot(a, gh, ROWS_DIM) + vgrad_state[:, part]).astype(jnp.bfloat16)

    for i in range(blocks):
        block(i)


def bit_of(device_ref, bit):
    return (lax.shift_right_logical(device_ref[0], bit) & 1) == 1


def add_kernel(device_ref, mine_ref, came_ref, tick_ref, out_ref):
    out_ref[...] = mine_ref[...] + came_ref[...]


def pick_kernel(bit, device_ref, mine_ref, came_ref, tick_ref, out_ref):
    up, down = pl.ds(0, E), pl.ds(E, E)
    out_ref[...] = jnp.where(
        bit_of(device_ref, bit), mine_ref[down, :] + came_ref[down, :],
        mine_ref[up, :] + came_ref[up, :],
    )


def combine_kernel(device_ref, keep_ref, beside_ref, last_ref, tick_ref, *refs):
    came, (own_ref, given_ref) = refs[:-2], refs[-2:]
    odd = bit_of(device_ref, 0)
    for upward, part in ((True, pl.ds(0, E)), (False, pl.ds(E, E))):

        def chosen(bit, value):
            there = bit_of(device_ref, bit)
            return jnp.where(there, value, 0.0) if upward else jnp.where(there, 0.0, value)

        total = chosen(len(came) + 1, last_ref[...])
        for r, ref in enumerate(came):
            total = total + chosen(r + 1, ref[part, :])
        beside, keep = beside_ref[part, :], keep_ref[part, :]
        own_ref[part, :] = total + chosen(0, beside)
        given_ref[part, :] = total + (keep - chosen(0, keep))


def last_kernel(mine, device_ref, s_ref, k_ref, v_ref, g_ref, state_ref, *refs):
    att, qgrad, kgrad, vgrad = refs[:4]
    outs, (held, plain, turned, sems) = refs[-8:-4], refs[-4:]
    rows, width = s_ref.shape
    head = device_ref[0] & 1
    if not mine:
        head = 1 - head
    cols = head_columns(head)
    up, down = pl.ds(0, E), pl.ds(E, E)
    plain[...] = jnp.zeros_like(plain)
    turned[...] = jnp.zeros_like(turned)
    for part in (up, down):
        state = state_ref[part, :]
        plain[part, part] = state.astype(jnp.bfloat16)
        turned[part, part] = state.T.astype(jnp.bfloat16)
    copies = []
    for c in range(rows // SEND):
        at = pl.ds(c * SEND, SEND)
        scale = scales(device_ref[0] * rows + c * SEND, SEND)
        left = jnp.concatenate([s_ref[at, cols], k_ref[at, cols]], axis=1)
        right = jnp.concatenate([g_ref[at, cols], v_ref[at, cols]], axis=1)
        first, second = dot(left, plain[...], PLAIN), dot(right, turned[...], PLAIN)
        sums = (first[:, :E], second[:, :E] * scale, second[:, E:], first[:, E:])
        for o, part in enumerate((att, qgrad, kgrad, vgrad)):
            value = part[at, cols].astype(jnp.float32) + sums[o]
            held[o, at, :] = value.astype(jnp.bfloat16)
        for o in range(4):
            copy = pltpu.make_async_copy(held.at[o, at], outs[o].at[at, cols], sems.at[o, c])
            copy.start()
            copies.append(copy)
    for copy in copies:
        copy.wait()


VM = pl.BlockSpec(memory_space=pltpu.VMEM)
ANY = pl.BlockSpec(memory_space=pl.ANY)
SM = pl.BlockSpec(memory_space=pltpu.SMEM)
PARAMS = pltpu.CompilerParams(vmem_limit_bytes=24 * MIB)
FUSED = pltpu.CompilerParams(vmem_limit_bytes=24 * MIB, fuse_transposed_lhs_in_matmul=True)


def in_vmem(x):
    return pltpu.with_memory_space_constraint(x, pltpu.VMEM)


def in_hbm(x):
    return pltpu.with_memory_space_constraint(x, pltpu.HBM)


def from_others(send, keep, count, device_ref, work):
    def exchange(x, bit):
        return lax.ppermute(x, AXES, [(d, d ^ (1 << bit)) for d in range(count)])

    def call(kernel, outs, name, *operands):
        shapes = [jax.ShapeDtypeStruct(shape, jnp.float32) for shape in outs]
        return pl.pallas_call(
            kernel,
            out_shape=shapes,
            in_specs=[SM] + [VM] * len(operands),
            out_specs=[VM] * len(outs),
            compiler_params=PARAMS,
            name=name,
        )(device_ref, *operands)

    full, half = send.shape, (E, E)
    last = count.bit_length() - 2
    beside = exchange(send, 0)
    tick = work(0, keep)
    [running] = call(add_kernel, [full], "add_round", keep, beside, tick)
    came = []
    for bit in range(1, last):
        came.append(exchange(running, bit))
        if bit < 3:
            tick = work(bit, running)
        if bit < last - 1:
            [running] = call(add_kernel, [full], "add_round", running, came[-1], tick)
    tick = work(3, running)
    [picked] = call(
        functools.partial(pick_kernel, last), [half], "pick_half", running, came[-1], tick
    )
    crossed = exchange(picked, last)
    tick = work(4, picked)
    own, given = call(combine_kernel, [full] * 2, "combine_rounds", keep, beside, crossed, tick, *came)
    other = exchange(given, 0)
    work(5, given)
    return own, other


def on_device(count, query, keys, values, out_grad):
    rows, width = query.shape
    bf16 = jnp.bfloat16
    subs = rows // SUB
    chunks = rows // CHUNK
    device_ref = lax.axis_index(AXES).astype(jnp.int32).reshape(1)
    array = pltpu.VMEM((rows, width), bf16)
    states = pltpu.VMEM((subs, width, width), bf16)
    half = jax.ShapeDtypeStruct((2 * E, E), jnp.float32)

    def sums(kept, name, *filled):
        return pl.pallas_call(
            functools.partial(sums_kernel, kept),
            out_shape=(array,) * 4 + (states,) * 2 + (half,),
            in_specs=[SM] + [ANY] * 4 + [VM] * len(filled[:6]) + [ANY] * len(filled[6:]),
            out_specs=[VM] * 7,
            input_output_aliases={5 + o: o for o in range(len(filled[:6]))},
            scratch_shapes=[
                pltpu.VMEM((rows, E), bf16),
                pltpu.VMEM((E, E), jnp.float32),
                pltpu.VMEM((E, E), jnp.float32),
                pltpu.SemaphoreType.DMA((4, chunks + 1)),
            ],
            compiler_params=FUSED,
            name=name,
        )(
            device_ref,
            *[in_hbm(x) for x in (keys, values, query, out_grad)],
            *[in_vmem(x) for x in filled[:6]],
            *filled[6:],
        )

    sent = sums(False, "sent_head_sums")
    send = sent[6]
    *filled, keep = sums(True, "kept_head_sums", *sent)
    k_vm, v_vm, g_vm, s_vm, before, after = filled

    parts = []
    tick_shape = pltpu.VMEM((8, E), jnp.float32)

    def work(p, mark):
        first = subs * sum(WEIGHTS[:p]) // sum(WEIGHTS)
        blocks = subs * sum(WEIGHTS[:p + 1]) // sum(WEIGHTS) - first
        operands = [s_vm, k_vm, v_vm, g_vm, before, after, *parts]
        *parts[:], tick = pl.pallas_call(
            functools.partial(inner_kernel, first, blocks),
            out_shape=(array,) * 4 + (tick_shape,),
            in_specs=[SM] + [VM] * len(operands) + [ANY],
            out_specs=[VM] * 5,
            input_output_aliases={7 + o: o for o in range(len(parts))},
            compiler_params=FUSED,
            cost_estimate=pl.CostEstimate(
                flops=575_000_000 * blocks, bytes_accessed=MIB * blocks, transcendentals=0
            ),
            name="within_blocks",
        )(device_ref, *[in_vmem(x) for x in operands], mark)
        return tick

    own, other = from_others(send, keep, count, device_ref, work)

    result = jax.ShapeDtypeStruct((rows, width), bf16)
    outs = ()
    for mine, state, name in ((True, own, "add_own_head"), (False, other, "add_other_head")):
        outs = pl.pallas_call(
            functools.partial(last_kernel, mine),
            out_shape=(result,) * 4,
            in_specs=[SM] + [VM] * 9 + [ANY] * len(outs),
            out_specs=[ANY] * 4,
            input_output_aliases={10 + o: o for o in range(len(outs))},
            scratch_shapes=[
                pltpu.VMEM((4, rows, E), bf16),
                pltpu.VMEM((2 * E, 2 * E), bf16),
                pltpu.VMEM((2 * E, 2 * E), bf16),
                pltpu.SemaphoreType.DMA((4, rows // SEND)),
            ],
            compiler_params=PARAMS,
            name=name,
        )(
            device_ref,
            *[in_vmem(x) for x in (s_vm, k_vm, v_vm, g_vm)],
            state,
            *[in_vmem(x) for x in parts],
            *[in_hbm(x) for x in outs],
        )
    return tuple(outs)


def solution(mesh):
    spec = P(AXES, None)
    count = mesh.shape["outer"] * mesh.shape["inner"]
    return jax.shard_map(
        functools.partial(on_device, count),
        mesh=mesh,
        in_specs=(spec,) * 4,
        out_specs=(spec,) * 4,
        check_vma=False,
    )
```

```python
import functools

import jax
import jax.numpy as jnp
from jax import lax
from jax.experimental import pallas as pl
from jax.experimental.pallas import tpu as pltpu
from jax.sharding import PartitionSpec as P

E = 128
SUB = 256
CHUNK = 1024
SEND = 512
WEIGHTS = (3, 4, 5, 1, 3)
AXES = ("outer", "inner")
MIB = 1 << 20
ROWS_DIM = (((0,), (0,)), ((), ()))
COLS_DIM = (((1,), (1,)), ((), ()))
PLAIN = (((1,), (0,)), ((), ()))


def dot(a, b, dims):
    return lax.dot_general(a, b, dims, preferred_element_type=jnp.float32)


def scales(first, rows):
    place = first + lax.broadcasted_iota(jnp.int32, (rows, E), 0)
    return lax.rsqrt(place.astype(jnp.float32) + 1.0)


def head_columns(head):
    return pl.ds(pl.multiple_of(head * E, E), E)


def add_block(left, right, head, acc, states_out, b):
    cols = head_columns(head)
    states_out[b, cols, cols] = acc[...].astype(jnp.bfloat16)
    states_out[b, cols, head_columns(1 - head)] = jnp.zeros((E, E), jnp.bfloat16)
    acc[...] += dot(left, right, ROWS_DIM)


def head_sums(device_ref, head, blocks, k_ref, v_ref, q_ref, g_ref, s_out, before_out, after_out,
              kv_acc, qg_acc):
    rows = k_ref.shape[0]
    cols = head_columns(head)
    for b in blocks:
        at = pl.ds(b * SUB, SUB)
        add_block(k_ref[at, cols], v_ref[at, cols], head, kv_acc, before_out, b)
        b = rows // SUB - 1 - b
        at = pl.ds(b * SUB, SUB)
        scale = scales(device_ref[0] * rows + b * SUB, SUB)
        scaled = (q_ref[at, cols].astype(jnp.float32) * scale).astype(jnp.bfloat16)
        s_out[at, cols] = scaled
        add_block(scaled, g_ref[at, cols], head, qg_acc, after_out, b)


def sent_kernel(device_ref, k_hbm, v_hbm, q_hbm, g_hbm, k_out, v_out, q_out, g_out, s_out,
                before_out, after_out, send_out, kv_acc, qg_acc, sems):
    rows = k_hbm.shape[0]
    ends = list(range(CHUNK, rows, CHUNK)) + [rows - CHUNK // 2, rows]
    starts = [0] + ends[:-1]
    copies = []
    for c, (start, end) in enumerate(zip(starts, ends)):
        at, back = pl.ds(start, end - start), pl.ds(rows - end, end - start)
        copies.append([
            pltpu.make_async_copy(k_hbm.at[at], k_out.at[at], sems.at[0, c]),
            pltpu.make_async_copy(v_hbm.at[at], v_out.at[at], sems.at[1, c]),
            pltpu.make_async_copy(q_hbm.at[back], q_out.at[back], sems.at[2, c]),
            pltpu.make_async_copy(g_hbm.at[back], g_out.at[back], sems.at[3, c]),
        ])
        for copy in copies[c]:
            copy.start()
    kv_acc[...] = jnp.zeros_like(kv_acc)
    qg_acc[...] = jnp.zeros_like(qg_acc)
    head = 1 - (device_ref[0] & 1)
    for c, (start, end) in enumerate(zip(starts, ends)):
        for copy in copies[c]:
            copy.wait()
        head_sums(device_ref, head, range(start // SUB, end // SUB), k_out, v_out, q_out, g_out,
                  s_out, before_out, after_out, kv_acc, qg_acc)
    send_out[pl.ds(0, E), :] = kv_acc[...]
    send_out[pl.ds(E, E), :] = qg_acc[...]


def kept_kernel(device_ref, k_ref, v_ref, q_ref, g_ref, s_in, before_in, after_in, earlier, s_out,
                before_out, after_out, keep_out, kv_acc, qg_acc):
    kv_acc[...] = jnp.zeros_like(kv_acc)
    qg_acc[...] = jnp.zeros_like(qg_acc)
    head_sums(device_ref, device_ref[0] & 1, range(k_ref.shape[0] // SUB), k_ref, v_ref, q_ref,
              g_ref, s_out, before_out, after_out, kv_acc, qg_acc)
    keep_out[pl.ds(0, E), :] = kv_acc[...]
    keep_out[pl.ds(E, E), :] = qg_acc[...]


def inner_kernel(first, blocks, device_ref, s_ref, k_ref, v_ref, g_ref, before_ref, after_ref,
                 *refs):
    att_ref, qgrad_ref, kgrad_ref, vgrad_ref, tick_ref = refs[-5:]
    tick_ref[...] = jnp.zeros_like(tick_ref)
    rows, width = s_ref.shape
    heads = width // E
    t = lax.broadcasted_iota(jnp.int32, (SUB, SUB), 0)
    s = lax.broadcasted_iota(jnp.int32, (SUB, SUB), 1)
    causal = s <= t

    def block(i):
        b = first + i
        at = pl.ds(b * SUB, SUB)
        scale = scales(device_ref[0] * rows + b * SUB, SUB)
        att_state = dot(s_ref[at, :], before_ref[b], PLAIN)
        qgrad_state = dot(g_ref[at, :], before_ref[b], COLS_DIM)
        kgrad_state = dot(v_ref[at, :], after_ref[b], COLS_DIM)
        vgrad_state = dot(k_ref[at, :], after_ref[b], PLAIN)
        for h in range(heads):
            cols = pl.ds(h * E, E)
            part = slice(h * E, (h + 1) * E)
            sh, kh, vh, gh = s_ref[at, cols], k_ref[at, cols], v_ref[at, cols], g_ref[at, cols]
            a = jnp.where(causal, dot(sh, kh, COLS_DIM), 0.0).astype(jnp.bfloat16)
            m = jnp.where(causal, dot(gh, vh, COLS_DIM), 0.0).astype(jnp.bfloat16)
            att_ref[at, cols] = (dot(a, vh, PLAIN) + att_state[:, part]).astype(jnp.bfloat16)
            qgrad_ref[at, cols] = (
                (dot(m, kh, PLAIN) + qgrad_state[:, part]) * scale
            ).astype(jnp.bfloat16)
            kgrad_ref[at, cols] = (dot(m, sh, ROWS_DIM) + kgrad_state[:, part]).astype(jnp.bfloat16)
            vgrad_ref[at, cols] = (dot(a, gh, ROWS_DIM) + vgrad_state[:, part]).astype(jnp.bfloat16)

    for i in range(blocks):
        block(i)


def bit_of(device_ref, bit):
    return (lax.shift_right_logical(device_ref[0], bit) & 1) == 1


def add_kernel(device_ref, mine_ref, came_ref, tick_ref, out_ref):
    out_ref[...] = mine_ref[...] + came_ref[...]


def pick_kernel(bit, device_ref, mine_ref, came_ref, tick_ref, out_ref):
    up, down = pl.ds(0, E), pl.ds(E, E)
    out_ref[...] = jnp.where(
        bit_of(device_ref, bit), mine_ref[down, :] + came_ref[down, :],
        mine_ref[up, :] + came_ref[up, :],
    )


def combine_kernel(device_ref, keep_ref, beside_ref, last_ref, tick_ref, *refs):
    came, (own_ref, given_ref) = refs[:-2], refs[-2:]
    odd = bit_of(device_ref, 0)
    for upward, part in ((True, pl.ds(0, E)), (False, pl.ds(E, E))):

        def chosen(bit, value):
            there = bit_of(device_ref, bit)
            return jnp.where(there, value, 0.0) if upward else jnp.where(there, 0.0, value)

        total = chosen(len(came) + 1, last_ref[...])
        for r, ref in enumerate(came):
            total = total + chosen(r + 1, ref[part, :])
        beside, keep = beside_ref[part, :], keep_ref[part, :]
        own_ref[part, :] = total + chosen(0, beside)
        given_ref[part, :] = total + (keep - chosen(0, keep))


def last_kernel(mine, device_ref, s_ref, k_ref, v_ref, g_ref, state_ref, *refs):
    att, qgrad, kgrad, vgrad = refs[:4]
    outs, (held, plain, turned, sems) = refs[-8:-4], refs[-4:]
    rows, width = s_ref.shape
    head = device_ref[0] & 1
    if not mine:
        head = 1 - head
    cols = head_columns(head)
    up, down = pl.ds(0, E), pl.ds(E, E)
    plain[...] = jnp.zeros_like(plain)
    turned[...] = jnp.zeros_like(turned)
    for part in (up, down):
        state = state_ref[part, :]
        plain[part, part] = state.astype(jnp.bfloat16)
        turned[part, part] = state.T.astype(jnp.bfloat16)
    copies = []
    for c in range(rows // SEND):
        at = pl.ds(c * SEND, SEND)
        scale = scales(device_ref[0] * rows + c * SEND, SEND)
        left = jnp.concatenate([s_ref[at, cols], k_ref[at, cols]], axis=1)
        right = jnp.concatenate([g_ref[at, cols], v_ref[at, cols]], axis=1)
        first, second = dot(left, plain[...], PLAIN), dot(right, turned[...], PLAIN)
        sums = (first[:, :E], second[:, :E] * scale, second[:, E:], first[:, E:])
        for o, part in enumerate((att, qgrad, kgrad, vgrad)):
            value = part[at, cols].astype(jnp.float32) + sums[o]
            held[o, at, :] = value.astype(jnp.bfloat16)
        for o in range(4):
            copy = pltpu.make_async_copy(held.at[o, at], outs[o].at[at, cols], sems.at[o, c])
            copy.start()
            copies.append(copy)
    for copy in copies:
        copy.wait()


VM = pl.BlockSpec(memory_space=pltpu.VMEM)
ANY = pl.BlockSpec(memory_space=pl.ANY)
SM = pl.BlockSpec(memory_space=pltpu.SMEM)
PARAMS = pltpu.CompilerParams(vmem_limit_bytes=24 * MIB)
FUSED = pltpu.CompilerParams(vmem_limit_bytes=24 * MIB, fuse_transposed_lhs_in_matmul=True)


def in_vmem(x):
    return pltpu.with_memory_space_constraint(x, pltpu.VMEM)


def in_hbm(x):
    return pltpu.with_memory_space_constraint(x, pltpu.HBM)


def from_others(send, count, device_ref, keep_sums, work):
    def exchange(x, bit):
        return lax.ppermute(x, AXES, [(d, d ^ (1 << bit)) for d in range(count)])

    def call(kernel, outs, name, *operands):
        shapes = [jax.ShapeDtypeStruct(shape, jnp.float32) for shape in outs]
        return pl.pallas_call(
            kernel,
            out_shape=shapes,
            in_specs=[SM] + [VM] * len(operands),
            out_specs=[VM] * len(outs),
            compiler_params=PARAMS,
            name=name,
        )(device_ref, *operands)

    full, half = send.shape, (E, E)
    last = count.bit_length() - 2
    beside = exchange(send, 0)
    keep = keep_sums()
    tick = work(0, keep)
    [running] = call(add_kernel, [full], "add_round", keep, beside, tick)
    came = []
    for bit in range(1, last):
        came.append(exchange(running, bit))
        if bit < 3:
            tick = work(bit, running)
        if bit < last - 1:
            [running] = call(add_kernel, [full], "add_round", running, came[-1], tick)
    tick = work(3, running)
    [picked] = call(
        functools.partial(pick_kernel, last), [half], "pick_half", running, came[-1], tick
    )
    crossed = exchange(picked, last)
    tick = work(4, picked)
    own, given = call(combine_kernel, [full] * 2, "combine_rounds", keep, beside, crossed, tick, *came)
    return own, exchange(given, 0)


def on_device(count, query, keys, values, out_grad):
    rows, width = query.shape
    bf16 = jnp.bfloat16
    subs = rows // SUB
    chunks = rows // CHUNK
    device_ref = lax.axis_index(AXES).astype(jnp.int32).reshape(1)
    array = pltpu.VMEM((rows, width), bf16)
    states = pltpu.VMEM((subs, width, width), bf16)
    half = jax.ShapeDtypeStruct((2 * E, E), jnp.float32)

    sums = [pltpu.VMEM((E, E), jnp.float32)] * 2
    k_vm, v_vm, q_vm, g_vm, s_vm, before, after, send = pl.pallas_call(
        sent_kernel,
        out_shape=(array,) * 5 + (states,) * 2 + (half,),
        in_specs=[SM] + [ANY] * 4,
        out_specs=[VM] * 8,
        scratch_shapes=sums + [pltpu.SemaphoreType.DMA((4, chunks + 1))],
        compiler_params=PARAMS,
        name="sent_head_sums",
    )(device_ref, *[in_hbm(x) for x in (keys, values, query, out_grad)])

    def keep_sums():
        nonlocal s_vm, before, after
        operands = (k_vm, v_vm, q_vm, g_vm, s_vm, before, after)
        s_vm, before, after, keep = pl.pallas_call(
            kept_kernel,
            out_shape=(array,) + (states,) * 2 + (half,),
            in_specs=[SM] + [VM] * 7 + [ANY],
            out_specs=[VM] * 4,
            input_output_aliases={5: 0, 6: 1, 7: 2},
            scratch_shapes=sums,
            compiler_params=PARAMS,
            name="kept_head_sums",
        )(device_ref, *[in_vmem(x) for x in operands], send)
        return keep

    parts = []
    tick_shape = pltpu.VMEM((8, E), jnp.float32)

    def work(p, mark):
        first = subs * sum(WEIGHTS[:p]) // sum(WEIGHTS)
        blocks = subs * sum(WEIGHTS[:p + 1]) // sum(WEIGHTS) - first
        operands = [s_vm, k_vm, v_vm, g_vm, before, after, *parts]
        *parts[:], tick = pl.pallas_call(
            functools.partial(inner_kernel, first, blocks),
            out_shape=(array,) * 4 + (tick_shape,),
            in_specs=[SM] + [VM] * len(operands) + [ANY],
            out_specs=[VM] * 5,
            input_output_aliases={7 + o: o for o in range(len(parts))},
            compiler_params=FUSED,
            cost_estimate=pl.CostEstimate(
                flops=575_000_000 * blocks, bytes_accessed=MIB * blocks, transcendentals=0
            ),
            name="within_blocks",
        )(device_ref, *[in_vmem(x) for x in operands], mark)
        return tick

    own, other = from_others(send, count, device_ref, keep_sums, work)

    result = jax.ShapeDtypeStruct((rows, width), bf16)
    outs = ()
    for mine, state, name in ((True, own, "add_own_head"), (False, other, "add_other_head")):
        outs = pl.pallas_call(
            functools.partial(last_kernel, mine),
            out_shape=(result,) * 4,
            in_specs=[SM] + [VM] * 9 + [ANY] * len(outs),
            out_specs=[ANY] * 4,
            input_output_aliases={10 + o: o for o in range(len(outs))},
            scratch_shapes=[
                pltpu.VMEM((4, rows, E), bf16),
                pltpu.VMEM((2 * E, 2 * E), bf16),
                pltpu.VMEM((2 * E, 2 * E), bf16),
                pltpu.SemaphoreType.DMA((4, rows // SEND)),
            ],
            compiler_params=PARAMS,
            name=name,
        )(
            device_ref,
            *[in_vmem(x) for x in (s_vm, k_vm, v_vm, g_vm)],
            state,
            *[in_vmem(x) for x in parts],
            *[in_hbm(x) for x in outs],
        )
    return tuple(outs)


def solution(mesh):
    spec = P(AXES, None)
    count = mesh.shape["outer"] * mesh.shape["inner"]
    return jax.shard_map(
        functools.partial(on_device, count),
        mesh=mesh,
        in_specs=(spec,) * 4,
        out_specs=(spec,) * 4,
        check_vma=False,
    )
```

```python
import functools

import jax
import jax.numpy as jnp
from jax import lax
from jax.experimental import pallas as pl
from jax.experimental.pallas import tpu as pltpu
from jax.sharding import PartitionSpec as P

E = 128
SUB = 256
CHUNK = 1024
SEND = 512
WEIGHTS = (2, 4, 6, 1, 3)
AXES = ("outer", "inner")
MIB = 1 << 20
ROWS_DIM = (((0,), (0,)), ((), ()))
COLS_DIM = (((1,), (1,)), ((), ()))
PLAIN = (((1,), (0,)), ((), ()))


def dot(a, b, dims):
    return lax.dot_general(a, b, dims, preferred_element_type=jnp.float32)


def scales(first, rows):
    place = first + lax.broadcasted_iota(jnp.int32, (rows, E), 0)
    return lax.rsqrt(place.astype(jnp.float32) + 1.0)


def head_columns(head):
    return pl.ds(pl.multiple_of(head * E, E), E)


def add_block(left, right, head, acc, states_out, b):
    cols = head_columns(head)
    states_out[b, cols, cols] = acc[...].astype(jnp.bfloat16)
    states_out[b, cols, head_columns(1 - head)] = jnp.zeros((E, E), jnp.bfloat16)
    acc[...] += dot(left, right, ROWS_DIM)


def head_sums(kept, device_ref, head, hbm, k_out, v_out, g_out, s_out, before_out, after_out, held,
              kv_acc, qg_acc, sems):
    k_hbm, v_hbm, q_hbm, g_hbm = hbm
    rows = k_hbm.shape[0]
    cols = head_columns(head)
    ends = list(range(CHUNK, rows, CHUNK)) + [rows - CHUNK // 2, rows]
    starts = [0] + ends[:-1]
    copies = []
    for c, (start, end) in enumerate(zip(starts, ends)):
        at, back = pl.ds(start, end - start), pl.ds(rows - end, end - start)
        copies.append([
            pltpu.make_async_copy(q_hbm.at[back, cols], held.at[back], sems.at[2, c]),
            pltpu.make_async_copy(g_hbm.at[back, cols], g_out.at[back, cols], sems.at[3, c]),
        ])
        if not kept:
            copies[c] += [
                pltpu.make_async_copy(k_hbm.at[at], k_out.at[at], sems.at[0, c]),
                pltpu.make_async_copy(v_hbm.at[at], v_out.at[at], sems.at[1, c]),
            ]
        for copy in copies[c]:
            copy.start()
    kv_acc[...] = jnp.zeros_like(kv_acc)
    qg_acc[...] = jnp.zeros_like(qg_acc)
    for c, (start, end) in enumerate(zip(starts, ends)):
        for copy in copies[c]:
            copy.wait()
        for b in range(start // SUB, end // SUB):
            at = pl.ds(b * SUB, SUB)
            add_block(k_out[at, cols], v_out[at, cols], head, kv_acc, before_out, b)
            b = rows // SUB - 1 - b
            at = pl.ds(b * SUB, SUB)
            scale = scales(device_ref[0] * rows + b * SUB, SUB)
            scaled = (held[at, :].astype(jnp.float32) * scale).astype(jnp.bfloat16)
            s_out[at, cols] = scaled
            add_block(scaled, g_out[at, cols], head, qg_acc, after_out, b)


def sums_kernel(kept, device_ref, *refs):
    hbm, refs = refs[:4], refs[-11:]
    outs, total_out, (held, kv_acc, qg_acc, sems) = refs[:6], refs[6], refs[7:]
    head = device_ref[0] & 1
    if not kept:
        head = 1 - head
    head_sums(kept, device_ref, head, hbm, *outs, held, kv_acc, qg_acc, sems)
    total_out[pl.ds(0, E), :] = kv_acc[...]
    total_out[pl.ds(E, E), :] = qg_acc[...]


def inner_kernel(first, blocks, device_ref, s_ref, k_ref, v_ref, g_ref, before_ref, after_ref,
                 *refs):
    att_ref, qgrad_ref, kgrad_ref, vgrad_ref, tick_ref = refs[-5:]
    tick_ref[...] = jnp.zeros_like(tick_ref)
    rows, width = s_ref.shape
    heads = width // E
    t = lax.broadcasted_iota(jnp.int32, (SUB, SUB), 0)
    s = lax.broadcasted_iota(jnp.int32, (SUB, SUB), 1)
    causal = s <= t

    def block(i):
        b = first + i
        at = pl.ds(b * SUB, SUB)
        scale = scales(device_ref[0] * rows + b * SUB, SUB)
        att_state = dot(s_ref[at, :], before_ref[b], PLAIN)
        qgrad_state = dot(g_ref[at, :], before_ref[b], COLS_DIM)
        kgrad_state = dot(v_ref[at, :], after_ref[b], COLS_DIM)
        vgrad_state = dot(k_ref[at, :], after_ref[b], PLAIN)
        for h in range(heads):
            cols = pl.ds(h * E, E)
            part = slice(h * E, (h + 1) * E)
            sh, kh, vh, gh = s_ref[at, cols], k_ref[at, cols], v_ref[at, cols], g_ref[at, cols]
            a = jnp.where(causal, dot(sh, kh, COLS_DIM), 0.0).astype(jnp.bfloat16)
            m = jnp.where(causal, dot(gh, vh, COLS_DIM), 0.0).astype(jnp.bfloat16)
            att_ref[at, cols] = (dot(a, vh, PLAIN) + att_state[:, part]).astype(jnp.bfloat16)
            qgrad_ref[at, cols] = (
                (dot(m, kh, PLAIN) + qgrad_state[:, part]) * scale
            ).astype(jnp.bfloat16)
            kgrad_ref[at, cols] = (dot(m, sh, ROWS_DIM) + kgrad_state[:, part]).astype(jnp.bfloat16)
            vgrad_ref[at, cols] = (dot(a, gh, ROWS_DIM) + vgrad_state[:, part]).astype(jnp.bfloat16)

    for i in range(blocks):
        block(i)


def bit_of(device_ref, bit):
    return (lax.shift_right_logical(device_ref[0], bit) & 1) == 1


def add_kernel(device_ref, mine_ref, came_ref, tick_ref, out_ref):
    out_ref[...] = mine_ref[...] + came_ref[...]


def pick_kernel(bit, device_ref, mine_ref, came_ref, tick_ref, out_ref):
    up, down = pl.ds(0, E), pl.ds(E, E)
    out_ref[...] = jnp.where(
        bit_of(device_ref, bit), mine_ref[down, :] + came_ref[down, :],
        mine_ref[up, :] + came_ref[up, :],
    )


def combine_kernel(device_ref, keep_ref, beside_ref, last_ref, tick_ref, *refs):
    came, (own_ref, given_ref) = refs[:-2], refs[-2:]
    odd = bit_of(device_ref, 0)
    for upward, part in ((True, pl.ds(0, E)), (False, pl.ds(E, E))):

        def chosen(bit, value):
            there = bit_of(device_ref, bit)
            return jnp.where(there, value, 0.0) if upward else jnp.where(there, 0.0, value)

        total = chosen(len(came) + 1, last_ref[...])
        for r, ref in enumerate(came):
            total = total + chosen(r + 1, ref[part, :])
        beside, keep = beside_ref[part, :], keep_ref[part, :]
        own_ref[part, :] = total + chosen(0, beside)
        given_ref[part, :] = total + (keep - chosen(0, keep))


def last_kernel(mine, device_ref, s_ref, k_ref, v_ref, g_ref, state_ref, *refs):
    att, qgrad, kgrad, vgrad = refs[:4]
    outs, (held, plain, turned, sems) = refs[-8:-4], refs[-4:]
    rows, width = s_ref.shape
    head = device_ref[0] & 1
    if not mine:
        head = 1 - head
    cols = head_columns(head)
    up, down = pl.ds(0, E), pl.ds(E, E)
    plain[...] = jnp.zeros_like(plain)
    turned[...] = jnp.zeros_like(turned)
    for part in (up, down):
        state = state_ref[part, :]
        plain[part, part] = state.astype(jnp.bfloat16)
        turned[part, part] = state.T.astype(jnp.bfloat16)
    copies = []
    for c in range(rows // SEND):
        at = pl.ds(c * SEND, SEND)
        scale = scales(device_ref[0] * rows + c * SEND, SEND)
        left = jnp.concatenate([s_ref[at, cols], k_ref[at, cols]], axis=1)
        right = jnp.concatenate([g_ref[at, cols], v_ref[at, cols]], axis=1)
        first, second = dot(left, plain[...], PLAIN), dot(right, turned[...], PLAIN)
        sums = (first[:, :E], second[:, :E] * scale, second[:, E:], first[:, E:])
        for o, part in enumerate((att, qgrad, kgrad, vgrad)):
            value = part[at, cols].astype(jnp.float32) + sums[o]
            held[o, at, :] = value.astype(jnp.bfloat16)
        for o in range(4):
            copy = pltpu.make_async_copy(held.at[o, at], outs[o].at[at, cols], sems.at[o, c])
            copy.start()
            copies.append(copy)
    for copy in copies:
        copy.wait()


VM = pl.BlockSpec(memory_space=pltpu.VMEM)
ANY = pl.BlockSpec(memory_space=pl.ANY)
SM = pl.BlockSpec(memory_space=pltpu.SMEM)
PARAMS = pltpu.CompilerParams(vmem_limit_bytes=24 * MIB)
FUSED = pltpu.CompilerParams(vmem_limit_bytes=24 * MIB, fuse_transposed_lhs_in_matmul=True)


def in_vmem(x):
    return pltpu.with_memory_space_constraint(x, pltpu.VMEM)


def in_hbm(x):
    return pltpu.with_memory_space_constraint(x, pltpu.HBM)


def from_others(send, keep, count, device_ref, work):
    def exchange(x, bit):
        return lax.ppermute(x, AXES, [(d, d ^ (1 << bit)) for d in range(count)])

    def call(kernel, outs, name, *operands):
        shapes = [jax.ShapeDtypeStruct(shape, jnp.float32) for shape in outs]
        return pl.pallas_call(
            kernel,
            out_shape=shapes,
            in_specs=[SM] + [VM] * len(operands),
            out_specs=[VM] * len(outs),
            compiler_params=PARAMS,
            name=name,
        )(device_ref, *operands)

    full, half = send.shape, (E, E)
    last = count.bit_length() - 2
    beside = exchange(send, 0)
    tick = work(0, keep)
    [running] = call(add_kernel, [full], "add_round", keep, beside, tick)
    came = []
    for bit in range(1, last):
        came.append(exchange(running, bit))
        if bit < 3:
            tick = work(bit, running)
        if bit < last - 1:
            [running] = call(add_kernel, [full], "add_round", running, came[-1], tick)
    tick = work(3, running)
    [picked] = call(
        functools.partial(pick_kernel, last), [half], "pick_half", running, came[-1], tick
    )
    crossed = exchange(picked, last)
    tick = work(4, picked)
    own, given = call(combine_kernel, [full] * 2, "combine_rounds", keep, beside, crossed, tick, *came)
    return own, exchange(given, 0)


def on_device(count, query, keys, values, out_grad):
    rows, width = query.shape
    bf16 = jnp.bfloat16
    subs = rows // SUB
    chunks = rows // CHUNK
    device_ref = lax.axis_index(AXES).astype(jnp.int32).reshape(1)
    array = pltpu.VMEM((rows, width), bf16)
    states = pltpu.VMEM((subs, width, width), bf16)
    half = jax.ShapeDtypeStruct((2 * E, E), jnp.float32)

    def sums(kept, name, *filled):
        return pl.pallas_call(
            functools.partial(sums_kernel, kept),
            out_shape=(array,) * 4 + (states,) * 2 + (half,),
            in_specs=[SM] + [ANY] * 4 + [VM] * len(filled[:6]) + [ANY] * len(filled[6:]),
            out_specs=[VM] * 7,
            input_output_aliases={5 + o: o for o in range(len(filled[:6]))},
            scratch_shapes=[
                pltpu.VMEM((rows, E), bf16),
                pltpu.VMEM((E, E), jnp.float32),
                pltpu.VMEM((E, E), jnp.float32),
                pltpu.SemaphoreType.DMA((4, chunks + 1)),
            ],
            compiler_params=PARAMS,
            name=name,
        )(
            device_ref,
            *[in_hbm(x) for x in (keys, values, query, out_grad)],
            *[in_vmem(x) for x in filled[:6]],
            *filled[6:],
        )

    sent = sums(False, "sent_head_sums")
    send = sent[6]
    *filled, keep = sums(True, "kept_head_sums", *sent)
    k_vm, v_vm, g_vm, s_vm, before, after = filled

    parts = []
    tick_shape = pltpu.VMEM((8, E), jnp.float32)

    def work(p, mark):
        first = subs * sum(WEIGHTS[:p]) // sum(WEIGHTS)
        blocks = subs * sum(WEIGHTS[:p + 1]) // sum(WEIGHTS) - first
        operands = [s_vm, k_vm, v_vm, g_vm, before, after, *parts]
        *parts[:], tick = pl.pallas_call(
            functools.partial(inner_kernel, first, blocks),
            out_shape=(array,) * 4 + (tick_shape,),
            in_specs=[SM] + [VM] * len(operands) + [ANY],
            out_specs=[VM] * 5,
            input_output_aliases={7 + o: o for o in range(len(parts))},
            compiler_params=FUSED,
            cost_estimate=pl.CostEstimate(
                flops=575_000_000 * blocks, bytes_accessed=MIB * blocks, transcendentals=0
            ),
            name="within_blocks",
        )(device_ref, *[in_vmem(x) for x in operands], mark)
        return tick

    own, other = from_others(send, keep, count, device_ref, work)

    result = jax.ShapeDtypeStruct((rows, width), bf16)
    outs = ()
    for mine, state, name in ((True, own, "add_own_head"), (False, other, "add_other_head")):
        outs = pl.pallas_call(
            functools.partial(last_kernel, mine),
            out_shape=(result,) * 4,
            in_specs=[SM] + [VM] * 9 + [ANY] * len(outs),
            out_specs=[ANY] * 4,
            input_output_aliases={10 + o: o for o in range(len(outs))},
            scratch_shapes=[
                pltpu.VMEM((4, rows, E), bf16),
                pltpu.VMEM((2 * E, 2 * E), bf16),
                pltpu.VMEM((2 * E, 2 * E), bf16),
                pltpu.SemaphoreType.DMA((4, rows // SEND)),
            ],
            compiler_params=PARAMS,
            name=name,
        )(
            device_ref,
            *[in_vmem(x) for x in (s_vm, k_vm, v_vm, g_vm)],
            state,
            *[in_vmem(x) for x in parts],
            *[in_hbm(x) for x in outs],
        )
    return tuple(outs)


def solution(mesh):
    spec = P(AXES, None)
    count = mesh.shape["outer"] * mesh.shape["inner"]
    return jax.shard_map(
        functools.partial(on_device, count),
        mesh=mesh,
        in_specs=(spec,) * 4,
        out_specs=(spec,) * 4,
        check_vma=False,
    )
```

```python
import functools

import jax
import jax.numpy as jnp
from jax import lax
from jax.experimental import pallas as pl
from jax.experimental.pallas import tpu as pltpu
from jax.sharding import PartitionSpec as P

E = 128
SUB = 256
CHUNK = 2048
SEND = 512
WEIGHTS = (2, 4, 6, 1, 3)
AXES = ("outer", "inner")
MIB = 1 << 20
ROWS_DIM = (((0,), (0,)), ((), ()))
COLS_DIM = (((1,), (1,)), ((), ()))
PLAIN = (((1,), (0,)), ((), ()))


def dot(a, b, dims):
    return lax.dot_general(a, b, dims, preferred_element_type=jnp.float32)


def scales(first, rows):
    place = first + lax.broadcasted_iota(jnp.int32, (rows, E), 0)
    return lax.rsqrt(place.astype(jnp.float32) + 1.0)


def head_columns(head):
    return pl.ds(pl.multiple_of(head * E, E), E)


def add_block(left, right, head, acc, states_out, b):
    cols = head_columns(head)
    states_out[b, cols, cols] = acc[...].astype(jnp.bfloat16)
    states_out[b, cols, head_columns(1 - head)] = jnp.zeros((E, E), jnp.bfloat16)
    acc[...] += dot(left, right, ROWS_DIM)


def head_sums(device_ref, head, blocks, k_ref, v_ref, q_ref, g_ref, s_out, before_out, after_out,
              kv_acc, qg_acc):
    rows = k_ref.shape[0]
    cols = head_columns(head)
    for b in blocks:
        at = pl.ds(b * SUB, SUB)
        add_block(k_ref[at, cols], v_ref[at, cols], head, kv_acc, before_out, b)
        b = rows // SUB - 1 - b
        at = pl.ds(b * SUB, SUB)
        scale = scales(device_ref[0] * rows + b * SUB, SUB)
        scaled = (q_ref[at, cols].astype(jnp.float32) * scale).astype(jnp.bfloat16)
        s_out[at, cols] = scaled
        add_block(scaled, g_ref[at, cols], head, qg_acc, after_out, b)


def sent_kernel(device_ref, k_hbm, v_hbm, q_hbm, g_hbm, k_out, v_out, q_out, g_out, s_out,
                before_out, after_out, send_out, kv_acc, qg_acc, sems):
    rows = k_hbm.shape[0]
    ends = list(range(CHUNK, rows, CHUNK)) + [rows - CHUNK // 2, rows]
    starts = [0] + ends[:-1]
    copies = []
    for c, (start, end) in enumerate(zip(starts, ends)):
        at, back = pl.ds(start, end - start), pl.ds(rows - end, end - start)
        copies.append([
            pltpu.make_async_copy(k_hbm.at[at], k_out.at[at], sems.at[0, c]),
            pltpu.make_async_copy(v_hbm.at[at], v_out.at[at], sems.at[1, c]),
            pltpu.make_async_copy(q_hbm.at[back], q_out.at[back], sems.at[2, c]),
            pltpu.make_async_copy(g_hbm.at[back], g_out.at[back], sems.at[3, c]),
        ])
        for copy in copies[c]:
            copy.start()
    kv_acc[...] = jnp.zeros_like(kv_acc)
    qg_acc[...] = jnp.zeros_like(qg_acc)
    head = 1 - (device_ref[0] & 1)
    for c, (start, end) in enumerate(zip(starts, ends)):
        for copy in copies[c]:
            copy.wait()
        head_sums(device_ref, head, range(start // SUB, end // SUB), k_out, v_out, q_out, g_out,
                  s_out, before_out, after_out, kv_acc, qg_acc)
    send_out[pl.ds(0, E), :] = kv_acc[...]
    send_out[pl.ds(E, E), :] = qg_acc[...]


def kept_kernel(device_ref, k_ref, v_ref, q_ref, g_ref, s_in, before_in, after_in, earlier, s_out,
                before_out, after_out, keep_out, kv_acc, qg_acc):
    kv_acc[...] = jnp.zeros_like(kv_acc)
    qg_acc[...] = jnp.zeros_like(qg_acc)
    head_sums(device_ref, device_ref[0] & 1, range(k_ref.shape[0] // SUB), k_ref, v_ref, q_ref,
              g_ref, s_out, before_out, after_out, kv_acc, qg_acc)
    keep_out[pl.ds(0, E), :] = kv_acc[...]
    keep_out[pl.ds(E, E), :] = qg_acc[...]


def inner_kernel(first, blocks, device_ref, s_ref, k_ref, v_ref, g_ref, before_ref, after_ref,
                 *refs):
    att_ref, qgrad_ref, kgrad_ref, vgrad_ref, tick_ref = refs[-5:]
    tick_ref[...] = jnp.zeros_like(tick_ref)
    rows, width = s_ref.shape
    heads = width // E
    t = lax.broadcasted_iota(jnp.int32, (SUB, SUB), 0)
    s = lax.broadcasted_iota(jnp.int32, (SUB, SUB), 1)
    causal = s <= t

    def block(i):
        b = first + i
        at = pl.ds(b * SUB, SUB)
        scale = scales(device_ref[0] * rows + b * SUB, SUB)
        att_state = dot(s_ref[at, :], before_ref[b], PLAIN)
        qgrad_state = dot(g_ref[at, :], before_ref[b], COLS_DIM)
        kgrad_state = dot(v_ref[at, :], after_ref[b], COLS_DIM)
        vgrad_state = dot(k_ref[at, :], after_ref[b], PLAIN)
        for h in range(heads):
            cols = pl.ds(h * E, E)
            part = slice(h * E, (h + 1) * E)
            sh, kh, vh, gh = s_ref[at, cols], k_ref[at, cols], v_ref[at, cols], g_ref[at, cols]
            a = jnp.where(causal, dot(sh, kh, COLS_DIM), 0.0).astype(jnp.bfloat16)
            m = jnp.where(causal, dot(gh, vh, COLS_DIM), 0.0).astype(jnp.bfloat16)
            att_ref[at, cols] = (dot(a, vh, PLAIN) + att_state[:, part]).astype(jnp.bfloat16)
            qgrad_ref[at, cols] = (
                (dot(m, kh, PLAIN) + qgrad_state[:, part]) * scale
            ).astype(jnp.bfloat16)
            kgrad_ref[at, cols] = (dot(m, sh, ROWS_DIM) + kgrad_state[:, part]).astype(jnp.bfloat16)
            vgrad_ref[at, cols] = (dot(a, gh, ROWS_DIM) + vgrad_state[:, part]).astype(jnp.bfloat16)

    for i in range(blocks):
        block(i)


def bit_of(device_ref, bit):
    return (lax.shift_right_logical(device_ref[0], bit) & 1) == 1


def add_kernel(device_ref, mine_ref, came_ref, tick_ref, out_ref):
    out_ref[...] = mine_ref[...] + came_ref[...]


def pick_kernel(bit, device_ref, mine_ref, came_ref, tick_ref, out_ref):
    up, down = pl.ds(0, E), pl.ds(E, E)
    out_ref[...] = jnp.where(
        bit_of(device_ref, bit), mine_ref[down, :] + came_ref[down, :],
        mine_ref[up, :] + came_ref[up, :],
    )


def combine_kernel(device_ref, keep_ref, beside_ref, last_ref, tick_ref, *refs):
    came, (own_ref, given_ref) = refs[:-2], refs[-2:]
    odd = bit_of(device_ref, 0)
    for upward, part in ((True, pl.ds(0, E)), (False, pl.ds(E, E))):

        def chosen(bit, value):
            there = bit_of(device_ref, bit)
            return jnp.where(there, value, 0.0) if upward else jnp.where(there, 0.0, value)

        total = chosen(len(came) + 1, last_ref[...])
        for r, ref in enumerate(came):
            total = total + chosen(r + 1, ref[part, :])
        beside, keep = beside_ref[part, :], keep_ref[part, :]
        own_ref[part, :] = total + chosen(0, beside)
        given_ref[part, :] = total + (keep - chosen(0, keep))


def last_kernel(mine, device_ref, s_ref, k_ref, v_ref, g_ref, state_ref, *refs):
    att, qgrad, kgrad, vgrad = refs[:4]
    outs, (held, plain, turned, sems) = refs[-8:-4], refs[-4:]
    rows, width = s_ref.shape
    head = device_ref[0] & 1
    if not mine:
        head = 1 - head
    cols = head_columns(head)
    up, down = pl.ds(0, E), pl.ds(E, E)
    plain[...] = jnp.zeros_like(plain)
    turned[...] = jnp.zeros_like(turned)
    for part in (up, down):
        state = state_ref[part, :]
        plain[part, part] = state.astype(jnp.bfloat16)
        turned[part, part] = state.T.astype(jnp.bfloat16)
    copies = []
    for c in range(rows // SEND):
        at = pl.ds(c * SEND, SEND)
        scale = scales(device_ref[0] * rows + c * SEND, SEND)
        left = jnp.concatenate([s_ref[at, cols], k_ref[at, cols]], axis=1)
        right = jnp.concatenate([g_ref[at, cols], v_ref[at, cols]], axis=1)
        first, second = dot(left, plain[...], PLAIN), dot(right, turned[...], PLAIN)
        sums = (first[:, :E], second[:, :E] * scale, second[:, E:], first[:, E:])
        for o, part in enumerate((att, qgrad, kgrad, vgrad)):
            value = part[at, cols].astype(jnp.float32) + sums[o]
            held[o, at, :] = value.astype(jnp.bfloat16)
        for o in range(4):
            copy = pltpu.make_async_copy(held.at[o, at], outs[o].at[at, cols], sems.at[o, c])
            copy.start()
            copies.append(copy)
    for copy in copies:
        copy.wait()


VM = pl.BlockSpec(memory_space=pltpu.VMEM)
ANY = pl.BlockSpec(memory_space=pl.ANY)
SM = pl.BlockSpec(memory_space=pltpu.SMEM)
PARAMS = pltpu.CompilerParams(vmem_limit_bytes=24 * MIB)
FUSED = pltpu.CompilerParams(vmem_limit_bytes=24 * MIB, fuse_transposed_lhs_in_matmul=True)


def in_vmem(x):
    return pltpu.with_memory_space_constraint(x, pltpu.VMEM)


def in_hbm(x):
    return pltpu.with_memory_space_constraint(x, pltpu.HBM)


def from_others(send, count, device_ref, keep_sums, work):
    def exchange(x, bit):
        return lax.ppermute(x, AXES, [(d, d ^ (1 << bit)) for d in range(count)])

    def call(kernel, outs, name, *operands):
        shapes = [jax.ShapeDtypeStruct(shape, jnp.float32) for shape in outs]
        return pl.pallas_call(
            kernel,
            out_shape=shapes,
            in_specs=[SM] + [VM] * len(operands),
            out_specs=[VM] * len(outs),
            compiler_params=PARAMS,
            name=name,
        )(device_ref, *operands)

    full, half = send.shape, (E, E)
    last = count.bit_length() - 2
    beside = exchange(send, 0)
    keep = keep_sums()
    tick = work(0, keep)
    [running] = call(add_kernel, [full], "add_round", keep, beside, tick)
    came = []
    for bit in range(1, last):
        came.append(exchange(running, bit))
        if bit < 3:
            tick = work(bit, running)
        if bit < last - 1:
            [running] = call(add_kernel, [full], "add_round", running, came[-1], tick)
    tick = work(3, running)
    [picked] = call(
        functools.partial(pick_kernel, last), [half], "pick_half", running, came[-1], tick
    )
    crossed = exchange(picked, last)
    tick = work(4, picked)
    own, given = call(combine_kernel, [full] * 2, "combine_rounds", keep, beside, crossed, tick, *came)
    return own, exchange(given, 0)


def on_device(count, query, keys, values, out_grad):
    rows, width = query.shape
    bf16 = jnp.bfloat16
    subs = rows // SUB
    chunks = rows // CHUNK
    device_ref = lax.axis_index(AXES).astype(jnp.int32).reshape(1)
    array = pltpu.VMEM((rows, width), bf16)
    states = pltpu.VMEM((subs, width, width), bf16)
    half = jax.ShapeDtypeStruct((2 * E, E), jnp.float32)

    sums = [pltpu.VMEM((E, E), jnp.float32)] * 2
    k_vm, v_vm, q_vm, g_vm, s_vm, before, after, send = pl.pallas_call(
        sent_kernel,
        out_shape=(array,) * 5 + (states,) * 2 + (half,),
        in_specs=[SM] + [ANY] * 4,
        out_specs=[VM] * 8,
        scratch_shapes=sums + [pltpu.SemaphoreType.DMA((4, chunks + 1))],
        compiler_params=PARAMS,
        name="sent_head_sums",
    )(device_ref, *[in_hbm(x) for x in (keys, values, query, out_grad)])

    def keep_sums():
        nonlocal s_vm, before, after
        operands = (k_vm, v_vm, q_vm, g_vm, s_vm, before, after)
        s_vm, before, after, keep = pl.pallas_call(
            kept_kernel,
            out_shape=(array,) + (states,) * 2 + (half,),
            in_specs=[SM] + [VM] * 7 + [ANY],
            out_specs=[VM] * 4,
            input_output_aliases={5: 0, 6: 1, 7: 2},
            scratch_shapes=sums,
            compiler_params=PARAMS,
            name="kept_head_sums",
        )(device_ref, *[in_vmem(x) for x in operands], send)
        return keep

    parts = []
    tick_shape = pltpu.VMEM((8, E), jnp.float32)

    def work(p, mark):
        first = subs * sum(WEIGHTS[:p]) // sum(WEIGHTS)
        blocks = subs * sum(WEIGHTS[:p + 1]) // sum(WEIGHTS) - first
        operands = [s_vm, k_vm, v_vm, g_vm, before, after, *parts]
        *parts[:], tick = pl.pallas_call(
            functools.partial(inner_kernel, first, blocks),
            out_shape=(array,) * 4 + (tick_shape,),
            in_specs=[SM] + [VM] * len(operands) + [ANY],
            out_specs=[VM] * 5,
            input_output_aliases={7 + o: o for o in range(len(parts))},
            compiler_params=FUSED,
            cost_estimate=pl.CostEstimate(
                flops=575_000_000 * blocks, bytes_accessed=MIB * blocks, transcendentals=0
            ),
            name="within_blocks",
        )(device_ref, *[in_vmem(x) for x in operands], mark)
        return tick

    own, other = from_others(send, count, device_ref, keep_sums, work)

    result = jax.ShapeDtypeStruct((rows, width), bf16)
    outs = ()
    for mine, state, name in ((True, own, "add_own_head"), (False, other, "add_other_head")):
        outs = pl.pallas_call(
            functools.partial(last_kernel, mine),
            out_shape=(result,) * 4,
            in_specs=[SM] + [VM] * 9 + [ANY] * len(outs),
            out_specs=[ANY] * 4,
            input_output_aliases={10 + o: o for o in range(len(outs))},
            scratch_shapes=[
                pltpu.VMEM((4, rows, E), bf16),
                pltpu.VMEM((2 * E, 2 * E), bf16),
                pltpu.VMEM((2 * E, 2 * E), bf16),
                pltpu.SemaphoreType.DMA((4, rows // SEND)),
            ],
            compiler_params=PARAMS,
            name=name,
        )(
            device_ref,
            *[in_vmem(x) for x in (s_vm, k_vm, v_vm, g_vm)],
            state,
            *[in_vmem(x) for x in parts],
            *[in_hbm(x) for x in outs],
        )
    return tuple(outs)


def solution(mesh):
    spec = P(AXES, None)
    count = mesh.shape["outer"] * mesh.shape["inner"]
    return jax.shard_map(
        functools.partial(on_device, count),
        mesh=mesh,
        in_specs=(spec,) * 4,
        out_specs=(spec,) * 4,
        check_vma=False,
    )
```
